128 devices in a mesh: seq: 32 (over y, z, core), mp: 4 (over x).
Axes of the slice: x: 4, y: 4, z: 4, core: 2. Of those that a mesh axis runs over, the one named last changes fastest.
Arguments:
- tokens: bfloat16 [65536, 4096], P('seq', 'mp'), may hold values from -6 to 6
- cotangent: bfloat16 [65536, 4096], P('seq', 'mp'), may hold values from -6 to 6
- norm_gain: float32 [4096], replicated, may hold values from 0.5 to 2
- router_weight: float32 [4096], replicated, may hold values from -0.09375 to 0.09375
- w_query: bfloat16 [4096, 2048], P(None, 'mp'), may hold values from -0.09375 to 0.09375
- w_key: bfloat16 [4096, 512], P(None, 'mp'), may hold values from -0.09375 to 0.09375
- w_value: bfloat16 [4096, 512], P(None, 'mp'), may hold values from -0.09375 to 0.09375
- w_out: bfloat16 [2048, 4096], P('mp'), may hold values from -0.125 to 0.125
- routed_index: int32 [32, 512], P('seq'), may hold values from 0 to 2047, as said below
- routed_count: int32 [32], P('seq'), may hold values from 0 to 512, as said below
- routed_dest: int32 [32, 512], P('seq'), may hold values from 0 to 8191, as said below
Outputs:
- input_grad: bfloat16 [65536, 4096], P('seq', 'mp')
The draws below stay inside these ranges and needn't reach their ends.
Inputs may be any that keep to these rules, and one draw needn't show every extreme that they name: `routed_count`: the counts add up to 8192; in every draw one index of seq has 512 routed tokens and another has none. `routed_index`: for each index of seq the first routed_count entries are distinct local token indices in increasing order; the others are 0. `routed_dest`: place q belongs to compacted owner q // 256, slot q % 256; every place from 0 to 8191 is taken by exactly one routed token, so every owner receives exactly 256. One index of seq sends at most 16 tokens to one owner, and that many in every draw. Within one owner the places follow the sending index of seq, and within one sender the order of its token indices. Entries past routed_count are 0.
All inputs are finite; a program needn't handle non-finite values.
Results may differ from the reference program's by a relative error of at most 0.0039.
Values may be sent and summed in bfloat16 or wider, within the bound.
A program may use at most 128 MiB of HBM per device.

```python
import math
import jax
import jax.numpy as jnp
from jax import lax

D = 4096
HEAD_DIM = 128
HEADS = 16
KV_HEADS = 4
TOK_DEV = 2048
ROUTED_DEV = 256
CAP = 512
TOKENS = 65536
N_SEQ = 32


def routing_plan(key):
    half_load = ROUTED_DEV // N_SEQ
    pair_total = N_SEQ // 2
    sender_order = jax.random.permutation(jax.random.fold_in(key, 11), N_SEQ).astype(jnp.int32)
    shifts = jax.random.randint(jax.random.fold_in(key, 12), (pair_total, N_SEQ), 0, half_load + 1).astype(jnp.int32)
    shifts = shifts.at[0].set(half_load)
    signed = jnp.zeros((N_SEQ, N_SEQ), jnp.int32)
    signed = signed.at[sender_order[0::2]].set(shifts)
    signed = signed.at[sender_order[1::2]].set(-shifts)
    pair_load = half_load + signed
    sender_counts = jnp.sum(pair_load, axis=1)
    before_rows = jnp.cumsum(pair_load, axis=0) - pair_load
    sender_keys = jax.random.split(jax.random.fold_in(key, 13), N_SEQ)

    def one_sender(load_row, before_row, sender_count, sender_key):
        slots = jnp.arange(CAP, dtype=jnp.int32)
        is_valid = slots < sender_count
        bounds = jnp.cumsum(load_row)
        sorted_owner = jnp.sum((bounds[None, :] <= slots[:, None]).astype(jnp.int32), axis=1)
        mix_scores = jax.random.randint(jax.random.fold_in(sender_key, 1), (CAP,), 0, 1 << 16) * CAP + slots
        mix_scores = jnp.where(is_valid, mix_scores, (1 << 30) + slots)
        mixing = jnp.argsort(mix_scores)
        owner_of = jnp.where(is_valid, sorted_owner[mixing], 0)
        pair_hits = jnp.logical_and(owner_of[:, None] == jnp.arange(N_SEQ, dtype=jnp.int32)[None, :], is_valid[:, None]).astype(jnp.int32)
        pair_rank = jnp.sum(jnp.cumsum(pair_hits, axis=0) * pair_hits, axis=1) - 1
        offset = jnp.sum(pair_hits * before_row[None, :], axis=1)
        destination = jnp.where(is_valid, owner_of * ROUTED_DEV + offset + pair_rank, 0)
        picks = jax.random.permutation(jax.random.fold_in(sender_key, 2), TOK_DEV)[:CAP].astype(jnp.int32)
        chosen = jnp.sort(jnp.where(is_valid, picks, TOK_DEV + slots))
        chosen = jnp.where(is_valid, chosen, 0)
        return (chosen, destination)
    chosen, destination = jax.vmap(one_sender)(pair_load, before_rows, sender_counts, sender_keys)
    return (chosen.astype(jnp.int32), sender_counts.astype(jnp.int32), destination.astype(jnp.int32))


def draw_routed_index(key, part):
    plan = routing_plan(key)
    return plan[0]


def draw_routed_count(key, part):
    plan = routing_plan(key)
    return plan[1]


def draw_routed_dest(key, part):
    plan = routing_plan(key)
    return plan[2]


def levels(own_key, extent, cuts, low, top_value):
    level = 1.0
    for dim, shards_of in cuts:
        heights = jax.random.uniform(jax.random.fold_in(jax.random.fold_in(own_key, 6), dim), (shards_of,), jnp.float32, low / len(cuts), top_value / len(cuts))
        level = level * jnp.repeat(jnp.exp(heights), extent[dim] // shards_of).reshape((-1,) + (1,) * (len(extent) - 1 - dim))
    return level


def gaussian(own_key, dims, width, reach, shards=(), kind=jnp.bfloat16):
    entries = width * jax.random.normal(own_key, dims, jnp.float32)
    if shards:
        entries = entries * levels(own_key, dims, shards, -0.22, 0.18)
    return jnp.clip(entries, -reach, reach).astype(kind)


def setup_inputs(seed: int = 0) -> dict:
    streams_of = jax.random.split(jax.random.key(seed), 12)
    tokens = gaussian(streams_of[0], (TOKENS, D), 1.0, 6.0, ((0, 32), (1, 4)))
    cotangent = gaussian(streams_of[1], (TOKENS, D), 1.0, 6.0, ((0, 32), (1, 4)))
    norm_gain = jnp.clip(jnp.exp(jax.random.uniform(streams_of[2], (D,), jnp.float32, math.log(0.5), math.log(2.0))), 0.5, 2.0)
    router_weight = gaussian(streams_of[3], (D,), D ** -0.5, 0.09375, (), jnp.float32)
    w_query = gaussian(streams_of[4], (D, HEADS * HEAD_DIM), D ** -0.5, 0.09375, ((1, 4),))
    w_key = gaussian(streams_of[5], (D, KV_HEADS * HEAD_DIM), D ** -0.5, 0.09375, ((1, 4),))
    w_value = gaussian(streams_of[6], (D, KV_HEADS * HEAD_DIM), D ** -0.5, 0.09375, ((1, 4),))
    w_out = gaussian(streams_of[7], (HEADS * HEAD_DIM, D), (HEADS * HEAD_DIM) ** -0.5, 0.125, ((0, 4),))
    routed_index = draw_routed_index(jax.random.fold_in(streams_of[11], 71), 0)
    routed_count = draw_routed_count(jax.random.fold_in(streams_of[11], 71), 0)
    routed_dest = draw_routed_dest(jax.random.fold_in(streams_of[11], 71), 0)
    return {"tokens": tokens, "cotangent": cotangent, "norm_gain": norm_gain, "router_weight": router_weight, "w_query": w_query, "w_key": w_key, "w_value": w_value, "w_out": w_out, "routed_index": routed_index, "routed_count": routed_count, "routed_dest": routed_dest}


norm_eps = 1e-05
score_cap = 5.0

def settle(array):
    return lax.optimization_barrier(array.astype(jnp.bfloat16)).astype(jnp.float32)

def head_forward(query_head, key_head, value_head, position):
    key_count = key_head.shape[0]
    row_block = min(512, key_count)
    score_scale = HEAD_DIM ** (-0.5)

    def one_block(block_start):
        rows_q = lax.dynamic_slice_in_dim(query_head, block_start, row_block, 0)
        rows_pos = lax.dynamic_slice_in_dim(position, block_start, row_block, 0)
        tanh_score = jnp.tanh(jnp.einsum('rgd,kd->rgk', rows_q, key_head) * score_scale / score_cap)
        live_mask = position[None, None, :] <= rows_pos[:, None, None]
        weights_un = jnp.where(live_mask, jnp.exp(score_cap * tanh_score), 0.0)
        denominator = lax.optimization_barrier(jnp.sum(weights_un, axis=2))
        numerator = jnp.einsum('rgk,kd->rgd', settle(weights_un), value_head)
        return ((numerator / denominator[:, :, None]).astype(jnp.bfloat16), denominator)
    starts = jnp.arange(key_count // row_block, dtype=jnp.int32) * row_block
    attended, denominator = lax.map(one_block, starts)
    return (attended.reshape(key_count, -1, HEAD_DIM), denominator.reshape(key_count, -1))

def head_backward(query_head, key_head, value_head, position, grad_head, denominator, row_delta):
    key_count = key_head.shape[0]
    row_block = min(512, key_count)
    score_scale = HEAD_DIM ** (-0.5)

    def one_block(running, block_start):
        key_sum, value_sum = running
        rows_q = lax.dynamic_slice_in_dim(query_head, block_start, row_block, 0)
        rows_pos = lax.dynamic_slice_in_dim(position, block_start, row_block, 0)
        rows_grad = lax.dynamic_slice_in_dim(grad_head, block_start, row_block, 0)
        rows_den = lax.dynamic_slice_in_dim(denominator, block_start, row_block, 0)
        rows_delta = lax.dynamic_slice_in_dim(row_delta, block_start, row_block, 0)
        tanh_score = jnp.tanh(jnp.einsum('rgd,kd->rgk', rows_q, key_head) * score_scale / score_cap)
        live_mask = position[None, None, :] <= rows_pos[:, None, None]
        prob = jnp.where(live_mask, jnp.exp(score_cap * tanh_score), 0.0) / rows_den[:, :, None]
        prob_grad = jnp.einsum('rgd,kd->rgk', rows_grad, value_head)
        raw_grad = settle(prob * (prob_grad - rows_delta[:, :, None]) * (1.0 - tanh_score * tanh_score))
        prob_round = settle(prob)
        query_part = jnp.einsum('rgk,kd->rgd', raw_grad, key_head) * score_scale
        key_sum = key_sum + jnp.einsum('rgk,rgd->kd', raw_grad, rows_q) * score_scale
        value_sum = value_sum + jnp.einsum('rgk,rgd->kd', prob_round, rows_grad)
        return ((key_sum, value_sum), query_part.astype(jnp.bfloat16))
    empty = jnp.zeros((key_count, HEAD_DIM), jnp.float32)
    starts = jnp.arange(key_count // row_block, dtype=jnp.int32) * row_block
    (key_sum, value_sum), query_grad = lax.scan(one_block, (empty, empty), starts)
    return (query_grad.reshape(key_count, -1, HEAD_DIM), key_sum, value_sum)

def reference(tokens, cotangent, norm_gain, router_weight, w_query, w_key, w_value, w_out, routed_index, routed_count, routed_dest):
    routed_total = ROUTED_DEV * N_SEQ
    group_size = HEADS // KV_HEADS
    slots = jnp.arange(CAP, dtype=jnp.int32)
    is_valid = slots[None, :] < routed_count[:, None]
    token_pos = routed_index + (jnp.arange(N_SEQ, dtype=jnp.int32) * TOK_DEV)[:, None]
    target = jnp.where(is_valid, routed_dest, routed_total).reshape(-1).astype(jnp.int32)
    position = jnp.zeros((routed_total,), jnp.int32).at[target].set(token_pos.reshape(-1).astype(jnp.int32), mode='drop')
    x_rows = tokens[position]
    dy_rows = cotangent[position]
    x_float = x_rows.astype(jnp.float32)
    inv_rms = lax.rsqrt(lax.optimization_barrier(jnp.mean(x_float * x_float, axis=1)) + norm_eps)
    normed = (x_float * inv_rms[:, None] * norm_gain[None, :]).astype(jnp.bfloat16)
    router = lax.optimization_barrier(jnp.sum(x_float * router_weight[None, :], axis=1))
    query_proj = jnp.dot(normed, w_query, preferred_element_type=jnp.float32).astype(jnp.bfloat16)
    key_proj = jnp.dot(normed, w_key, preferred_element_type=jnp.float32).astype(jnp.bfloat16)
    value_proj = jnp.dot(normed, w_value, preferred_element_type=jnp.float32).astype(jnp.bfloat16)
    query_heads = query_proj.astype(jnp.float32).reshape(routed_total, KV_HEADS, group_size, HEAD_DIM).transpose(1, 0, 2, 3)
    key_heads = key_proj.astype(jnp.float32).reshape(routed_total, KV_HEADS, HEAD_DIM).transpose(1, 0, 2)
    value_heads = value_proj.astype(jnp.float32).reshape(routed_total, KV_HEADS, HEAD_DIM).transpose(1, 0, 2)
    attended, denominator = lax.map(lambda pieces: head_forward(pieces[0], pieces[1], pieces[2], position), (query_heads, key_heads, value_heads))
    flat_att = attended.transpose(1, 0, 2, 3).reshape(routed_total, HEADS * HEAD_DIM)
    block_out = jnp.dot(flat_att, w_out, preferred_element_type=jnp.float32)
    dy_float = dy_rows.astype(jnp.float32)
    router_grad = lax.optimization_barrier(jnp.sum(dy_float * block_out, axis=1))
    out_grad = (router[:, None] * dy_float).astype(jnp.bfloat16)
    att_grad = jnp.dot(out_grad, w_out.T, preferred_element_type=jnp.float32).astype(jnp.bfloat16)
    grad_heads = att_grad.astype(jnp.float32).reshape(routed_total, KV_HEADS, group_size, HEAD_DIM).transpose(1, 0, 2, 3)
    row_delta = lax.optimization_barrier(jnp.sum(grad_heads * attended.astype(jnp.float32), axis=3))
    query_grad, key_sum, value_sum = lax.map(lambda pieces: head_backward(pieces[0], pieces[1], pieces[2], position, pieces[3], pieces[4], pieces[5]), (query_heads, key_heads, value_heads, grad_heads, denominator, row_delta))
    query_grad = query_grad.transpose(1, 0, 2, 3).reshape(routed_total, HEADS * HEAD_DIM)
    key_grad = key_sum.astype(jnp.bfloat16).transpose(1, 0, 2).reshape(routed_total, KV_HEADS * HEAD_DIM)
    value_grad = value_sum.astype(jnp.bfloat16).transpose(1, 0, 2).reshape(routed_total, KV_HEADS * HEAD_DIM)
    summed = jnp.dot(query_grad, w_query.T, preferred_element_type=jnp.float32)
    summed = summed + jnp.dot(key_grad, w_key.T, preferred_element_type=jnp.float32)
    summed = summed + jnp.dot(value_grad, w_value.T, preferred_element_type=jnp.float32)
    normed_grad = norm_gain[None, :] * summed
    stat = lax.optimization_barrier(jnp.sum(x_float * normed_grad, axis=1))
    branch = (inv_rms[:, None] * normed_grad - x_float * (inv_rms * inv_rms * inv_rms * stat / D)[:, None] + router_weight[None, :] * router_grad[:, None]).astype(jnp.bfloat16)
    updated = (dy_float + branch.astype(jnp.float32)).astype(jnp.bfloat16)
    return cotangent.at[position].set(updated)
```

```python
import functools

import jax
import jax.numpy as jnp
from jax import lax
from jax.experimental import pallas as pl
from jax.experimental.pallas import tpu as pltpu
from jax.sharding import PartitionSpec as P

HEAD_DIM = 128
ROUTED_DEV = 256
KEY_BLOCK = 512

norm_eps = 1e-05
score_cap = 5.0
LOG2E = 1.4426950408889634
SCALE = HEAD_DIM ** (-0.5)

NT = (((1,), (1,)), ((), ()))
NN = (((1,), (0,)), ((), ()))


def dot(a, b, dims=NN):
    return lax.dot_general(a, b, dims, preferred_element_type=jnp.float32)


def live(kpos_row, qpos):
    width = kpos_row.shape[1]
    parts = [kpos_row[:, c : c + 128] <= qpos for c in range(0, width, 128)]
    return jnp.concatenate(parts, axis=1)


def wide(column, width):
    return jnp.concatenate([column] * (width // 128), axis=1)


def forward_kernel(heads, q_ref, qpos_ref, k_ref, v_ref, kpos_ref, att_ref, lden_ref, acc, den):
    step = pl.program_id(0)

    @pl.when(step == 0)
    def _():
        acc[...] = jnp.zeros_like(acc)
        den[...] = jnp.zeros_like(den)

    keys = k_ref[...]
    values = v_ref[...]
    mask = live(kpos_ref[0], qpos_ref[...])
    for h in range(heads):
        cols = slice(h * HEAD_DIM, (h + 1) * HEAD_DIM)
        t = jnp.tanh(dot(q_ref[:, cols], keys, NT) * (SCALE / score_cap))
        w = jnp.where(mask, jnp.exp2(t * (score_cap * LOG2E)), 0.0)
        part = w[:, :128]
        for c in range(128, w.shape[1], 128):
            part = part + w[:, c : c + 128]
        den[h] += part
        acc[h] += dot(w.astype(jnp.bfloat16), values)

    @pl.when(step == pl.num_programs(0) - 1)
    def _():
        for h in range(heads):
            cols = slice(h * HEAD_DIM, (h + 1) * HEAD_DIM)
            total = jnp.sum(den[h], axis=1, keepdims=True)
            att_ref[:, cols] = (acc[h] / total).astype(jnp.bfloat16)
            lden_ref[h] = jnp.broadcast_to(jnp.log2(total), lden_ref.shape[1:])


def backward_kernel(
    heads, q_ref, qt_ref, g_ref, gt_ref, lden_ref, delta_ref, qpos_ref, k_ref, v_ref, kpos_ref,
    dq_ref, dkv_ref
):
    step = pl.program_id(0)

    @pl.when(step == 0)
    def _():
        dq_ref[...] = jnp.zeros_like(dq_ref)

    keys = k_ref[...]
    values = v_ref[...]
    width = keys.shape[0]
    mask = live(kpos_ref[0], qpos_ref[...])
    dk = jnp.zeros((HEAD_DIM, width), jnp.float32)
    dv = jnp.zeros((HEAD_DIM, width), jnp.float32)
    for h in range(heads):
        cols = slice(h * HEAD_DIM, (h + 1) * HEAD_DIM)
        t = jnp.tanh(dot(q_ref[:, cols], keys, NT) * (SCALE / score_cap))
        p = jnp.exp2(t * (score_cap * LOG2E) - wide(lden_ref[h], width))
        p = jnp.where(mask, p, 0.0)
        dp = dot(g_ref[:, cols], values, NT)
        ds = (p * (dp - wide(delta_ref[h], width)) * (1.0 - t * t)).astype(jnp.bfloat16)
        dv = dv + dot(gt_ref[cols, :], p.astype(jnp.bfloat16))
        dk = dk + dot(qt_ref[cols, :], ds)
        dq_ref[:, cols] += dot(ds, keys)
    rows = dkv_ref.shape[2]
    for b in range(width // rows):
        span = slice(b * rows, (b + 1) * rows)
        dkv_ref[b, :HEAD_DIM, :] = dk[:, span] * SCALE
        dkv_ref[b, HEAD_DIM:, :] = dv[:, span]


def whole(shape):
    return pl.BlockSpec(shape, lambda i: (0,) * len(shape))


PARAMS = pltpu.CompilerParams(
    dimension_semantics=("arbitrary",), vmem_limit_bytes=48 * 1024 * 1024
)


def attention_forward(queries, qpos, keys, values, kpos):
    rows, cols = queries.shape
    heads = cols // HEAD_DIM
    steps = keys.shape[0] // KEY_BLOCK
    block = pl.BlockSpec((KEY_BLOCK, HEAD_DIM), lambda i: (i, 0))
    return pl.pallas_call(
        functools.partial(forward_kernel, heads),
        grid=(steps,),
        in_specs=[
            whole((rows, cols)),
            whole((rows, 128)),
            block,
            block,
            pl.BlockSpec((1, 1, KEY_BLOCK), lambda i: (i, 0, 0)),
        ],
        out_specs=[whole((rows, cols)), whole((heads, rows, 128))],
        out_shape=[
            jax.ShapeDtypeStruct((rows, cols), jnp.bfloat16),
            jax.ShapeDtypeStruct((heads, rows, 128), jnp.float32),
        ],
        scratch_shapes=[
            pltpu.VMEM((heads, rows, HEAD_DIM), jnp.float32),
            pltpu.VMEM((heads, rows, 128), jnp.float32),
        ],
        compiler_params=PARAMS,
        name="attention_forward",
    )(queries, qpos, keys, values, kpos)


def attention_backward(queries, grads, lden, delta, qpos, keys, values, kpos):
    rows, cols = queries.shape
    heads = cols // HEAD_DIM
    steps = keys.shape[0] // KEY_BLOCK
    block = pl.BlockSpec((KEY_BLOCK, HEAD_DIM), lambda i: (i, 0))
    owners = KEY_BLOCK // ROUTED_DEV
    return pl.pallas_call(
        functools.partial(backward_kernel, heads),
        grid=(steps,),
        in_specs=[
            whole((rows, cols)),
            whole((cols, rows)),
            whole((rows, cols)),
            whole((cols, rows)),
            whole((heads, rows, 128)),
            whole((heads, rows, 128)),
            whole((rows, 128)),
            block,
            block,
            pl.BlockSpec((1, 1, KEY_BLOCK), lambda i: (i, 0, 0)),
        ],
        out_specs=[
            whole((rows, cols)),
            pl.BlockSpec((owners, 2 * HEAD_DIM, ROUTED_DEV), lambda i: (i, 0, 0)),
        ],
        out_shape=[
            jax.ShapeDtypeStruct((rows, cols), jnp.float32),
            jax.ShapeDtypeStruct(
                (steps * owners, 2 * HEAD_DIM, ROUTED_DEV), jnp.float32
            ),
        ],
        compiler_params=PARAMS,
        name="attention_backward",
    )(queries, queries.T, grads, grads.T, lden, delta, qpos, keys, values, kpos)


def on_device(
    tokens,
    cotangent,
    norm_gain,
    router_weight,
    w_query,
    w_key,
    w_value,
    w_out,
    routed_index,
    routed_count,
    routed_dest,
):
    seq_devices = lax.axis_size("seq")
    tok_rows, quarter = tokens.shape
    owner_rows = ROUTED_DEV
    pair_slots = 2 * owner_rows // seq_devices
    capacity = routed_index.shape[1]
    local_heads = w_query.shape[1] // HEAD_DIM
    model_width = norm_gain.shape[0]
    buffer_rows = seq_devices * pair_slots
    bf16 = jnp.bfloat16
    listed = jnp.arange(capacity, dtype=jnp.int32)
    is_valid = listed < routed_count[0]
    local_rows = routed_index[0]
    target = routed_dest[0]
    owner_index = jnp.where(is_valid, target // owner_rows, seq_devices)
    place_slot = target % owner_rows
    earlier = jnp.logical_and(
        owner_index[:, None] == owner_index[None, :], listed[None, :] < listed[:, None]
    )
    pair_rank = jnp.sum(earlier.astype(jnp.int32), axis=1)
    buffer_place = jnp.where(is_valid, owner_index * pair_slots + pair_rank, buffer_rows)
    slots = jnp.arange(buffer_rows, dtype=jnp.int32)
    hit = slots[:, None] == buffer_place[None, :]

    def placed(entries, empty):
        found = jnp.sum(jnp.where(hit, entries[None, :] - empty, 0), axis=1)
        return found + empty

    source = placed(local_rows, tok_rows)
    slot_buffer = placed(place_slot, owner_rows)
    pos_buffer = placed(lax.axis_index("seq") * tok_rows + local_rows, 0)
    row_meta = jnp.stack([slot_buffer, pos_buffer], axis=1)
    pick = (source[:, None] == jnp.arange(tok_rows, dtype=jnp.int32)[None, :]).astype(bf16)
    send_x = dot(pick, tokens).astype(bf16)
    send_dy = dot(pick, cotangent).astype(bf16)
    got_meta = lax.all_to_all(row_meta, "seq", split_axis=0, concat_axis=0, tiled=True)
    got_x = lax.all_to_all(send_x, "seq", split_axis=0, concat_axis=0, tiled=True)
    got_dy = lax.all_to_all(send_dy, "seq", split_axis=0, concat_axis=0, tiled=True)
    slot_in = got_meta[:, 0]
    place_hit = jnp.arange(owner_rows, dtype=jnp.int32)[:, None] == slot_in[None, :]
    place = place_hit.astype(bf16)
    compact_x = dot(place, got_x).astype(bf16)
    compact_dy = dot(place, got_dy).astype(bf16)
    row_pos = jnp.sum(jnp.where(place_hit, got_meta[:, 1][None, :], 0), axis=1)
    full_x, full_dy = (
        lax.all_gather(compact_x, "mp", axis=1, tiled=True),
        lax.all_gather(compact_dy, "mp", axis=1, tiled=True),
    )
    x_float = full_x.astype(jnp.float32)
    inv_rms = lax.rsqrt(jnp.mean(x_float * x_float, axis=1) + norm_eps)
    normed = (x_float * inv_rms[:, None] * norm_gain[None, :]).astype(bf16)
    router = jnp.sum(x_float * router_weight[None, :], axis=1)
    queries = dot(normed, w_query).astype(bf16)
    key_rows = dot(normed, w_key).astype(bf16)
    value_rows = dot(normed, w_value).astype(bf16)
    all_keys, all_values, all_pos = (
        lax.all_gather(key_rows, "seq", axis=0, tiled=True),
        lax.all_gather(value_rows, "seq", axis=0, tiled=True),
        lax.all_gather(row_pos, "seq", axis=0, tiled=True),
    )
    kpos = all_pos.reshape(-1, 1, KEY_BLOCK)
    qpos = jnp.broadcast_to(row_pos[:, None], (owner_rows, 128))
    attended, lden = attention_forward(queries, qpos, all_keys, all_values, kpos)
    pulled = dot(full_dy, w_out, NT)
    att_grad = (router[:, None] * pulled).astype(bf16)
    heads_shape = (owner_rows, local_heads, HEAD_DIM)
    att_float = attended.astype(jnp.float32)
    router_part = jnp.sum(pulled * att_float, axis=1)
    row_delta = jnp.sum((att_grad.astype(jnp.float32) * att_float).reshape(heads_shape), axis=2)
    delta = jnp.broadcast_to(row_delta.T[:, :, None], (local_heads, owner_rows, 128))
    query_sum, kv_parts = attention_backward(
        queries, att_grad, lden, delta, qpos, all_keys, all_values, kpos
    )
    kv_grad = lax.psum_scatter(kv_parts, "seq", scatter_dimension=0, tiled=True)[0]
    query_grad = (query_sum * SCALE).astype(bf16)
    key_grad = kv_grad[:HEAD_DIM].astype(bf16)
    value_grad = kv_grad[HEAD_DIM:].astype(bf16)
    summed = dot(w_query, query_grad, NT) + dot(w_key, key_grad) + dot(w_value, value_grad)
    normed_grad = lax.psum_scatter(
        norm_gain[:, None] * summed, "mp", scatter_dimension=0, tiled=True
    )
    x_part = compact_x.astype(jnp.float32).T
    feature_start = lax.axis_index("mp") * quarter
    router_part_w = lax.dynamic_slice_in_dim(router_weight, feature_start, quarter, 0)
    stat_part = jnp.sum(x_part * normed_grad, axis=0)
    router_grad, stat = lax.psum((router_part, stat_part), "mp")
    branch = (
        inv_rms[None, :] * normed_grad
        - x_part * (inv_rms * inv_rms * inv_rms * stat / model_width)[None, :]
        + router_part_w[:, None] * router_grad[None, :]
    ).astype(bf16)
    back_rows = dot(place, branch, (((0,), (1,)), ((), ()))).astype(bf16)
    returned = lax.all_to_all(back_rows, "seq", split_axis=0, concat_axis=0, tiled=True)
    put = (jnp.arange(tok_rows, dtype=jnp.int32)[:, None] == source[None, :]).astype(bf16)
    return (cotangent.astype(jnp.float32) + dot(put, returned)).astype(bf16)


def solution(mesh):
    in_specs = (
        P("seq", "mp"),
        P("seq", "mp"),
        P(),
        P(),
        P(None, "mp"),
        P(None, "mp"),
        P(None, "mp"),
        P("mp", None),
        P("seq", None),
        P("seq"),
        P("seq", None),
    )
    out_specs = P("seq", "mp")
    return jax.shard_map(
        on_device, mesh=mesh, in_specs=in_specs, out_specs=out_specs, check_vma=False
    )
```

```python
import jax
import jax.numpy as jnp
from jax import lax
from jax.experimental import pallas as pl
from jax.experimental.pallas import tpu as pltpu
from jax.sharding import PartitionSpec as P

HEAD_DIM = 128
ROUTED_DEV = 256
MESH = pl.DeviceIdType.MESH
NT = (((1,), (1,)), ((), ()))
NN = (((1,), (0,)), ((), ()))
TN = (((0,), (0,)), ((), ()))
MIB = 1024 * 1024
norm_eps = 1e-05
score_cap = 5.0
LOG2E = 1.4426950408889634
SCALE = HEAD_DIM ** (-0.5)


def dot(a, b, dims=NN):
    return lax.dot_general(a, b, dims, preferred_element_type=jnp.float32)


def iota(shape, dim):
    return lax.broadcasted_iota(jnp.int32, shape, dim)


def onehot(mask):
    return jnp.where(mask, 1.0, 0.0).astype(jnp.bfloat16)


def remote(src, dst, send_sem, recv_sem, axis, index):
    return pltpu.make_async_remote_copy(
        src_ref=src,
        dst_ref=dst,
        send_sem=send_sem,
        recv_sem=recv_sem,
        device_id={axis: index},
        device_id_type=MESH,
    )


def await_bytes(ref, sem):
    pltpu.make_async_copy(ref, ref, sem).wait()


def greet(axis, count):
    me = lax.axis_index(axis)
    barrier = pltpu.get_barrier_semaphore()

    def body(i, carry):
        pl.semaphore_signal(
            barrier, inc=1, device_id={axis: lax.rem(me + i, count)}, device_id_type=MESH
        )
        return carry

    lax.fori_loop(1, count, body, 0)


def send_pairs(peers, send, got, send_sem, recv_sem, rows):
    me = lax.axis_index("seq")
    mine = pl.ds(pl.multiple_of(me * rows, rows), rows)

    def body(i, carry):
        to = lax.rem(me + i, peers)
        block = send.at[pl.ds(pl.multiple_of(to * rows, rows), rows)]
        remote(block, got.at[mine], send_sem, recv_sem, "seq", to).start()
        return carry

    lax.fori_loop(1, peers, body, 0)
    got[mine, :] = send[mine, :]


def quarter_of(index, width):
    return pl.ds(pl.multiple_of(index * width, width), width)


def ring_send(full, send_sem, recv_sem, stage):
    m = lax.axis_index("mp")
    right, left = lax.rem(m + 1, 4), lax.rem(m + 3, 4)
    half = full.shape[0] // 2
    quarter = full.shape[1] // 4
    top, low = pl.ds(0, half), pl.ds(half, half)

    def move(block, rows, k, to):
        part = full.at[rows, quarter_of(block, quarter)]
        return remote(part, part, send_sem.at[k], recv_sem.at[k], "mp", to)

    if stage == 0:
        copies = [
            move(m, top, 0, right), move(m, low, 1, left),
            move(m, low, 2, right), move(m, top, 3, left),
        ]
        for c in copies:
            c.start()
    elif stage == 1:
        move(left, top, 0, right).wait_recv()
        move(left, top, 4, right).start()
        move(right, low, 1, left).wait_recv()
        move(right, low, 5, left).start()
    else:
        far = lax.rem(m + 2, 4)
        move(left, low, 2, right).wait_recv()
        move(right, top, 3, left).wait_recv()
        move(far, top, 4, right).wait_recv()
        move(far, low, 5, left).wait_recv()
        for k in range(6):
            move(m, top, k, right).wait_send()


def routing_kernel(
    idx_ref, dest_ref, count_ref, tok_hbm, cot_hbm,
    fullx, compactdy, place_ref, source_ref, qpos_ref, kpos_ref,
    tok, cot, pick, sendx, senddy, gotx, gotdy, sendm, gotm,
    load_sem, a2a_send, a2a_recv, mx_send, mx_recv,
):
    peers = lax.axis_size("seq")
    me = lax.axis_index("seq")
    m = lax.axis_index("mp")
    slots = sendx.shape[0]
    tok_rows, quarter = tok.shape
    pair = slots // peers
    load_x = pltpu.make_async_copy(tok_hbm, tok, load_sem.at[0])
    load_d = pltpu.make_async_copy(cot_hbm, cot, load_sem.at[1])
    load_x.start()
    load_d.start()
    greet("seq", peers)
    greet("mp", 4)

    idx = idx_ref[...]
    dest = dest_ref[...]
    listed = iota((1, slots), 1)
    valid = listed < count_ref[0]
    owner = jnp.where(valid, lax.shift_right_logical(dest, 8), peers)
    place_slot = jnp.bitwise_and(dest, ROUTED_DEV - 1)
    rows_i = iota((slots, slots), 0)
    cols_i = iota((slots, slots), 1)
    owner_col = jnp.sum(jnp.where(rows_i == cols_i, owner, 0), axis=1, keepdims=True)
    earlier = jnp.logical_and(owner_col == owner, rows_i < cols_i)
    rank = jnp.sum(jnp.where(earlier, 1, 0), axis=0, keepdims=True)
    buffer_place = jnp.where(valid, owner * pair + rank, slots)
    hit = rows_i == buffer_place
    source = jnp.sum(jnp.where(hit, idx - tok_rows, 0), axis=1, keepdims=True) + tok_rows
    pick[...] = onehot(iota((slots, tok_rows), 1) == source)
    source_row = jnp.sum(
        jnp.where(rows_i == cols_i, source, 0), axis=0, keepdims=True
    )
    source_ref[...] = jnp.broadcast_to(source_row, source_ref.shape)

    owner_hit = iota((peers, slots), 0) == owner
    rank_b = jnp.where(valid, rank, 128)
    lanes = iota((128, slots), 0)

    def spread(entries, shift):
        held = jnp.where(owner_hit, entries, 0).astype(jnp.float32).astype(jnp.bfloat16)
        return dot(held, onehot(lanes == rank_b + shift), NT)

    position = me * tok_rows + idx
    meta = (
        spread(place_slot + 1, 0)
        + spread(lax.shift_right_logical(position, 8), pair)
        + spread(jnp.bitwise_and(position, 255), 2 * pair)
    )
    sendm[...] = jnp.broadcast_to(meta[:, None, :], sendm.shape)

    barrier = pltpu.get_barrier_semaphore()
    pl.semaphore_wait(barrier, peers - 1 + 3)

    def send_meta(i, carry):
        to = lax.rem(me + i, peers)
        remote(
            sendm.at[to], gotm.at[me], a2a_send.at[2], a2a_recv.at[2], "seq", to
        ).start()
        return carry

    lax.fori_loop(1, peers, send_meta, 0)
    gotm[me] = sendm[me]

    def pack(held, send):
        def body(n, carry):
            cols = pl.ds(pl.multiple_of(n * 256, 256), 256)
            send[:, cols] = dot(pick[...], held[:, cols]).astype(jnp.bfloat16)
            return carry

        lax.fori_loop(0, quarter // 256, body, 0)

    load_x.wait()
    pack(tok, sendx)
    send_pairs(peers, sendx, gotx, a2a_send.at[0], a2a_recv.at[0], pair)
    load_d.wait()
    pack(cot, senddy)
    send_pairs(peers, senddy, gotdy, a2a_send.at[1], a2a_recv.at[1], pair)

    others = pl.ds(0, peers - 1)
    await_bytes(gotm.at[others], a2a_recv.at[2])
    got = gotm[:, 0, :].astype(jnp.bfloat16)
    column = iota((128, slots), 0)
    within = jnp.bitwise_and(iota((128, slots), 1), pair - 1)
    sender = iota((peers, slots), 0) == iota((peers, slots), 1) // pair

    def flat(shift):
        spread_out = dot(got, onehot(column == within + shift))
        return jnp.sum(jnp.where(sender, spread_out, 0.0), axis=0, keepdims=True)

    slot_in = flat(0)
    pos_in = flat(pair) * 256.0 + flat(2 * pair)
    here = iota((ROUTED_DEV, slots), 0).astype(jnp.float32) + 1.0 == slot_in
    place_ref[...] = onehot(here)
    qpos = jnp.sum(jnp.where(here, pos_in, 0.0), axis=1, keepdims=True)
    qpos_ref[...] = jnp.broadcast_to(qpos, qpos_ref.shape)
    eye = iota((ROUTED_DEV, ROUTED_DEV), 0) == iota((ROUTED_DEV, ROUTED_DEV), 1)
    kpos = jnp.sum(jnp.where(eye, qpos, 0.0), axis=0, keepdims=True)
    kpos_ref[...] = jnp.broadcast_to(kpos, kpos_ref.shape)

    def compact(got_rows, full, start):
        def body(n, carry):
            cols = pl.ds(pl.multiple_of(n * 256, 256), 256)
            to = pl.ds(pl.multiple_of(start + n * 256, 256), 256)
            full[:, to] = dot(place_ref[...], got_rows[:, cols]).astype(jnp.bfloat16)
            return carry

        lax.fori_loop(0, quarter // 256, body, 0)

    span = pl.ds(0, slots - pair)
    await_bytes(gotx.at[span], a2a_recv.at[0])
    compact(gotx, fullx, m * quarter)
    ring_send(fullx, mx_send, mx_recv, 0)
    await_bytes(gotdy.at[span], a2a_recv.at[1])
    compact(gotdy, compactdy, 0)
    ring_send(fullx, mx_send, mx_recv, 1)
    ring_send(fullx, mx_send, mx_recv, 2)
    await_bytes(sendx.at[span], a2a_send.at[0])
    await_bytes(senddy.at[span], a2a_send.at[1])
    await_bytes(sendm.at[others], a2a_send.at[2])


def route(tokens, cotangent, idx, count, dest):
    peers = lax.axis_size("seq")
    tok_rows, quarter = tokens.shape
    slots = 2 * ROUTED_DEV
    bf16, f32 = jnp.bfloat16, jnp.float32
    vmem = pl.BlockSpec(memory_space=pltpu.VMEM)
    shape = jax.ShapeDtypeStruct
    dma = pltpu.SemaphoreType.DMA
    return pl.pallas_call(
        routing_kernel,
        in_specs=[
            vmem, vmem, pl.BlockSpec(memory_space=pltpu.SMEM),
            pl.BlockSpec(memory_space=pl.ANY), pl.BlockSpec(memory_space=pl.ANY),
        ],
        out_specs=[vmem] * 6,
        out_shape=[
            shape((ROUTED_DEV, 4 * quarter), bf16),
            shape((ROUTED_DEV, quarter), bf16),
            shape((ROUTED_DEV, slots), bf16),
            shape((8, slots), jnp.int32),
            shape((ROUTED_DEV, 128), f32),
            shape((8, ROUTED_DEV), f32),
        ],
        scratch_shapes=[
            pltpu.VMEM((tok_rows, quarter), bf16),
            pltpu.VMEM((tok_rows, quarter), bf16),
            pltpu.VMEM((slots, tok_rows), bf16),
            pltpu.VMEM((slots, quarter), bf16),
            pltpu.VMEM((slots, quarter), bf16),
            pltpu.VMEM((slots, quarter), bf16),
            pltpu.VMEM((slots, quarter), bf16),
            pltpu.VMEM((peers, 8, 128), f32),
            pltpu.VMEM((peers, 8, 128), f32),
            dma((2,)), dma((3,)), dma((3,)), dma((6,)), dma((6,)),
        ],
        compiler_params=pltpu.CompilerParams(
            collective_id=0, has_side_effects=True, vmem_limit_bytes=48 * MIB
        ),
        name="route_rows",
    )(idx, dest, count, tokens, cotangent)


def live(kpos_row, qpos):
    parts = [kpos_row[:, c : c + 128] <= qpos for c in range(0, kpos_row.shape[1], 128)]
    return jnp.concatenate(parts, axis=1)


def wide(column, width):
    return jnp.concatenate([column] * (width // 128), axis=1)


class Place:
    def __init__(self):
        self.me = lax.axis_index("seq")
        self.c = lax.rem(self.me, 2)
        self.sa = 2 + 6 * self.c
        self.sb = 8 - 6 * self.c
        self.a = lax.rem(self.me // self.sa, 4)
        self.b = lax.rem(self.me // self.sb, 4)
        self.sibling = self.me + 1 - 2 * self.c

    def mine(self, i, j):
        return (
            lax.rem(self.a + i, 4) * self.sa + lax.rem(self.b + j, 4) * self.sb + self.c
        )

    def theirs(self, i, j):
        return (
            lax.rem(self.b + i, 4) * self.sb
            + lax.rem(self.a + j, 4) * self.sa
            + 1 - self.c
        )

    def greet(self):
        barrier = pltpu.get_barrier_semaphore()

        def signal(to):
            pl.semaphore_signal(
                barrier, inc=1, device_id={"seq": to}, device_id_type=MESH
            )

        for i in range(1, 4):
            signal(self.mine(i, 0))
            signal(self.mine(0, i))
        signal(self.sibling)
        return 7


def key_block(kv, block):
    rows = kv[block]
    keys = rows[:ROUTED_DEV, :HEAD_DIM]
    values = rows[:ROUTED_DEV, HEAD_DIM:]
    digits = rows[ROUTED_DEV:].astype(jnp.float32)
    return keys, values, digits[0:1] * 256.0 + digits[1:2]


def forward_kernel(
    q_ref, key_ref, value_ref, qpos_ref, kpos_ref, dy_ref,
    att_ref, lden_ref, kv, fulldy,
    acc, den, send_sem, recv_sem, md_send, md_recv,
):
    at = Place()
    heads = acc.shape[0]
    rows = q_ref.shape[0]
    quarter = dy_ref.shape[1]
    waits = at.greet()
    greet("mp", 4)
    kpos = kpos_ref[0:1, :].astype(jnp.int32)
    digits = jnp.where(
        iota((16, rows), 0) == 0,
        lax.shift_right_logical(kpos, 8),
        jnp.bitwise_and(kpos, 255),
    )
    kv[at.me, :rows, :HEAD_DIM] = key_ref[...]
    kv[at.me, :rows, HEAD_DIM:] = value_ref[...]
    kv[at.me, rows:, :] = digits.astype(jnp.float32).astype(jnp.bfloat16)
    fulldy[:, quarter_of(lax.axis_index("mp"), quarter)] = dy_ref[...]
    acc[...] = jnp.zeros_like(acc)
    den[...] = jnp.zeros_like(den)
    pl.semaphore_wait(pltpu.get_barrier_semaphore(), waits + 3)

    def send(block, to):
        here = kv.at[block]
        remote(here, here, send_sem, recv_sem.at[block], "seq", to).start()

    def receive(block):
        await_bytes(kv.at[block], recv_sem.at[block])

    def process(block):
        keys, values, key_pos = key_block(kv, block)
        mask = live(key_pos, qpos_ref[...])
        for h in range(heads):
            cols = slice(h * HEAD_DIM, (h + 1) * HEAD_DIM)
            t = jnp.tanh(dot(q_ref[:, cols], keys, NT) * (SCALE / score_cap))
            w = jnp.where(mask, jnp.exp2(t * (score_cap * LOG2E)), 0.0)
            den[h] += w[:, :128] + w[:, 128:]
            acc[h] += dot(w.astype(jnp.bfloat16), values)

    for i in range(1, 4):
        send(at.me, at.mine(i, 0))
    send(at.me, at.sibling)
    for j in range(1, 4):
        send(at.me, at.mine(0, j))
    ring_send(fulldy, md_send, md_recv, 0)
    process(at.me)

    def order(t):
        late = (t + 12) // 16
        return lax.rem(t, 4), late * (t // 4)

    def step(t, carry):
        block = at.mine(*order(t))
        receive(block)

        @pl.when(t < 4)
        def _():
            for j in range(1, 4):
                send(block, at.mine(0, j))

        send(block, at.sibling)

        @pl.when(t == 6)
        def _():
            ring_send(fulldy, md_send, md_recv, 1)

        other = at.theirs(*order(t - 1))
        receive(other)
        process(other)
        process(block)
        return carry

    lax.fori_loop(1, 16, step, 0)
    last = at.theirs(*order(15))
    receive(last)
    process(last)
    for h in range(heads):
        cols = slice(h * HEAD_DIM, (h + 1) * HEAD_DIM)
        total = jnp.sum(den[h], axis=1, keepdims=True)
        att_ref[:, cols] = (acc[h] / total).astype(jnp.bfloat16)
        lden_ref[h] = jnp.broadcast_to(jnp.log2(total), lden_ref.shape[1:])
    ring_send(fulldy, md_send, md_recv, 2)
    await_bytes(kv.at[pl.ds(0, kv.shape[0] - 1)], send_sem)


def attend(queries, keys, values, qpos, kpos, compact_dy):
    peers = lax.axis_size("seq")
    rows, cols = queries.shape
    heads = cols // HEAD_DIM
    vmem = pl.BlockSpec(memory_space=pltpu.VMEM)
    shape = jax.ShapeDtypeStruct
    dma = pltpu.SemaphoreType.DMA
    return pl.pallas_call(
        forward_kernel,
        in_specs=[vmem] * 6,
        out_specs=[vmem] * 4,
        out_shape=[
            shape((rows, cols), jnp.bfloat16),
            shape((heads, rows, 128), jnp.float32),
            shape((peers, rows + 16, 2 * HEAD_DIM), jnp.bfloat16),
            shape((rows, 4 * compact_dy.shape[1]), jnp.bfloat16),
        ],
        scratch_shapes=[
            pltpu.VMEM((heads, rows, HEAD_DIM), jnp.float32),
            pltpu.VMEM((heads, rows, 128), jnp.float32),
            dma, dma((peers,)), dma((6,)), dma((6,)),
        ],
        compiler_params=pltpu.CompilerParams(
            collective_id=1, has_side_effects=True, vmem_limit_bytes=48 * MIB
        ),
        name="attention_forward",
    )(queries, keys, values, qpos, kpos, compact_dy)


def backward_kernel(
    q_ref, qt_ref, g_ref, gt_ref, lden_ref, delta_ref, qpos_ref, kv,
    dq_ref, dkv_ref,
    dq, to_sib, from_sib, to_b, from_b, to_a, from_a, sends, sib_recv, b_recv, a_recv,
):
    at = Place()
    heads = lden_ref.shape[0]
    waits = at.greet()
    dq[...] = jnp.zeros_like(dq)
    pl.semaphore_wait(pltpu.get_barrier_semaphore(), waits)

    def terms(block):
        keys, values, key_pos = key_block(kv, block)
        width = keys.shape[0]
        mask = live(key_pos, qpos_ref[...])
        dk = jnp.zeros((HEAD_DIM, width), jnp.float32)
        dv = jnp.zeros((HEAD_DIM, width), jnp.float32)
        for h in range(heads):
            cols = slice(h * HEAD_DIM, (h + 1) * HEAD_DIM)
            t = jnp.tanh(dot(q_ref[:, cols], keys, NT) * (SCALE / score_cap))
            p = jnp.exp2(t * (score_cap * LOG2E) - wide(lden_ref[h], width))
            p = jnp.where(mask, p, 0.0)
            dp = dot(g_ref[:, cols], values, NT)
            ds = (p * (dp - wide(delta_ref[h], width)) * (1.0 - t * t)).astype(jnp.bfloat16)
            dv = dv + dot(gt_ref[cols, :], p.astype(jnp.bfloat16))
            dk = dk + dot(qt_ref[cols, :], ds)
            dq[:, cols] += dot(ds, keys)
        return jnp.concatenate([dk * SCALE, dv], axis=0)

    def step(k, carry):
        late = k // 12
        j = (1 + k // 4) * (1 - late)
        i = lax.rem(k + late, 4)
        to_sib[k] = terms(at.theirs(i, j)).astype(jnp.bfloat16)
        remote(
            to_sib.at[k], from_sib.at[k], sends.at[0], sib_recv.at[k], "seq", at.sibling
        ).start()
        own = terms(at.mine(i, j))
        await_bytes(from_sib.at[k], sib_recv.at[k])
        own = own + from_sib[k].astype(jnp.float32)

        @pl.when(late == 0)
        def _():
            to_b[k] = own.astype(jnp.bfloat16)
            slot = (4 - j) * 4 + i
            remote(
                to_b.at[k], from_b.at[slot], sends.at[1], b_recv.at[slot], "seq",
                at.mine(0, j),
            ).start()

        @pl.when(late == 1)
        def _():
            total = own
            for n in range(1, 4):
                await_bytes(from_b.at[n * 4 + i], b_recv.at[n * 4 + i])
                total = total + from_b[n * 4 + i].astype(jnp.float32)

            @pl.when(k < 15)
            def _():
                to_a[i] = total.astype(jnp.bfloat16)
                slot = 4 - i
                remote(
                    to_a.at[i], from_a.at[slot], sends.at[2], a_recv.at[slot], "seq",
                    at.mine(i, 0),
                ).start()

            @pl.when(k == 15)
            def _():
                final = total
                for n in range(1, 4):
                    await_bytes(from_a.at[n], a_recv.at[n])
                    final = final + from_a[n].astype(jnp.float32)
                dkv_ref[...] = final.T.astype(jnp.bfloat16)

        return carry

    lax.fori_loop(0, 16, step, 0)
    dq_ref[...] = (dq[...] * SCALE).astype(jnp.bfloat16)
    await_bytes(to_sib, sends.at[0])
    await_bytes(to_b, sends.at[1])
    await_bytes(to_a.at[pl.ds(0, 3)], sends.at[2])


def attend_backward(queries, grads, lden, delta, qpos, kv):
    rows, cols = queries.shape
    vmem = pl.BlockSpec(memory_space=pltpu.VMEM)
    shape = jax.ShapeDtypeStruct
    dma = pltpu.SemaphoreType.DMA

    def held(n):
        return pltpu.VMEM((n, 2 * HEAD_DIM, rows), jnp.bfloat16)

    return pl.pallas_call(
        backward_kernel,
        in_specs=[vmem] * 8,
        out_specs=[vmem] * 2,
        out_shape=[
            shape((rows, cols), jnp.bfloat16),
            shape((rows, 2 * HEAD_DIM), jnp.bfloat16),
        ],
        scratch_shapes=[
            pltpu.VMEM((rows, cols), jnp.float32),
            held(16), held(16), held(12), held(16), held(4), held(4),
            dma((3,)), dma((16,)), dma((16,)), dma((4,)),
        ],
        compiler_params=pltpu.CompilerParams(
            collective_id=2, has_side_effects=True, vmem_limit_bytes=48 * MIB
        ),
        name="attention_backward",
    )(queries, queries.T, grads, grads.T, lden, delta, qpos, kv)


def as_row(column):
    size = column.shape[0]
    eye = iota((size, size), 0) == iota((size, size), 1)
    return jnp.sum(jnp.where(eye, column, 0.0), axis=0, keepdims=True)


def as_column(row):
    size = row.shape[1]
    eye = iota((size, size), 0) == iota((size, size), 1)
    return jnp.sum(jnp.where(eye, row, 0.0), axis=1, keepdims=True)


def return_kernel(
    dq_ref, dkv_ref, wq_ref, wk_ref, wv_ref, gain_ref, rw_ref, x_ref, inv_ref, part_ref,
    place_ref, got,
    far, near, own, relay, arrived, branch, back, stats, sends, recvs, pair_sems,
):
    peers = lax.axis_size("seq")
    me = lax.axis_index("seq")
    m = lax.axis_index("mp")
    right, left = lax.rem(m + 1, 4), lax.rem(m + 3, 4)
    rows, quarter = x_ref.shape
    half = rows // 2
    slots = got.shape[0]
    pair = slots // peers
    tile = 256
    greet("seq", peers)
    greet("mp", 4)

    def contribution(index, write):
        def body(n, carry):
            f = pl.ds(pl.multiple_of(index * quarter + n * tile, tile), tile)
            cols = pl.ds(pl.multiple_of(n * tile, tile), tile)
            total = dot(dq_ref[...], wq_ref[f, :], NT)
            total = total + dot(dkv_ref[:, :HEAD_DIM], wk_ref[f, :], NT)
            total = total + dot(dkv_ref[:, HEAD_DIM:], wv_ref[f, :], NT)
            write(cols, total * gain_ref[:, f])
            return carry

        lax.fori_loop(0, quarter // tile, body, 0)

    def send(src, dst, k, to):
        copy = remote(src, dst, sends.at[k], recvs.at[k], "mp", to)
        copy.start()
        return copy

    def write_far(cols, total):
        far[:, cols] = total.astype(jnp.bfloat16)

    contribution(lax.rem(m + 2, 4), write_far)
    pl.semaphore_wait(pltpu.get_barrier_semaphore(), peers - 1 + 3)
    top, low = pl.ds(0, half), pl.ds(half, half)
    copies = [
        send(far.at[top], relay.at[0], 0, right),
        send(far.at[low], relay.at[1], 1, left),
    ]

    def write_near(side):
        def write(cols, total):
            near[side, :, cols] = total.astype(jnp.bfloat16)

        return write

    contribution(right, write_near(0))
    copies.append(send(near.at[0, low], arrived.at[0, low], 2, right))
    contribution(left, write_near(1))
    copies.append(send(near.at[1, top], arrived.at[1, top], 3, left))

    def add(side, span):
        summed = near[side, span, :].astype(jnp.float32)
        summed = summed + relay[side].astype(jnp.float32)
        near[side, span, :] = summed.astype(jnp.bfloat16)

    copies[0].wait_recv()
    add(0, slice(0, half))
    copies.append(send(near.at[0, top], arrived.at[0, top], 4, right))
    copies[1].wait_recv()
    add(1, slice(half, rows))
    copies.append(send(near.at[1, low], arrived.at[1, low], 5, left))

    def write_own(cols, total):
        own[:, cols] = total

    contribution(m, write_own)
    for c in copies[2:]:
        c.wait_recv()
    normed_grad = own[...] + arrived[0].astype(jnp.float32) + arrived[1].astype(jnp.float32)
    own[...] = normed_grad
    x = x_ref[...].astype(jnp.float32)
    stat = jnp.sum(x * normed_grad, axis=1, keepdims=True)
    first = iota((8, rows), 0) == 0
    stats[m] = jnp.where(first, as_row(stat), as_row(part_ref[:, 0:1]))

    def send_stats(i, carry):
        to = lax.rem(m + i, 4)
        remote(
            stats.at[m], stats.at[m], pair_sems.at[2], pair_sems.at[3], "mp", to
        ).start()
        return carry

    lax.fori_loop(1, 4, send_stats, 0)
    await_bytes(stats.at[pl.ds(0, 3)], pair_sems.at[3])
    sums = stats[0] + stats[1] + stats[2] + stats[3]
    stat = as_column(sums[0:1])
    router_grad = as_column(sums[1:2])
    inv = inv_ref[:, 0:1]
    factor = inv * inv * inv * stat * (1.0 / (4 * quarter))
    weight = rw_ref[:, quarter_of(m, quarter)]
    branch[...] = (
        inv * own[...] - x * factor + weight * router_grad
    ).astype(jnp.bfloat16)

    def unplace(n, carry):
        cols = pl.ds(pl.multiple_of(n * tile, tile), tile)
        back[:, cols] = dot(place_ref[...], branch[:, cols], TN).astype(jnp.bfloat16)
        return carry

    lax.fori_loop(0, quarter // tile, unplace, 0)
    send_pairs(peers, back, got, pair_sems.at[0], pair_sems.at[1], pair)
    for c in copies:
        c.wait_send()
    await_bytes(stats.at[pl.ds(0, 3)], pair_sems.at[2])
    span = pl.ds(0, slots - pair)
    await_bytes(got.at[span], pair_sems.at[1])
    await_bytes(back.at[span], pair_sems.at[0])


def give_back(dq, dkv, w_query, w_key, w_value, gain, router_weight, x, inv, part, place):
    rows, quarter = x.shape
    slots = place.shape[1]
    vmem = pl.BlockSpec(memory_space=pltpu.VMEM)
    bf16, f32 = jnp.bfloat16, jnp.float32
    dma = pltpu.SemaphoreType.DMA
    return pl.pallas_call(
        return_kernel,
        in_specs=[vmem] * 11,
        out_specs=vmem,
        out_shape=jax.ShapeDtypeStruct((slots, quarter), bf16),
        scratch_shapes=[
            pltpu.VMEM((rows, quarter), bf16),
            pltpu.VMEM((2, rows, quarter), bf16),
            pltpu.VMEM((rows, quarter), f32),
            pltpu.VMEM((2, rows // 2, quarter), bf16),
            pltpu.VMEM((2, rows, quarter), bf16),
            pltpu.VMEM((rows, quarter), bf16),
            pltpu.VMEM((slots, quarter), bf16),
            pltpu.VMEM((4, 8, rows), f32),
            dma((6,)), dma((6,)), dma((4,)),
        ],
        compiler_params=pltpu.CompilerParams(
            collective_id=3, has_side_effects=True, vmem_limit_bytes=48 * MIB
        ),
        name="return_rows",
    )(dq, dkv, w_query, w_key, w_value, gain, router_weight, x, inv, part, place)


def on_device(
    tokens,
    cotangent,
    norm_gain,
    router_weight,
    w_query,
    w_key,
    w_value,
    w_out,
    routed_index,
    routed_count,
    routed_dest,
):
    tok_rows, quarter = tokens.shape
    rows = ROUTED_DEV
    local_heads = w_query.shape[1] // HEAD_DIM
    bf16 = jnp.bfloat16
    full_x, compact_dy, place, source, qpos, kpos = route(
        tokens, cotangent, routed_index, routed_count, routed_dest
    )
    x_float = full_x.astype(jnp.float32)
    inv_rms = lax.rsqrt(jnp.mean(x_float * x_float, axis=1, keepdims=True) + norm_eps)
    normed = (x_float * inv_rms * norm_gain[None, :]).astype(bf16)
    router = jnp.sum(x_float * router_weight[None, :], axis=1)
    queries = dot(normed, w_query).astype(bf16)
    key_rows = dot(normed, w_key).astype(bf16)
    value_rows = dot(normed, w_value).astype(bf16)
    attended, lden, kv, full_dy = attend(
        queries, key_rows, value_rows, qpos, kpos, compact_dy
    )
    pulled = dot(full_dy, w_out, NT)
    att_grad = (router[:, None] * pulled).astype(bf16)
    att_float = attended.astype(jnp.float32)
    router_part = jnp.sum(pulled * att_float, axis=1, keepdims=True)
    products = (att_grad.astype(jnp.float32) * att_float).reshape(rows, local_heads, HEAD_DIM)
    delta = jnp.broadcast_to(
        jnp.sum(products, axis=2).T[:, :, None], (local_heads, rows, 128)
    )
    dq, dkv = attend_backward(queries, att_grad, lden, delta, qpos, kv)
    feature_start = lax.axis_index("mp") * quarter
    x = lax.dynamic_slice_in_dim(full_x, feature_start, quarter, 1)
    returned = give_back(
        dq,
        dkv,
        w_query,
        w_key,
        w_value,
        norm_gain[None, :],
        router_weight[None, :],
        x,
        jnp.broadcast_to(inv_rms, (rows, 128)),
        jnp.broadcast_to(router_part, (rows, 128)),
        place,
    )
    put = (jnp.arange(tok_rows, dtype=jnp.int32)[:, None] == source[0:1]).astype(bf16)
    return (cotangent.astype(jnp.float32) + dot(put, returned)).astype(bf16)


def solution(mesh):
    in_specs = (
        P("seq", "mp"),
        P("seq", "mp"),
        P(),
        P(),
        P(None, "mp"),
        P(None, "mp"),
        P(None, "mp"),
        P("mp", None),
        P("seq", None),
        P("seq"),
        P("seq", None),
    )
    out_specs = P("seq", "mp")
    return jax.shard_map(
        on_device, mesh=mesh, in_specs=in_specs, out_specs=out_specs, check_vma=False
    )
```

```python
import jax
import jax.numpy as jnp
from jax import lax
from jax.experimental import pallas as pl
from jax.experimental.pallas import tpu as pltpu
from jax.sharding import PartitionSpec as P

HEAD_DIM = 128
ROUTED_DEV = 256
MESH = pl.DeviceIdType.MESH
NT = (((1,), (1,)), ((), ()))
NN = (((1,), (0,)), ((), ()))
TN = (((0,), (0,)), ((), ()))
MIB = 1024 * 1024
VMEM_LIMIT = 60 * MIB
norm_eps = 1e-05
score_cap = 5.0
LOG2E = 1.4426950408889634
SCALE = HEAD_DIM ** (-0.5)


def dot(a, b, dims=NN):
    return lax.dot_general(a, b, dims, preferred_element_type=jnp.float32)


def iota(shape, dim):
    return lax.broadcasted_iota(jnp.int32, shape, dim)


def onehot(mask):
    return jnp.where(mask, 1.0, 0.0).astype(jnp.bfloat16)


def remote(src, dst, send_sem, recv_sem, axis, index):
    return pltpu.make_async_remote_copy(
        src_ref=src,
        dst_ref=dst,
        send_sem=send_sem,
        recv_sem=recv_sem,
        device_id={axis: index},
        device_id_type=MESH,
    )


def await_bytes(ref, sem):
    pltpu.make_async_copy(ref, ref, sem).wait()


def greet(axis, count):
    me = lax.axis_index(axis)
    barrier = pltpu.get_barrier_semaphore()

    def body(i, carry):
        pl.semaphore_signal(
            barrier, inc=1, device_id={axis: lax.rem(me + i, count)}, device_id_type=MESH
        )
        return carry

    lax.fori_loop(1, count, body, 0)


def span_of(start, width):
    return pl.ds(pl.multiple_of(start, width), width)


def send_pairs(peers, send, got, send_sem, recv_sem, rows, cols):
    me = lax.axis_index("seq")
    mine = span_of(me * rows, rows)

    def body(i, carry):
        to = lax.rem(me + i, peers)
        block = send.at[span_of(to * rows, rows), cols]
        remote(block, got.at[mine, cols], send_sem, recv_sem, "seq", to).start()
        return carry

    lax.fori_loop(1, peers, body, 0)
    got[mine, cols] = send[mine, cols]


class Ring:
    def __init__(self, full, send_sem, recv_sem, base, start, width):
        self.full, self.send_sem, self.recv_sem = full, send_sem, recv_sem
        self.base, self.start, self.width = base, start, width
        self.quarter = full.shape[1] // 4
        half = full.shape[0] // 2
        self.top, self.low = pl.ds(0, half), pl.ds(half, half)
        self.m = lax.axis_index("mp")
        self.right, self.left = lax.rem(self.m + 1, 4), lax.rem(self.m + 3, 4)
        self.far = lax.rem(self.m + 2, 4)

    def move(self, block, rows, k, to):
        part = self.full.at[rows, span_of(block * self.quarter + self.start, self.width)]
        k = self.base + k
        return remote(part, part, self.send_sem.at[k], self.recv_sem.at[k], "mp", to)

    def begin(self):
        self.move(self.m, self.top, 0, self.right).start()
        self.move(self.m, self.low, 1, self.left).start()
        self.move(self.m, self.low, 2, self.right).start()
        self.move(self.m, self.top, 3, self.left).start()

    def forward(self):
        self.move(self.left, self.top, 0, self.right).wait_recv()
        self.move(self.left, self.top, 4, self.right).start()
        self.move(self.right, self.low, 1, self.left).wait_recv()
        self.move(self.right, self.low, 5, self.left).start()

    def near(self):
        self.move(self.left, self.low, 2, self.right).wait_recv()
        self.move(self.right, self.top, 3, self.left).wait_recv()

    def end(self):
        self.move(self.far, self.top, 4, self.right).wait_recv()
        self.move(self.far, self.low, 5, self.left).wait_recv()

    def sent(self):
        for k in range(6):
            self.move(self.m, self.top, k, self.right).wait_send()


def live(kpos_row, qpos):
    parts = [kpos_row[:, c : c + 128] <= qpos for c in range(0, kpos_row.shape[1], 128)]
    return jnp.concatenate(parts, axis=1)


def wide(column, width):
    return jnp.concatenate([column] * (width // 128), axis=1)


def lane_parts(x):
    total = x[:, :128]
    for c in range(128, x.shape[1], 128):
        total = total + x[:, c : c + 128]
    return total


def as_row(column):
    size = column.shape[0]
    eye = iota((size, size), 0) == iota((size, size), 1)
    return jnp.sum(jnp.where(eye, column, 0.0), axis=0, keepdims=True)


def as_column(row):
    size = row.shape[1]
    eye = iota((size, size), 0) == iota((size, size), 1)
    return jnp.sum(jnp.where(eye, row, 0.0), axis=1, keepdims=True)


class Place:
    def __init__(self):
        self.me = lax.axis_index("seq")
        self.c = lax.rem(self.me, 2)
        self.sa = 2 + 6 * self.c
        self.sb = 8 - 6 * self.c
        self.a = lax.rem(self.me // self.sa, 4)
        self.b = lax.rem(self.me // self.sb, 4)
        self.sibling = self.me + 1 - 2 * self.c

    def mine(self, i, j):
        return (
            lax.rem(self.a + i, 4) * self.sa + lax.rem(self.b + j, 4) * self.sb + self.c
        )

    def theirs(self, i, j):
        return (
            lax.rem(self.b + i, 4) * self.sb
            + lax.rem(self.a + j, 4) * self.sa
            + 1 - self.c
        )


def key_block(kv, block):
    rows = kv[block]
    keys = rows[:ROUTED_DEV, :HEAD_DIM]
    values = rows[:ROUTED_DEV, HEAD_DIM:]
    digits = rows[ROUTED_DEV:].astype(jnp.float32)
    return keys, values, digits[0:1] * 256.0 + digits[1:2]


CHUNK = 512
TILE = 256


def sublayer_kernel(
    idx_ref, dest_ref, count_ref, gain_ref, rw_ref,
    tok_hbm, cot_hbm, wq_hbm, wk_hbm, wv_hbm, wo_hbm,
    got, source_ref, factor_ref,
    tok, cot, wq, wkv, wo, pick, sendx, senddy, gotx, gotdy, sendm, gotm, sendf, gotf,
    fullx, fulldy, place, qpos, qkv, sums, q4, qt4, g4, gt4, acc, den, lden, delta,
    inv_col, router_col, dq, dqb, dkv,
    kv, to_sib, from_sib, to_b, from_b, to_a, from_a, far, near, relay, arrived, stats,
    load_sem, a2a_send, a2a_recv, x_send, x_recv, d_send, d_recv, kv_send, kv_recv,
    sends, sib_recv, b_recv, a_recv, rs_send, rs_recv, back_send, back_recv, st_send, st_recv,
):
    peers = lax.axis_size("seq")
    m = lax.axis_index("mp")
    at = Place()
    me = at.me
    bf16, f32 = jnp.bfloat16, jnp.float32
    slots = sendx.shape[0]
    tok_rows, quarter = tok.shape
    rows = ROUTED_DEV
    heads = wq.shape[1] // HEAD_DIM
    pair = slots // peers
    right, left, across = lax.rem(m + 1, 4), lax.rem(m + 3, 4), lax.rem(m + 2, 4)
    loads = [
        pltpu.make_async_copy(src, dst, load_sem.at[n])
        for n, (src, dst) in enumerate(
            [
                (tok_hbm, tok),
                (cot_hbm, cot),
                (wq_hbm, wq),
                (wk_hbm, wkv.at[:, pl.ds(0, HEAD_DIM)]),
                (wv_hbm, wkv.at[:, pl.ds(HEAD_DIM, HEAD_DIM)]),
                (wo_hbm, wo),
            ]
        )
    ]
    for load in loads:
        load.start()
    greet("seq", peers)
    greet("mp", 4)

    idx = idx_ref[...]
    dest = dest_ref[...]
    valid = iota((1, slots), 1) < count_ref[0]
    owner = jnp.where(valid, lax.shift_right_logical(dest, 8), peers)
    place_slot = jnp.bitwise_and(dest, rows - 1)
    rows_i = iota((slots, slots), 0)
    cols_i = iota((slots, slots), 1)
    owner_col = jnp.sum(jnp.where(rows_i == cols_i, owner, 0), axis=1, keepdims=True)
    earlier = jnp.logical_and(owner_col == owner, rows_i < cols_i)
    rank = jnp.sum(jnp.where(earlier, 1, 0), axis=0, keepdims=True)
    buffer_place = jnp.where(valid, owner * pair + rank, slots)
    hit = rows_i == buffer_place
    source = jnp.sum(jnp.where(hit, idx - tok_rows, 0), axis=1, keepdims=True) + tok_rows
    pick[...] = onehot(iota((slots, tok_rows), 1) == source)

    lanes = iota((128, slots), 0)

    def spread(hits, entries, lane, shift):
        held = jnp.where(hits, entries, 0.0).astype(bf16)
        return dot(held, onehot(lanes == lane + shift), NT)

    owner_hit = iota((peers, slots), 0) == owner
    rank_lane = jnp.where(valid, rank, 128)
    position = me * tok_rows + idx
    digits = [
        place_slot + 1,
        lax.shift_right_logical(position, 8),
        jnp.bitwise_and(position, 255),
    ]
    meta = sum(
        spread(owner_hit, d.astype(f32), rank_lane, n * pair) for n, d in enumerate(digits)
    )
    sendm[...] = jnp.broadcast_to(meta[:, None, :], sendm.shape)

    pl.semaphore_wait(pltpu.get_barrier_semaphore(), peers - 1 + 3)

    def send_meta(src, dst, k):
        def body(i, carry):
            to = lax.rem(me + i, peers)
            remote(src.at[to], dst.at[me], a2a_send.at[k], a2a_recv.at[k], "seq", to).start()
            return carry

        lax.fori_loop(1, peers, body, 0)
        dst[me] = src[me]

    send_meta(sendm, gotm, 3)

    def pack(held, send, start, width):
        def body(n, carry):
            cols = span_of(start + n * TILE, TILE)
            send[:, cols] = dot(pick[...], held[:, cols]).astype(bf16)
            return carry

        lax.fori_loop(0, width // TILE, body, 0)
        return pl.ds(start, width)

    loads[0].wait()
    for n in range(2):
        cols = pack(tok, sendx, n * CHUNK, CHUNK)
        send_pairs(peers, sendx, gotx, a2a_send.at[n], a2a_recv.at[n], pair, cols)
    loads[1].wait()
    cols = pack(cot, senddy, 0, quarter)
    send_pairs(peers, senddy, gotdy, a2a_send.at[2], a2a_recv.at[2], pair, cols)
    source_row = jnp.sum(jnp.where(rows_i == cols_i, source, 0), axis=0, keepdims=True)
    source_ref[...] = jnp.broadcast_to(source_row, source_ref.shape)

    others = pl.ds(0, peers - 1)
    column = iota((128, slots), 0)
    within = jnp.bitwise_and(iota((128, slots), 1), pair - 1)
    sender = iota((peers, slots), 0) == iota((peers, slots), 1) // pair

    def flat(got_rows, shift):
        out = dot(got_rows, onehot(column == within + shift))
        return jnp.sum(jnp.where(sender, out, 0.0), axis=0, keepdims=True)

    await_bytes(gotm.at[others], a2a_recv.at[3])
    got_meta = gotm[:, 0, :].astype(bf16)
    slot_in = flat(got_meta, 0)
    pos_in = flat(got_meta, pair) * 256.0 + flat(got_meta, 2 * pair)
    here = iota((rows, slots), 0).astype(f32) + 1.0 == slot_in
    place[...] = onehot(here)
    row_pos = jnp.sum(jnp.where(here, pos_in, 0.0), axis=1, keepdims=True)
    qpos[...] = jnp.broadcast_to(row_pos, qpos.shape)
    kpos = as_row(row_pos).astype(jnp.int32)
    pos_digits = jnp.where(
        iota((16, rows), 0) == 0,
        lax.shift_right_logical(kpos, 8),
        jnp.bitwise_and(kpos, 255),
    )
    kv[me, rows:, :] = pos_digits.astype(f32).astype(bf16)

    def compact(got_rows, full, start, width):
        def body(n, carry):
            to = span_of(m * quarter + start + n * TILE, TILE)
            part = got_rows[:, span_of(start + n * TILE, TILE)]
            full[:, to] = dot(place[...], part).astype(bf16)
            return carry

        lax.fori_loop(0, width // TILE, body, 0)

    def arrived_span(ref, width, start=0):
        return ref.at[pl.ds(0, slots - pair), pl.ds(start, width)]

    qkv[...] = jnp.zeros_like(qkv)
    sums[...] = jnp.zeros_like(sums)

    def project(block, start, width):
        f = span_of(block * quarter + start, width)
        x = fullx[:, f].astype(f32)
        sums[0] += lane_parts(x * x)
        sums[1] += lane_parts(x * rw_ref[:, f])
        scaled = (x * gain_ref[:, f]).astype(bf16)
        split = heads * HEAD_DIM
        qkv[:, :split] += dot(scaled, wq[f, :])
        qkv[:, split:] += dot(scaled, wkv[f, :])

    rings = [Ring(fullx, x_send, x_recv, 6 * n, n * CHUNK, CHUNK) for n in range(2)]
    for n in range(2):
        await_bytes(arrived_span(gotx, CHUNK, n * CHUNK), a2a_recv.at[n])
        compact(gotx, fullx, n * CHUNK, CHUNK)
        rings[n].begin()
    for n in range(2, 5):
        loads[n].wait()
    project(m, 0, quarter)
    rings[0].forward()
    rings[0].near()
    project(left, 0, CHUNK)
    project(right, 0, CHUNK)
    rings[1].forward()
    rings[0].end()
    project(across, 0, CHUNK)
    rings[1].near()
    project(left, CHUNK, CHUNK)
    project(right, CHUNK, CHUNK)
    await_bytes(arrived_span(gotdy, quarter), a2a_recv.at[2])
    compact(gotdy, fulldy, 0, quarter)
    rings[1].end()
    project(across, CHUNK, CHUNK)

    mean = jnp.sum(sums[0], axis=1, keepdims=True) * (1.0 / (4 * quarter))
    inv = lax.rsqrt(mean + norm_eps)
    inv_col[...] = jnp.broadcast_to(inv, inv_col.shape)
    router_col[...] = jnp.broadcast_to(
        jnp.sum(sums[1], axis=1, keepdims=True), router_col.shape
    )
    split = heads * HEAD_DIM
    kv[me, :rows, :] = (qkv[:, split:] * inv).astype(bf16)

    half = rows // 2
    whole, top, low = pl.ds(0, rows + 16), pl.ds(0, half), pl.ds(half, half + 16)

    def send(block, to, part=whole):
        span = kv.at[block, part]
        remote(span, span, kv_send, kv_recv.at[block], "seq", to).start()

    def receive(block):
        await_bytes(kv.at[block], kv_recv.at[block])

    send(me, at.mine(1, 0))
    send(me, at.mine(3, 0))
    send(me, at.sibling)
    send(me, at.mine(0, 1))
    send(me, at.mine(0, 3))
    dy_ring = Ring(fulldy, d_send, d_recv, 0, 0, quarter)
    dy_ring.begin()
    for h in range(heads):
        part = (qkv[:, h * HEAD_DIM : (h + 1) * HEAD_DIM] * inv).astype(bf16)
        q4[h * rows : (h + 1) * rows, :] = part
    acc[...] = jnp.zeros_like(acc)
    den[...] = jnp.zeros_like(den)

    def masks(key_pos):
        mask = live(key_pos, qpos[...])
        return jnp.concatenate([mask] * (CHUNK // rows), axis=0)

    def process(block):
        keys, values, key_pos = key_block(kv, block)
        mask = masks(key_pos)
        for start in range(0, heads * rows, CHUNK):
            r = slice(start, start + CHUNK)
            t = jnp.tanh(dot(q4[r, :], keys, NT) * (SCALE / score_cap))
            w = jnp.where(mask, jnp.exp2(t * (score_cap * LOG2E)), 0.0)
            den[r] += lane_parts(w)
            acc[r] += dot(w.astype(bf16), values)

    def order(t):
        a = (t + 12) // 16
        b = (t + 4) // 16
        u = (1 - a) * t + (a - b) * lax.div(t - 4, 2) + b * (t - 12)
        i = u + (u // 2) * (1 - 2 * lax.rem(u, 2))
        j = (a - b) * (1 + 2 * lax.rem(t, 2)) + 2 * b
        return i, j

    def take(t):
        block = at.mine(*order(t))
        receive(block)

        @pl.when(t == 1)
        def _():
            send(block, at.mine(3, 0), low)

        @pl.when(t == 2)
        def _():
            send(block, at.mine(1, 0), top)

        @pl.when(t < 4)
        def _():
            send(block, at.mine(0, 1))
            send(block, at.mine(0, 3))

        @pl.when(jnp.logical_and(t >= 4, t < 12))
        def _():
            @pl.when(lax.rem(t, 2) == 0)
            def _():
                send(block, at.mine(0, 3), low)

            @pl.when(lax.rem(t, 2) == 1)
            def _():
                send(block, at.mine(0, 1), top)

        send(block, at.sibling)
        return block

    def pair_of(t):
        a, b = at.theirs(*order(t)), at.theirs(*order(t + 1))
        receive(a)
        receive(b)
        return a, b

    process(me)
    for h in range(heads):
        r = slice(h * rows, (h + 1) * rows)
        qt4[:, r] = q4[r, :].T

    def step(s, carry):
        t = 1 + 2 * s
        a = take(t)
        b = take(t + 1)

        @pl.when(s == 2)
        def _():
            dy_ring.forward()

        process(a)
        process(b)
        c, d = pair_of(t - 1)
        process(c)
        process(d)
        return carry

    lax.fori_loop(0, 7, step, 0)
    a = take(15)
    process(a)
    c, d = pair_of(14)
    process(c)
    process(d)

    loads[5].wait()
    dy_ring.near()
    dy_ring.end()
    router = router_col[...]
    dots = jnp.zeros((rows, 1), f32)
    for n in range(split // TILE):
        pulled = dot(fulldy[...], wo[n * TILE : (n + 1) * TILE, :], NT)
        for g in range(TILE // HEAD_DIM):
            h = n * (TILE // HEAD_DIM) + g
            r = slice(h * rows, (h + 1) * rows)
            mine = pulled[:, g * HEAD_DIM : (g + 1) * HEAD_DIM]
            total = jnp.sum(den[r], axis=1, keepdims=True)
            att = (acc[r] / total).astype(bf16).astype(f32)
            lden[r] = jnp.broadcast_to(jnp.log2(total), (rows, 128))
            grad = (mine * router).astype(bf16)
            g4[r, :] = grad
            gt4[:, r] = grad.T
            row_delta = jnp.sum(grad.astype(f32) * att, axis=1, keepdims=True)
            delta[r] = jnp.broadcast_to(row_delta, (rows, 128))
            dots = dots + jnp.sum(mine * att, axis=1, keepdims=True)

    def send_stats(k):
        def body(i, carry):
            to = lax.rem(m + i, 4)
            here = stats.at[k, m]
            remote(here, here, st_send.at[k], st_recv.at[k], "mp", to).start()
            return carry

        lax.fori_loop(1, 4, body, 0)

    def take_stats(k):
        await_bytes(stats.at[k, pl.ds(0, 3)], st_recv.at[k])
        return as_column((stats[k, 0] + stats[k, 1] + stats[k, 2] + stats[k, 3])[0:1])

    stats[0, m] = jnp.broadcast_to(as_row(dots), stats.shape[2:])
    send_stats(0)

    dq[...] = jnp.zeros_like(dq)

    def terms(block):
        keys, values, key_pos = key_block(kv, block)
        width = keys.shape[0]
        mask = masks(key_pos)
        probs, grads = [], []
        for start in range(0, heads * rows, CHUNK):
            r = slice(start, start + CHUNK)
            t = jnp.tanh(dot(q4[r, :], keys, NT) * (SCALE / score_cap))
            p = jnp.exp2(t * (score_cap * LOG2E) - wide(lden[r], width))
            p = jnp.where(mask, p, 0.0)
            dp = dot(g4[r, :], values, NT)
            probs.append(p.astype(bf16))
            grads.append((p * (dp - wide(delta[r], width)) * (1.0 - t * t)).astype(bf16))
        probs, grads = jnp.concatenate(probs, axis=0), jnp.concatenate(grads, axis=0)
        dq[...] += dot(grads, keys)
        dk = dot(qt4[...], grads) * SCALE
        return jnp.concatenate([dk, dot(gt4[...], probs)], axis=0)

    def pass_on(k, late, i, j):
        await_bytes(from_sib.at[k], sib_recv.at[k])

        @pl.when(late == 0)
        def _():
            summed = to_b[k].astype(f32) + from_sib[k].astype(f32)
            to_b[k] = summed.astype(bf16)
            slot = (4 - j) * 4 + i
            remote(
                to_b.at[k], from_b.at[slot], sends.at[1], b_recv.at[slot], "seq",
                at.mine(0, j),
            ).start()

        @pl.when(late == 1)
        def _():
            total = to_b[k].astype(f32) + from_sib[k].astype(f32)
            for n in range(1, 4):
                await_bytes(from_b.at[n * 4 + i], b_recv.at[n * 4 + i])
                total = total + from_b[n * 4 + i].astype(f32)

            @pl.when(k < 15)
            def _():
                to_a[i] = total.astype(bf16)
                slot = 4 - i
                remote(
                    to_a.at[i], from_a.at[slot], sends.at[2], a_recv.at[slot], "seq",
                    at.mine(i, 0),
                ).start()

            @pl.when(k == 15)
            def _():
                final = total
                for n in range(1, 4):
                    await_bytes(from_a.at[n], a_recv.at[n])
                    final = final + from_a[n].astype(f32)
                dkv[...] = final.T.astype(bf16)

    def back_step(s, carry):
        late = s // 6
        places = []
        for n in range(2):
            k = 2 * s + n
            j = (1 + k // 4) * (1 - late)
            i = lax.rem(k + late, 4)
            places.append((k, late, i, j))
        for k, _, i, j in places:
            to_sib[k] = terms(at.theirs(i, j)).astype(bf16)
            remote(
                to_sib.at[k], from_sib.at[k], sends.at[0], sib_recv.at[k], "seq", at.sibling
            ).start()
        for k, _, i, j in places:
            to_b[k] = terms(at.mine(i, j)).astype(bf16)
        for where in places:
            pass_on(*where)
        return carry

    lax.fori_loop(0, 8, back_step, 0)
    for h in range(heads):
        r = slice(h * rows, (h + 1) * rows)
        dqb[:, h * HEAD_DIM : (h + 1) * HEAD_DIM] = (dq[r] * SCALE).astype(bf16)

    chunks = quarter // TILE

    def contribution(block, n):
        f = span_of(block * quarter + n * TILE, TILE)
        total = dot(dqb[...], wq[f, :], NT) + dot(dkv[...], wkv[f, :], NT)
        return total * gain_ref[:, f]

    def rs(src, dst, n, k, to):
        k = 6 * n + k
        return remote(src, dst, rs_send.at[k], rs_recv.at[k], "mp", to)

    top, low = pl.ds(0, half), pl.ds(half, half)
    copies = []

    def hand_over(n):
        cols = pl.ds(n * TILE, TILE)
        copies[n][0].wait_recv()
        near[0, top, cols] = (
            near[0, top, cols].astype(f32) + relay[0, :, cols].astype(f32)
        ).astype(bf16)
        copies[n].append(rs(near.at[0, top, cols], arrived.at[0, top, cols], n, 4, right))
        copies[n][4].start()
        copies[n][1].wait_recv()
        near[1, low, cols] = (
            near[1, low, cols].astype(f32) + relay[1, :, cols].astype(f32)
        ).astype(bf16)
        copies[n].append(rs(near.at[1, low, cols], arrived.at[1, low, cols], n, 5, left))
        copies[n][5].start()

    for n in range(chunks):
        cols = pl.ds(n * TILE, TILE)
        far[:, cols] = contribution(across, n).astype(bf16)
        first = rs(far.at[top, cols], relay.at[0, :, cols], n, 0, right)
        second = rs(far.at[low, cols], relay.at[1, :, cols], n, 1, left)
        first.start()
        second.start()
        near[0, :, cols] = contribution(right, n).astype(bf16)
        third = rs(near.at[0, low, cols], arrived.at[0, low, cols], n, 2, right)
        third.start()
        near[1, :, cols] = contribution(left, n).astype(bf16)
        fourth = rs(near.at[1, top, cols], arrived.at[1, top, cols], n, 3, left)
        fourth.start()
        copies.append([first, second, third, fourth])
        if n > 0:
            hand_over(n - 1)
    hand_over(chunks - 1)

    router_grad = take_stats(0)
    await_bytes(arrived_span(sendx, CHUNK), a2a_send.at[0])
    await_bytes(arrived_span(sendx, CHUNK, CHUNK), a2a_send.at[1])
    back = sendx
    inv = inv_col[:, 0:1]
    stat = jnp.zeros((rows, 128), f32)
    for n in range(chunks):
        cols = pl.ds(n * TILE, TILE)
        f = span_of(m * quarter + n * TILE, TILE)
        own = contribution(m, n)
        for c in copies[n][2:]:
            c.wait_recv()
        own = own + arrived[0, :, cols].astype(f32) + arrived[1, :, cols].astype(f32)
        stat = stat + lane_parts(fullx[:, f].astype(f32) * own)
        branch = (inv * own + rw_ref[:, f] * router_grad).astype(bf16)
        back[:, cols] = dot(place[...], branch, TN).astype(bf16)
        send_pairs(peers, back, got, back_send.at[n], back_recv.at[n], pair, cols)

    stats[1, m] = jnp.broadcast_to(
        as_row(jnp.sum(stat, axis=1, keepdims=True)), stats.shape[2:]
    )
    send_stats(1)
    factor = inv * inv * inv * take_stats(1) * (1.0 / (4 * quarter))
    rest = jnp.sum(jnp.where(place[...].astype(f32) > 0.5, factor, 0.0), axis=0, keepdims=True)
    slot_lane = jnp.bitwise_and(iota((1, slots), 1), pair - 1)
    meta = jnp.zeros((peers, 128), f32)
    for n in range(3):
        piece = rest.astype(bf16).astype(f32)
        rest = rest - piece
        meta = meta + spread(sender, piece, slot_lane, n * pair)
    sendf[...] = jnp.broadcast_to(meta[:, None, :], sendf.shape)
    send_meta(sendf, gotf, 4)
    await_bytes(gotf.at[others], a2a_recv.at[4])
    got_meta = gotf[:, 0, :].astype(bf16)
    factor_row = flat(got_meta, 0) + flat(got_meta, pair) + flat(got_meta, 2 * pair)
    factor_ref[...] = jnp.broadcast_to(factor_row, factor_ref.shape)

    for n in range(chunks):
        await_bytes(arrived_span(got, TILE, n * TILE), back_recv.at[n])
        await_bytes(arrived_span(back, TILE, n * TILE), back_send.at[n])
    await_bytes(arrived_span(senddy, quarter), a2a_send.at[2])
    await_bytes(sendm.at[others], a2a_send.at[3])
    await_bytes(sendf.at[others], a2a_send.at[4])
    for ring in rings:
        ring.sent()
    dy_ring.sent()
    for group in copies:
        for c in group:
            c.wait_send()
    for k in range(2):
        await_bytes(stats.at[k, pl.ds(0, 3)], st_send.at[k])
    await_bytes(to_sib, sends.at[0])
    await_bytes(to_b.at[pl.ds(0, 12)], sends.at[1])
    await_bytes(to_a.at[pl.ds(0, 3)], sends.at[2])
    await_bytes(kv.at[others], kv_send)


def sublayer(tokens, cotangent, gain, router_weight, w_query, w_key, w_value, w_out, idx, count, dest):
    peers = lax.axis_size("seq")
    tok_rows, quarter = tokens.shape
    width = 4 * quarter
    split = w_query.shape[1]
    heads = split // HEAD_DIM
    rows = ROUTED_DEV
    slots = 2 * rows
    bf16, f32 = jnp.bfloat16, jnp.float32
    vmem = pl.BlockSpec(memory_space=pltpu.VMEM)
    hbm = pl.BlockSpec(memory_space=pl.ANY)
    shape = jax.ShapeDtypeStruct
    dma = pltpu.SemaphoreType.DMA
    ram = pltpu.VMEM
    stacked = heads * rows

    def held(n):
        return ram((n, 2 * HEAD_DIM, rows), bf16)

    return pl.pallas_call(
        sublayer_kernel,
        in_specs=[vmem, vmem, pl.BlockSpec(memory_space=pltpu.SMEM), vmem, vmem] + [hbm] * 6,
        out_specs=[vmem] * 3,
        out_shape=[
            shape((slots, quarter), bf16),
            shape((8, slots), jnp.int32),
            shape((8, slots), f32),
        ],
        scratch_shapes=[
            ram((tok_rows, quarter), bf16), ram((tok_rows, quarter), bf16),
            ram((width, split), bf16), ram((width, 2 * HEAD_DIM), bf16), ram((split, width), bf16),
            ram((slots, tok_rows), bf16),
            ram((slots, quarter), bf16), ram((slots, quarter), bf16),
            ram((slots, quarter), bf16), ram((slots, quarter), bf16),
            ram((peers, 8, 128), f32), ram((peers, 8, 128), f32),
            ram((peers, 8, 128), f32), ram((peers, 8, 128), f32),
            ram((rows, width), bf16), ram((rows, width), bf16),
            ram((rows, slots), bf16), ram((rows, 128), f32),
            ram((rows, split + 2 * HEAD_DIM), f32), ram((2, rows, 128), f32),
            ram((stacked, HEAD_DIM), bf16), ram((HEAD_DIM, stacked), bf16),
            ram((stacked, HEAD_DIM), bf16), ram((HEAD_DIM, stacked), bf16),
            ram((stacked, HEAD_DIM), f32), ram((stacked, 128), f32),
            ram((stacked, 128), f32), ram((stacked, 128), f32),
            ram((rows, 128), f32), ram((rows, 128), f32),
            ram((stacked, HEAD_DIM), f32), ram((rows, split), bf16),
            ram((rows, 2 * HEAD_DIM), bf16),
            ram((peers, rows + 16, 2 * HEAD_DIM), bf16),
            held(16), held(16), held(16), held(16), held(4), held(4),
            ram((rows, quarter), bf16), ram((2, rows, quarter), bf16),
            ram((2, rows // 2, quarter), bf16), ram((2, rows, quarter), bf16),
            ram((2, 4, 8, rows), f32),
            dma((6,)), dma((5,)), dma((5,)), dma((12,)), dma((12,)), dma((6,)), dma((6,)),
            dma, dma((peers,)),
            dma((3,)), dma((16,)), dma((16,)), dma((4,)), dma((24,)), dma((24,)),
            dma((4,)), dma((4,)), dma((2,)), dma((2,)),
        ],
        compiler_params=pltpu.CompilerParams(
            collective_id=0, has_side_effects=True, vmem_limit_bytes=VMEM_LIMIT
        ),
        name="sublayer",
    )(
        idx, dest, count, gain, router_weight,
        tokens, cotangent, w_query, w_key, w_value, w_out,
    )


def final_kernel(tok_ref, cot_ref, got_ref, source_ref, factor_ref, out_ref):
    block, slots = tok_ref.shape[0], got_ref.shape[0]
    first = pl.program_id(0) * block
    put = iota((block, slots), 0) + first == source_ref[0:1, :]
    factor = jnp.sum(jnp.where(put, factor_ref[0:1, :], 0.0), axis=1, keepdims=True)
    moved = dot(onehot(put), got_ref[...])
    out = cot_ref[...].astype(jnp.float32) + moved
    out_ref[...] = (out - tok_ref[...].astype(jnp.float32) * factor).astype(jnp.bfloat16)


def finish(tokens, cotangent, got, source, factor):
    tok_rows, quarter = tokens.shape
    block = pl.BlockSpec((256, quarter), lambda i: (i, 0))

    def whole(array):
        return pl.BlockSpec(array.shape, lambda i: (0, 0))

    return pl.pallas_call(
        final_kernel,
        grid=(tok_rows // 256,),
        in_specs=[block, block, whole(got), whole(source), whole(factor)],
        out_specs=block,
        out_shape=jax.ShapeDtypeStruct(tokens.shape, jnp.bfloat16),
        compiler_params=pltpu.CompilerParams(
            dimension_semantics=("arbitrary",), vmem_limit_bytes=32 * MIB
        ),
        name="add_branch",
    )(tokens, cotangent, got, source, factor)


def on_device(
    tokens,
    cotangent,
    norm_gain,
    router_weight,
    w_query,
    w_key,
    w_value,
    w_out,
    routed_index,
    routed_count,
    routed_dest,
):
    got, source, factor = sublayer(
        tokens,
        cotangent,
        norm_gain[None, :],
        router_weight[None, :],
        w_query,
        w_key,
        w_value,
        w_out,
        routed_index,
        routed_count,
        routed_dest,
    )
    return finish(tokens, cotangent, got, source, factor)


def solution(mesh):
    in_specs = (
        P("seq", "mp"),
        P("seq", "mp"),
        P(),
        P(),
        P(None, "mp"),
        P(None, "mp"),
        P(None, "mp"),
        P("mp", None),
        P("seq", None),
        P("seq"),
        P("seq", None),
    )
    out_specs = P("seq", "mp")
    return jax.shard_map(
        on_device, mesh=mesh, in_specs=in_specs, out_specs=out_specs, check_vma=False
    )
```

```python
import jax
import jax.numpy as jnp
from jax import lax
from jax.experimental import pallas as pl
from jax.experimental.pallas import tpu as pltpu
from jax.sharding import PartitionSpec as P

HEAD_DIM = 128
ROUTED_DEV = 256
MESH = pl.DeviceIdType.MESH
NT = (((1,), (1,)), ((), ()))
NN = (((1,), (0,)), ((), ()))
TN = (((0,), (0,)), ((), ()))
MIB = 1024 * 1024
VMEM_LIMIT = 60 * MIB
norm_eps = 1e-05
score_cap = 5.0
LOG2E = 1.4426950408889634
SCALE = HEAD_DIM ** (-0.5)


def dot(a, b, dims=NN):
    return lax.dot_general(a, b, dims, preferred_element_type=jnp.float32)


def iota(shape, dim):
    return lax.broadcasted_iota(jnp.int32, shape, dim)


def onehot(mask):
    return jnp.where(mask, 1.0, 0.0).astype(jnp.bfloat16)


def remote(src, dst, send_sem, recv_sem, axis, index):
    return pltpu.make_async_remote_copy(
        src_ref=src,
        dst_ref=dst,
        send_sem=send_sem,
        recv_sem=recv_sem,
        device_id={axis: index},
        device_id_type=MESH,
    )


def await_bytes(ref, sem):
    pltpu.make_async_copy(ref, ref, sem).wait()


def greet(axis, count):
    me = lax.axis_index(axis)
    barrier = pltpu.get_barrier_semaphore()

    def body(i, carry):
        pl.semaphore_signal(
            barrier, inc=1, device_id={axis: lax.rem(me + i, count)}, device_id_type=MESH
        )
        return carry

    lax.fori_loop(1, count, body, 0)


def span_of(start, width):
    return pl.ds(pl.multiple_of(start, width), width)


def send_pairs(peers, send, got, send_sem, recv_sem, rows, cols):
    me = lax.axis_index("seq")
    mine = span_of(me * rows, rows)

    def body(i, carry):
        to = lax.rem(me + i, peers)
        block = send.at[span_of(to * rows, rows), cols]
        remote(block, got.at[mine, cols], send_sem, recv_sem, "seq", to).start()
        return carry

    lax.fori_loop(1, peers, body, 0)
    got[mine, cols] = send[mine, cols]


class Ring:
    def __init__(self, full, send_sem, recv_sem, base, start, width):
        self.full, self.send_sem, self.recv_sem = full, send_sem, recv_sem
        self.base, self.start, self.width = base, start, width
        self.quarter = full.shape[1] // 4
        half = full.shape[0] // 2
        self.top, self.low = pl.ds(0, half), pl.ds(half, half)
        self.m = lax.axis_index("mp")
        self.right, self.left = lax.rem(self.m + 1, 4), lax.rem(self.m + 3, 4)
        self.far = lax.rem(self.m + 2, 4)

    def move(self, block, rows, k, to):
        part = self.full.at[rows, span_of(block * self.quarter + self.start, self.width)]
        k = self.base + k
        return remote(part, part, self.send_sem.at[k], self.recv_sem.at[k], "mp", to)

    def begin(self):
        self.move(self.m, self.top, 0, self.right).start()
        self.move(self.m, self.low, 1, self.left).start()
        self.move(self.m, self.low, 2, self.right).start()
        self.move(self.m, self.top, 3, self.left).start()

    def forward(self):
        self.move(self.left, self.top, 0, self.right).wait_recv()
        self.move(self.left, self.top, 4, self.right).start()
        self.move(self.right, self.low, 1, self.left).wait_recv()
        self.move(self.right, self.low, 5, self.left).start()

    def near(self):
        self.move(self.left, self.low, 2, self.right).wait_recv()
        self.move(self.right, self.top, 3, self.left).wait_recv()

    def end(self):
        self.move(self.far, self.top, 4, self.right).wait_recv()
        self.move(self.far, self.low, 5, self.left).wait_recv()

    def sent(self):
        for k in range(6):
            self.move(self.m, self.top, k, self.right).wait_send()


def live(kpos_row, qpos):
    parts = [kpos_row[:, c : c + 128] <= qpos for c in range(0, kpos_row.shape[1], 128)]
    return jnp.concatenate(parts, axis=1)


def wide(column, width):
    return jnp.concatenate([column] * (width // 128), axis=1)


def lane_parts(x):
    total = x[:, :128]
    for c in range(128, x.shape[1], 128):
        total = total + x[:, c : c + 128]
    return total


def as_row(column):
    size = column.shape[0]
    eye = iota((size, size), 0) == iota((size, size), 1)
    return jnp.sum(jnp.where(eye, column, 0.0), axis=0, keepdims=True)


def as_column(row):
    size = row.shape[1]
    eye = iota((size, size), 0) == iota((size, size), 1)
    return jnp.sum(jnp.where(eye, row, 0.0), axis=1, keepdims=True)


class Place:
    def __init__(self):
        self.me = lax.axis_index("seq")
        self.c = lax.rem(self.me, 2)
        self.sa = 2 + 6 * self.c
        self.sb = 8 - 6 * self.c
        self.a = lax.rem(self.me // self.sa, 4)
        self.b = lax.rem(self.me // self.sb, 4)
        self.sibling = self.me + 1 - 2 * self.c
        self.on_a = [lax.rem(self.a + i, 4) * self.sa for i in range(4)]
        self.on_b = [lax.rem(self.b + j, 4) * self.sb for j in range(4)]

    def first(self, i):
        return self.on_a[i] if isinstance(i, int) else lax.rem(self.a + i, 4) * self.sa

    def second(self, j):
        return self.on_b[j] if isinstance(j, int) else lax.rem(self.b + j, 4) * self.sb

    def mine(self, i, j):
        return self.first(i) + self.second(j) + self.c

    def theirs(self, i, j):
        return self.second(i) + self.first(j) + 1 - self.c


def key_block(kv, block):
    rows = kv[block]
    keys = rows[:ROUTED_DEV, :HEAD_DIM]
    values = rows[:ROUTED_DEV, HEAD_DIM:]
    digits = rows[ROUTED_DEV:].astype(jnp.float32)
    return keys, values, digits[0:1] * 256.0 + digits[1:2]


CHUNK = 512
TILE = 256


def sublayer_kernel(
    idx_ref, dest_ref, count_ref, gain_ref, rw_ref,
    tok_hbm, cot_hbm, wq_hbm, wk_hbm, wv_hbm, wo_hbm,
    got, source_ref,
    tok, cot, wq, wkv, wo, pick, sendx, senddy, gotx, gotdy, sendm, gotm,
    fullx, fulldy, place, qpos, qkv, sums, q4, qt4, g4, gt4, acc, den, lden, delta,
    inv_col, router_col, dq, dqb, dkv,
    kv, to_sib, from_sib, to_b, from_b, to_a, from_a, far, near, relay, arrived, stats,
    load_sem, a2a_send, a2a_recv, x_send, x_recv, d_send, d_recv, kv_send, kv_recv,
    sends, sib_recv, b_recv, a_recv, rs_send, rs_recv, back_send, back_recv, st_send, st_recv,
):
    peers = lax.axis_size("seq")
    m = lax.axis_index("mp")
    at = Place()
    me = at.me
    bf16, f32 = jnp.bfloat16, jnp.float32
    slots = sendx.shape[0]
    tok_rows, quarter = tok.shape
    rows = ROUTED_DEV
    heads = wq.shape[1] // HEAD_DIM
    pair = slots // peers
    parts = quarter // TILE
    right, left, across = lax.rem(m + 1, 4), lax.rem(m + 3, 4), lax.rem(m + 2, 4)
    loads = [
        pltpu.make_async_copy(src, dst, load_sem.at[n])
        for n, (src, dst) in enumerate(
            [
                (tok_hbm, tok),
                (cot_hbm, cot),
                (wq_hbm, wq),
                (wk_hbm, wkv.at[:, pl.ds(0, HEAD_DIM)]),
                (wv_hbm, wkv.at[:, pl.ds(HEAD_DIM, HEAD_DIM)]),
                (wo_hbm, wo),
            ]
        )
    ]
    for load in loads:
        load.start()
    greet("seq", peers)
    greet("mp", 4)

    idx = idx_ref[...]
    dest = dest_ref[...]
    valid = iota((1, slots), 1) < count_ref[0]
    owner = jnp.where(valid, lax.shift_right_logical(dest, 8), peers)
    place_slot = jnp.bitwise_and(dest, rows - 1)
    rows_i = iota((slots, slots), 0)
    cols_i = iota((slots, slots), 1)
    owner_col = jnp.sum(jnp.where(rows_i == cols_i, owner, 0), axis=1, keepdims=True)
    earlier = jnp.logical_and(owner_col == owner, rows_i < cols_i)
    rank = jnp.sum(jnp.where(earlier, 1, 0), axis=0, keepdims=True)
    buffer_place = jnp.where(valid, owner * pair + rank, slots)
    hit = rows_i == buffer_place
    source = jnp.sum(jnp.where(hit, idx - tok_rows, 0), axis=1, keepdims=True) + tok_rows
    pick[...] = onehot(iota((slots, tok_rows), 1) == source)

    lanes = iota((128, slots), 0)

    def spread(hits, entries, lane, shift):
        held = jnp.where(hits, entries, 0.0).astype(bf16)
        return dot(held, onehot(lanes == lane + shift), NT)

    owner_hit = iota((peers, slots), 0) == owner
    rank_lane = jnp.where(valid, rank, 128)
    position = me * tok_rows + idx
    digits = [
        place_slot + 1,
        lax.shift_right_logical(position, 8),
        jnp.bitwise_and(position, 255),
    ]
    meta = sum(
        spread(owner_hit, d.astype(f32), rank_lane, n * pair) for n, d in enumerate(digits)
    )
    sendm[...] = jnp.broadcast_to(meta[:, None, :], sendm.shape)

    pl.semaphore_wait(pltpu.get_barrier_semaphore(), peers - 1 + 3)

    def send_meta(src, dst, k):
        def body(i, carry):
            to = lax.rem(me + i, peers)
            remote(src.at[to], dst.at[me], a2a_send.at[k], a2a_recv.at[k], "seq", to).start()
            return carry

        lax.fori_loop(1, peers, body, 0)
        dst[me] = src[me]

    send_meta(sendm, gotm, 5)

    def pack(held, send, start, width):
        def body(n, carry):
            cols = span_of(start + n * TILE, TILE)
            send[:, cols] = dot(pick[...], held[:, cols]).astype(bf16)
            return carry

        lax.fori_loop(0, width // TILE, body, 0)
        return pl.ds(start, width)

    loads[0].wait()
    for n in range(parts):
        cols = pack(tok, sendx, n * TILE, TILE)
        send_pairs(peers, sendx, gotx, a2a_send.at[n], a2a_recv.at[n], pair, cols)
    loads[1].wait()
    pack(cot, senddy, 0, quarter)
    source_row = jnp.sum(jnp.where(rows_i == cols_i, source, 0), axis=0, keepdims=True)
    source_ref[...] = jnp.broadcast_to(source_row, source_ref.shape)

    others = pl.ds(0, peers - 1)
    column = iota((128, slots), 0)
    within = jnp.bitwise_and(iota((128, slots), 1), pair - 1)
    sender = iota((peers, slots), 0) == iota((peers, slots), 1) // pair

    def flat(got_rows, shift):
        out = dot(got_rows, onehot(column == within + shift))
        return jnp.sum(jnp.where(sender, out, 0.0), axis=0, keepdims=True)

    await_bytes(gotm.at[others], a2a_recv.at[5])
    got_meta = gotm[:, 0, :].astype(bf16)
    slot_in = flat(got_meta, 0)
    pos_in = flat(got_meta, pair) * 256.0 + flat(got_meta, 2 * pair)
    here = iota((rows, slots), 0).astype(f32) + 1.0 == slot_in
    place[...] = onehot(here)
    row_pos = jnp.sum(jnp.where(here, pos_in, 0.0), axis=1, keepdims=True)
    qpos[...] = jnp.broadcast_to(row_pos, qpos.shape)
    kpos = as_row(row_pos).astype(jnp.int32)
    pos_digits = jnp.where(
        iota((16, rows), 0) == 0,
        lax.shift_right_logical(kpos, 8),
        jnp.bitwise_and(kpos, 255),
    )
    kv[me, rows:, :] = pos_digits.astype(f32).astype(bf16)

    def compact(got_rows, full, start, width):
        def body(n, carry):
            to = span_of(m * quarter + start + n * TILE, TILE)
            part = got_rows[:, span_of(start + n * TILE, TILE)]
            full[:, to] = dot(place[...], part).astype(bf16)
            return carry

        lax.fori_loop(0, width // TILE, body, 0)

    def arrived_span(ref, width, start=0):
        return ref.at[pl.ds(0, slots - pair), pl.ds(start, width)]

    qkv[...] = jnp.zeros_like(qkv)
    sums[...] = jnp.zeros_like(sums)

    def project(block, start, width):
        f = span_of(block * quarter + start, width)
        x = fullx[:, f].astype(f32)
        sums[0] += lane_parts(x * x)
        sums[1] += lane_parts(x * rw_ref[:, f])
        scaled = (x * gain_ref[:, f]).astype(bf16)
        split = heads * HEAD_DIM
        qkv[:, :split] += dot(scaled, wq[f, :])
        qkv[:, split:] += dot(scaled, wkv[f, :])

    rings = [Ring(fullx, x_send, x_recv, 6 * n, n * TILE, TILE) for n in range(parts)]
    for n in range(parts):
        await_bytes(arrived_span(gotx, TILE, n * TILE), a2a_recv.at[n])
        compact(gotx, fullx, n * TILE, TILE)
        rings[n].begin()
        if n > 0:
            rings[n - 1].forward()
    whole_cols = pl.ds(0, quarter)
    send_pairs(peers, senddy, gotdy, a2a_send.at[4], a2a_recv.at[4], pair, whole_cols)
    for n in range(2, 5):
        loads[n].wait()
    project(m, 0, quarter)
    rings[parts - 1].forward()
    for n in range(parts):
        rings[n].near()
        rings[n].end()

        def body(i, carry):
            project(lax.rem(m + i, 4), n * TILE, TILE)
            return carry

        lax.fori_loop(1, 4, body, 0)

    mean = jnp.sum(sums[0], axis=1, keepdims=True) * (1.0 / (4 * quarter))
    inv = lax.rsqrt(mean + norm_eps)
    inv_col[...] = jnp.broadcast_to(inv, inv_col.shape)
    router_col[...] = jnp.broadcast_to(
        jnp.sum(sums[1], axis=1, keepdims=True), router_col.shape
    )
    split = heads * HEAD_DIM
    kv[me, :rows, :] = (qkv[:, split:] * inv).astype(bf16)

    await_bytes(arrived_span(gotdy, quarter), a2a_recv.at[4])
    compact(gotdy, fulldy, 0, quarter)
    half = rows // 2
    whole, top, low = pl.ds(0, rows + 16), pl.ds(0, half), pl.ds(half, half + 16)

    def send(block, to, part=whole):
        span = kv.at[block, part]
        remote(span, span, kv_send, kv_recv.at[block], "seq", to).start()

    def receive(block):
        await_bytes(kv.at[block], kv_recv.at[block])

    send(me, at.mine(1, 0))
    send(me, at.mine(3, 0))
    send(me, at.sibling)
    send(me, at.mine(0, 1))
    send(me, at.mine(0, 3))
    dy_ring = Ring(fulldy, d_send, d_recv, 0, 0, quarter)
    dy_ring.begin()
    for h in range(heads):
        part = (qkv[:, h * HEAD_DIM : (h + 1) * HEAD_DIM] * inv).astype(bf16)
        q4[h * rows : (h + 1) * rows, :] = part
    acc[...] = jnp.zeros_like(acc)
    den[...] = jnp.zeros_like(den)

    def masks(key_pos):
        mask = live(key_pos, qpos[...])
        return jnp.concatenate([mask] * (CHUNK // rows), axis=0)

    def process(block):
        keys, values, key_pos = key_block(kv, block)
        mask = masks(key_pos)
        for start in range(0, heads * rows, CHUNK):
            r = slice(start, start + CHUNK)
            t = jnp.tanh(dot(q4[r, :], keys, NT) * (SCALE / score_cap))
            w = jnp.where(mask, jnp.exp2(t * (score_cap * LOG2E)), 0.0)
            den[r] += lane_parts(w)
            acc[r] += dot(w.astype(bf16), values)

    def order(t):
        if isinstance(t, int):
            t = max(0, t)
            u = t if t < 4 else (t - 4) // 2 if t < 12 else t - 12
            return [0, 1, 3, 2][u], 0 if t < 4 else 1 + 2 * (t % 2) if t < 12 else 2
        a = lax.div(t + 12, 16)
        b = lax.div(t + 4, 16)
        u = (1 - a) * t + (a - b) * lax.div(t - 4, 2) + b * (t - 12)
        i = u + lax.div(u, 2) * (1 - 2 * lax.rem(u, 2))
        j = (a - b) * (1 + 2 * lax.rem(t, 2)) + 2 * b
        return i, j

    def take(t):
        i, j = order(t)
        block = at.mine(i, j)
        receive(block)
        if isinstance(t, int):
            if t == 1:
                send(block, at.mine(3, 0), low)
            if t == 2:
                send(block, at.mine(1, 0), top)
            if t < 4:
                send(block, at.mine(0, 1))
                send(block, at.mine(0, 3))
        else:

            @pl.when(t < 4)
            def _():
                send(block, at.mine(0, 1))
                send(block, at.mine(0, 3))

            @pl.when(jnp.logical_and(t >= 4, j == 1))
            def _():
                send(block, at.mine(0, 3), low)

            @pl.when(j == 3)
            def _():
                send(block, at.mine(0, 1), top)

        send(block, at.sibling)
        return block

    def other(t):
        block = at.theirs(*order(t))
        receive(block)
        return block

    process(me)
    for h in range(heads):
        r = slice(h * rows, (h + 1) * rows)
        qt4[:, r] = q4[r, :].T
    blocks = [take(1), take(2), other(0)]
    for block in blocks:
        process(block)

    def step(s, carry):
        t = 1 + 2 * s
        blocks = [take(t), take(t + 1), other(t - 2), other(t - 1)]

        @pl.when(s == 2)
        def _():
            dy_ring.forward()

        for block in blocks:
            process(block)
        return carry

    lax.fori_loop(1, 7, step, 0)
    blocks = [other(13), other(14), take(15), other(15)]
    for block in blocks:
        process(block)

    loads[5].wait()
    dy_ring.near()
    dy_ring.end()
    router = router_col[...]
    dots = jnp.zeros((rows, 1), f32)
    for n in range(split // TILE):
        pulled = dot(fulldy[...], wo[n * TILE : (n + 1) * TILE, :], NT)
        for g in range(TILE // HEAD_DIM):
            h = n * (TILE // HEAD_DIM) + g
            r = slice(h * rows, (h + 1) * rows)
            mine = pulled[:, g * HEAD_DIM : (g + 1) * HEAD_DIM]
            total = jnp.sum(den[r], axis=1, keepdims=True)
            att = (acc[r] / total).astype(bf16).astype(f32)
            lden[r] = jnp.broadcast_to(jnp.log2(total), (rows, 128))
            grad = (mine * router).astype(bf16)
            g4[r, :] = grad
            gt4[:, r] = grad.T
            row_delta = jnp.sum(grad.astype(f32) * att, axis=1, keepdims=True)
            delta[r] = jnp.broadcast_to(row_delta, (rows, 128))
            dots = dots + jnp.sum(mine * att, axis=1, keepdims=True)

    def send_stats(k):
        def body(i, carry):
            to = lax.rem(m + i, 4)
            here = stats.at[k, m]
            remote(here, here, st_send.at[k], st_recv.at[k], "mp", to).start()
            return carry

        lax.fori_loop(1, 4, body, 0)

    def take_stats(k):
        await_bytes(stats.at[k, pl.ds(0, 3)], st_recv.at[k])
        return as_column((stats[k, 0] + stats[k, 1] + stats[k, 2] + stats[k, 3])[0:1])

    stats[0, m] = jnp.broadcast_to(as_row(dots), stats.shape[2:])
    send_stats(0)

    dq[...] = jnp.zeros_like(dq)

    def terms(block):
        keys, values, key_pos = key_block(kv, block)
        width = keys.shape[0]
        mask = masks(key_pos)
        probs, grads = [], []
        for start in range(0, heads * rows, CHUNK):
            r = slice(start, start + CHUNK)
            t = jnp.tanh(dot(q4[r, :], keys, NT) * (SCALE / score_cap))
            p = jnp.exp2(t * (score_cap * LOG2E) - wide(lden[r], width))
            p = jnp.where(mask, p, 0.0)
            dp = dot(g4[r, :], values, NT)
            probs.append(p.astype(bf16))
            grads.append((p * (dp - wide(delta[r], width)) * (1.0 - t * t)).astype(bf16))
        probs, grads = jnp.concatenate(probs, axis=0), jnp.concatenate(grads, axis=0)
        dq[...] += dot(grads, keys)
        dk = dot(qt4[...], grads) * SCALE
        return jnp.concatenate([dk, dot(gt4[...], probs)], axis=0)

    def pass_on(k, late, i, j):
        await_bytes(from_sib.at[k], sib_recv.at[k])

        @pl.when(late == 0)
        def _():
            summed = to_b[k].astype(f32) + from_sib[k].astype(f32)
            to_b[k] = summed.astype(bf16)
            slot = (4 - j) * 4 + i
            remote(
                to_b.at[k], from_b.at[slot], sends.at[1], b_recv.at[slot], "seq",
                at.mine(0, j),
            ).start()

        @pl.when(late == 1)
        def _():
            total = to_b[k].astype(f32) + from_sib[k].astype(f32)
            for n in range(1, 4):
                await_bytes(from_b.at[n * 4 + i], b_recv.at[n * 4 + i])
                total = total + from_b[n * 4 + i].astype(f32)

            @pl.when(k < 15)
            def _():
                to_a[i] = total.astype(bf16)
                slot = 4 - i
                remote(
                    to_a.at[i], from_a.at[slot], sends.at[2], a_recv.at[slot], "seq",
                    at.mine(i, 0),
                ).start()

            @pl.when(k == 15)
            def _():
                final = total
                for n in range(1, 4):
                    await_bytes(from_a.at[n], a_recv.at[n])
                    final = final + from_a[n].astype(f32)
                dkv[...] = final.T.astype(bf16)

    def back_step(s, carry):
        late = s // 6
        places = []
        for n in range(2):
            k = 2 * s + n
            j = (1 + k // 4) * (1 - late)
            i = lax.rem(k + late, 4)
            places.append((k, late, i, j))
        for k, _, i, j in places:
            to_sib[k] = terms(at.theirs(i, j)).astype(bf16)
            remote(
                to_sib.at[k], from_sib.at[k], sends.at[0], sib_recv.at[k], "seq", at.sibling
            ).start()
        for k, _, i, j in places:
            to_b[k] = terms(at.mine(i, j)).astype(bf16)
        for where in places:
            pass_on(*where)
        return carry

    lax.fori_loop(0, 8, back_step, 0)
    for h in range(heads):
        r = slice(h * rows, (h + 1) * rows)
        dqb[:, h * HEAD_DIM : (h + 1) * HEAD_DIM] = (dq[r] * SCALE).astype(bf16)

    chunks = quarter // TILE
    stat = jnp.sum(dqb[...].astype(f32) * qkv[:, :split], axis=1, keepdims=True)
    stat = stat + jnp.sum(dkv[...].astype(f32) * qkv[:, split:], axis=1, keepdims=True)
    stats[1, m] = jnp.broadcast_to(as_row(stat), stats.shape[2:])
    send_stats(1)

    def contribution(block, n):
        f = span_of(block * quarter + n * TILE, TILE)
        total = dot(dqb[...], wq[f, :], NT) + dot(dkv[...], wkv[f, :], NT)
        return total * gain_ref[:, f]

    def rs(src, dst, n, k, to):
        k = 6 * n + k
        return remote(src, dst, rs_send.at[k], rs_recv.at[k], "mp", to)

    top, low = pl.ds(0, half), pl.ds(half, half)
    copies = []

    def hand_over(n):
        cols = pl.ds(n * TILE, TILE)
        copies[n][0].wait_recv()
        near[0, top, cols] = (
            near[0, top, cols].astype(f32) + relay[0, :, cols].astype(f32)
        ).astype(bf16)
        copies[n].append(rs(near.at[0, top, cols], arrived.at[0, top, cols], n, 4, right))
        copies[n][4].start()
        copies[n][1].wait_recv()
        near[1, low, cols] = (
            near[1, low, cols].astype(f32) + relay[1, :, cols].astype(f32)
        ).astype(bf16)
        copies[n].append(rs(near.at[1, low, cols], arrived.at[1, low, cols], n, 5, left))
        copies[n][5].start()

    back = sendx

    def finish_part(n):
        cols = pl.ds(n * TILE, TILE)
        f = span_of(m * quarter + n * TILE, TILE)
        own = contribution(m, n)
        for c in copies[n][2:]:
            c.wait_recv()
        own = own + arrived[0, :, cols].astype(f32) + arrived[1, :, cols].astype(f32)
        branch = inv * own - fullx[:, f].astype(f32) * factor + rw_ref[:, f] * router_grad
        back[:, cols] = dot(place[...], branch.astype(bf16), TN).astype(bf16)
        send_pairs(peers, back, got, back_send.at[n], back_recv.at[n], pair, cols)

    for n in range(chunks):
        cols = pl.ds(n * TILE, TILE)
        far[:, cols] = contribution(across, n).astype(bf16)
        first = rs(far.at[top, cols], relay.at[0, :, cols], n, 0, right)
        second = rs(far.at[low, cols], relay.at[1, :, cols], n, 1, left)
        first.start()
        second.start()
        near[0, :, cols] = contribution(right, n).astype(bf16)
        third = rs(near.at[0, low, cols], arrived.at[0, low, cols], n, 2, right)
        third.start()
        near[1, :, cols] = contribution(left, n).astype(bf16)
        fourth = rs(near.at[1, top, cols], arrived.at[1, top, cols], n, 3, left)
        fourth.start()
        copies.append([first, second, third, fourth])
        if n == 0:
            router_grad = take_stats(0)
            inv = inv_col[:, 0:1]
            for k in range(parts):
                await_bytes(arrived_span(sendx, TILE, k * TILE), a2a_send.at[k])
            factor = inv * inv * inv * take_stats(1) * (1.0 / (4 * quarter))
        if n > 0:
            hand_over(n - 1)
        if n > 1:
            finish_part(n - 2)
    hand_over(chunks - 1)
    finish_part(chunks - 2)
    finish_part(chunks - 1)

    for n in range(chunks):
        await_bytes(arrived_span(got, TILE, n * TILE), back_recv.at[n])
        await_bytes(arrived_span(back, TILE, n * TILE), back_send.at[n])
    await_bytes(arrived_span(senddy, quarter), a2a_send.at[4])
    await_bytes(sendm.at[others], a2a_send.at[5])
    for ring in rings:
        ring.sent()
    dy_ring.sent()
    for group in copies:
        for c in group:
            c.wait_send()
    for k in range(2):
        await_bytes(stats.at[k, pl.ds(0, 3)], st_send.at[k])
    await_bytes(to_sib, sends.at[0])
    await_bytes(to_b.at[pl.ds(0, 12)], sends.at[1])
    await_bytes(to_a.at[pl.ds(0, 3)], sends.at[2])
    await_bytes(kv.at[others], kv_send)


def sublayer(tokens, cotangent, gain, router_weight, w_query, w_key, w_value, w_out, idx, count, dest):
    peers = lax.axis_size("seq")
    tok_rows, quarter = tokens.shape
    width = 4 * quarter
    split = w_query.shape[1]
    heads = split // HEAD_DIM
    rows = ROUTED_DEV
    slots = 2 * rows
    bf16, f32 = jnp.bfloat16, jnp.float32
    vmem = pl.BlockSpec(memory_space=pltpu.VMEM)
    hbm = pl.BlockSpec(memory_space=pl.ANY)
    shape = jax.ShapeDtypeStruct
    dma = pltpu.SemaphoreType.DMA
    ram = pltpu.VMEM
    stacked = heads * rows

    def held(n):
        return ram((n, 2 * HEAD_DIM, rows), bf16)

    return pl.pallas_call(
        sublayer_kernel,
        in_specs=[vmem, vmem, pl.BlockSpec(memory_space=pltpu.SMEM), vmem, vmem] + [hbm] * 6,
        out_specs=[vmem] * 2,
        out_shape=[
            shape((slots, quarter), bf16),
            shape((8, slots), jnp.int32),
        ],
        scratch_shapes=[
            ram((tok_rows, quarter), bf16), ram((tok_rows, quarter), bf16),
            ram((width, split), bf16), ram((width, 2 * HEAD_DIM), bf16), ram((split, width), bf16),
            ram((slots, tok_rows), bf16),
            ram((slots, quarter), bf16), ram((slots, quarter), bf16),
            ram((slots, quarter), bf16), ram((slots, quarter), bf16),
            ram((peers, 8, 128), f32), ram((peers, 8, 128), f32),
            ram((rows, width), bf16), ram((rows, width), bf16),
            ram((rows, slots), bf16), ram((rows, 128), f32),
            ram((rows, split + 2 * HEAD_DIM), f32), ram((2, rows, 128), f32),
            ram((stacked, HEAD_DIM), bf16), ram((HEAD_DIM, stacked), bf16),
            ram((stacked, HEAD_DIM), bf16), ram((HEAD_DIM, stacked), bf16),
            ram((stacked, HEAD_DIM), f32), ram((stacked, 128), f32),
            ram((stacked, 128), f32), ram((stacked, 128), f32),
            ram((rows, 128), f32), ram((rows, 128), f32),
            ram((stacked, HEAD_DIM), f32), ram((rows, split), bf16),
            ram((rows, 2 * HEAD_DIM), bf16),
            ram((peers, rows + 16, 2 * HEAD_DIM), bf16),
            held(16), held(16), held(16), held(16), held(4), held(4),
            ram((rows, quarter), bf16), ram((2, rows, quarter), bf16),
            ram((2, rows // 2, quarter), bf16), ram((2, rows, quarter), bf16),
            ram((2, 4, 8, rows), f32),
            dma((6,)), dma((6,)), dma((6,)), dma((24,)), dma((24,)), dma((6,)), dma((6,)),
            dma, dma((peers,)),
            dma((3,)), dma((16,)), dma((16,)), dma((4,)), dma((24,)), dma((24,)),
            dma((4,)), dma((4,)), dma((2,)), dma((2,)),
        ],
        compiler_params=pltpu.CompilerParams(
            collective_id=0, has_side_effects=True, vmem_limit_bytes=VMEM_LIMIT
        ),
        name="sublayer",
    )(
        idx, dest, count, gain, router_weight,
        tokens, cotangent, w_query, w_key, w_value, w_out,
    )


def final_kernel(cot_ref, got_ref, source_ref, out_ref):
    block, slots = cot_ref.shape[0], got_ref.shape[0]
    first = pl.program_id(0) * block
    put = onehot(iota((block, slots), 0) + first == source_ref[0:1, :])
    out = cot_ref[...].astype(jnp.float32) + dot(put, got_ref[...])
    out_ref[...] = out.astype(jnp.bfloat16)


def finish(cotangent, got, source):
    tok_rows, quarter = cotangent.shape
    block = pl.BlockSpec((256, quarter), lambda i: (i, 0))

    def whole(array):
        return pl.BlockSpec(array.shape, lambda i: (0, 0))

    return pl.pallas_call(
        final_kernel,
        grid=(tok_rows // 256,),
        in_specs=[block, whole(got), whole(source)],
        out_specs=block,
        out_shape=jax.ShapeDtypeStruct(cotangent.shape, jnp.bfloat16),
        compiler_params=pltpu.CompilerParams(
            dimension_semantics=("arbitrary",), vmem_limit_bytes=VMEM_LIMIT
        ),
        name="add_branch",
    )(cotangent, got, source)


def on_device(
    tokens,
    cotangent,
    norm_gain,
    router_weight,
    w_query,
    w_key,
    w_value,
    w_out,
    routed_index,
    routed_count,
    routed_dest,
):
    got, source = sublayer(
        tokens,
        cotangent,
        norm_gain[None, :],
        router_weight[None, :],
        w_query,
        w_key,
        w_value,
        w_out,
        routed_index,
        routed_count,
        routed_dest,
    )
    return finish(cotangent, got, source)


def solution(mesh):
    in_specs = (
        P("seq", "mp"),
        P("seq", "mp"),
        P(),
        P(),
        P(None, "mp"),
        P(None, "mp"),
        P(None, "mp"),
        P("mp", None),
        P("seq", None),
        P("seq"),
        P("seq", None),
    )
    out_specs = P("seq", "mp")
    return jax.shard_map(
        on_device, mesh=mesh, in_specs=in_specs, out_specs=out_specs, check_vma=False
    )
```

```python
import jax
import jax.numpy as jnp
from jax import lax
from jax.experimental import pallas as pl
from jax.experimental.pallas import tpu as pltpu
from jax.sharding import PartitionSpec as P

HEAD_DIM = 128
ROUTED_DEV = 256
MESH = pl.DeviceIdType.MESH
NT = (((1,), (1,)), ((), ()))
NN = (((1,), (0,)), ((), ()))
TN = (((0,), (0,)), ((), ()))
MIB = 1024 * 1024
VMEM_LIMIT = 60 * MIB
norm_eps = 1e-05
score_cap = 5.0
LOG2E = 1.4426950408889634
SCALE = HEAD_DIM ** (-0.5)


def dot(a, b, dims=NN):
    return lax.dot_general(a, b, dims, preferred_element_type=jnp.float32)


def iota(shape, dim):
    return lax.broadcasted_iota(jnp.int32, shape, dim)


def onehot(mask):
    return jnp.where(mask, 1.0, 0.0).astype(jnp.bfloat16)


def remote(src, dst, send_sem, recv_sem, axis, index):
    return pltpu.make_async_remote_copy(
        src_ref=src,
        dst_ref=dst,
        send_sem=send_sem,
        recv_sem=recv_sem,
        device_id={axis: index},
        device_id_type=MESH,
    )


def await_bytes(ref, sem):
    pltpu.make_async_copy(ref, ref, sem).wait()


def greet(axis, count):
    me = lax.axis_index(axis)
    barrier = pltpu.get_barrier_semaphore()

    def body(i, carry):
        pl.semaphore_signal(
            barrier, inc=1, device_id={axis: lax.rem(me + i, count)}, device_id_type=MESH
        )
        return carry

    lax.fori_loop(1, count, body, 0)


def span_of(start, width):
    return pl.ds(pl.multiple_of(start, width), width)


def send_pairs(peers, send, got, send_sem, recv_sem, rows, cols):
    me = lax.axis_index("seq")
    mine = span_of(me * rows, rows)

    def body(i, carry):
        to = lax.rem(me + i, peers)
        block = send.at[span_of(to * rows, rows), cols]
        remote(block, got.at[mine, cols], send_sem, recv_sem, "seq", to).start()
        return carry

    lax.fori_loop(1, peers, body, 0)
    got[mine, cols] = send[mine, cols]


class Ring:
    def __init__(self, full, send_sem, recv_sem, base, start, width):
        self.full, self.send_sem, self.recv_sem = full, send_sem, recv_sem
        self.base, self.start, self.width = base, start, width
        self.quarter = full.shape[1] // 4
        half = full.shape[0] // 2
        self.top, self.low = pl.ds(0, half), pl.ds(half, half)
        self.m = lax.axis_index("mp")
        self.right, self.left = lax.rem(self.m + 1, 4), lax.rem(self.m + 3, 4)
        self.far = lax.rem(self.m + 2, 4)

    def move(self, block, rows, k, to):
        part = self.full.at[rows, span_of(block * self.quarter + self.start, self.width)]
        k = self.base + k
        return remote(part, part, self.send_sem.at[k], self.recv_sem.at[k], "mp", to)

    def begin(self):
        self.move(self.m, self.top, 0, self.right).start()
        self.move(self.m, self.low, 1, self.left).start()
        self.move(self.m, self.low, 2, self.right).start()
        self.move(self.m, self.top, 3, self.left).start()

    def forward(self):
        self.move(self.left, self.top, 0, self.right).wait_recv()
        self.move(self.left, self.top, 4, self.right).start()
        self.move(self.right, self.low, 1, self.left).wait_recv()
        self.move(self.right, self.low, 5, self.left).start()

    def whole(self, block, k, to):
        every = pl.ds(0, self.full.shape[0])
        return self.move(block, every, k, to)

    def direct(self):
        self.whole(self.m, 0, self.right).start()
        self.whole(self.m, 1, self.left).start()
        self.whole(self.m, 4, self.far).start()

    def direct_end(self):
        self.whole(self.left, 0, self.right).wait_recv()
        self.whole(self.right, 1, self.left).wait_recv()
        self.whole(self.far, 4, self.far).wait_recv()

    def direct_sent(self):
        for k in (0, 1, 4):
            self.whole(self.m, k, self.right).wait_send()

    def near(self):
        self.move(self.left, self.low, 2, self.right).wait_recv()
        self.move(self.right, self.top, 3, self.left).wait_recv()

    def end(self):
        self.move(self.far, self.top, 4, self.right).wait_recv()
        self.move(self.far, self.low, 5, self.left).wait_recv()

    def sent(self):
        for k in range(6):
            self.move(self.m, self.top, k, self.right).wait_send()


def live(kpos_row, qpos):
    parts = [kpos_row[:, c : c + 128] <= qpos for c in range(0, kpos_row.shape[1], 128)]
    return jnp.concatenate(parts, axis=1)


def wide(column, width):
    return jnp.concatenate([column] * (width // 128), axis=1)


def lane_parts(x):
    total = x[:, :128]
    for c in range(128, x.shape[1], 128):
        total = total + x[:, c : c + 128]
    return total


def as_row(column):
    size = column.shape[0]
    eye = iota((size, size), 0) == iota((size, size), 1)
    return jnp.sum(jnp.where(eye, column, 0.0), axis=0, keepdims=True)


def as_column(row):
    size = row.shape[1]
    eye = iota((size, size), 0) == iota((size, size), 1)
    return jnp.sum(jnp.where(eye, row, 0.0), axis=1, keepdims=True)


class Place:
    def __init__(self):
        self.me = lax.axis_index("seq")
        self.c = lax.rem(self.me, 2)
        self.sa = 2 + 6 * self.c
        self.sb = 8 - 6 * self.c
        self.a = lax.rem(self.me // self.sa, 4)
        self.b = lax.rem(self.me // self.sb, 4)
        self.sibling = self.me + 1 - 2 * self.c
        self.on_a = [lax.rem(self.a + i, 4) * self.sa for i in range(4)]
        self.on_b = [lax.rem(self.b + j, 4) * self.sb for j in range(4)]

    def first(self, i):
        return self.on_a[i] if isinstance(i, int) else lax.rem(self.a + i, 4) * self.sa

    def second(self, j):
        return self.on_b[j] if isinstance(j, int) else lax.rem(self.b + j, 4) * self.sb

    def mine(self, i, j):
        return self.first(i) + self.second(j) + self.c

    def theirs(self, i, j):
        return self.second(i) + self.first(j) + 1 - self.c


def key_block(kv, block):
    rows = kv[block]
    keys = rows[:ROUTED_DEV, :HEAD_DIM]
    values = rows[:ROUTED_DEV, HEAD_DIM:]
    digits = rows[ROUTED_DEV:].astype(jnp.float32)
    return keys, values, digits[0:1] * 256.0 + digits[1:2]


CHUNK = 512
FINAL_ROWS = 512
TILE = 256


def sublayer_kernel(
    idx_ref, dest_ref, count_ref, gain_ref, rw_ref,
    tok_hbm, cot_hbm, wq_hbm, wk_hbm, wv_hbm, wo_hbm,
    got, source_ref,
    tok, cot, wq, wkv, wo, pick, sendx, senddy, gotx, gotdy, sendm, gotm,
    fullx, fulldy, place, qpos, qkv, sums, q4, qt4, g4, gt4, acc, den, lden, delta,
    inv_col, router_col, dq, dqb, dkv,
    kv, to_sib, from_sib, to_b, from_b, to_a, from_a, far, near, relay, arrived, stats,
    load_sem, a2a_send, a2a_recv, x_send, x_recv, d_send, d_recv, kv_send, kv_recv,
    sends, sib_recv, b_recv, a_recv, rs_send, rs_recv, back_send, back_recv, st_send, st_recv,
):
    peers = lax.axis_size("seq")
    m = lax.axis_index("mp")
    at = Place()
    me = at.me
    bf16, f32 = jnp.bfloat16, jnp.float32
    slots = sendx.shape[0]
    tok_rows, quarter = tok.shape
    rows = ROUTED_DEV
    heads = wq.shape[1] // HEAD_DIM
    pair = slots // peers
    parts = quarter // TILE
    right, left, across = lax.rem(m + 1, 4), lax.rem(m + 3, 4), lax.rem(m + 2, 4)
    loads = [
        pltpu.make_async_copy(src, dst, load_sem.at[n])
        for n, (src, dst) in enumerate(
            [
                (tok_hbm, tok),
                (cot_hbm, cot),
                (wq_hbm, wq),
                (wk_hbm, wkv.at[:, pl.ds(0, HEAD_DIM)]),
                (wv_hbm, wkv.at[:, pl.ds(HEAD_DIM, HEAD_DIM)]),
                (wo_hbm, wo),
            ]
        )
    ]
    loads[0].start()
    greet("seq", peers)
    greet("mp", 4)

    idx = idx_ref[...]
    dest = dest_ref[...]
    valid = iota((1, slots), 1) < count_ref[0]
    owner = jnp.where(valid, lax.shift_right_logical(dest, 8), peers)
    place_slot = jnp.bitwise_and(dest, rows - 1)
    rows_i = iota((slots, slots), 0)
    cols_i = iota((slots, slots), 1)
    owner_col = jnp.sum(jnp.where(rows_i == cols_i, owner, 0), axis=1, keepdims=True)
    earlier = jnp.logical_and(owner_col == owner, rows_i < cols_i)
    rank = jnp.sum(jnp.where(earlier, 1, 0), axis=0, keepdims=True)
    buffer_place = jnp.where(valid, owner * pair + rank, slots)
    hit = rows_i == buffer_place
    source = jnp.sum(jnp.where(hit, idx - tok_rows, 0), axis=1, keepdims=True) + tok_rows
    pick[...] = onehot(iota((slots, tok_rows), 1) == source)

    lanes = iota((128, slots), 0)

    def spread(hits, entries, lane, shift):
        held = jnp.where(hits, entries, 0.0).astype(bf16)
        return dot(held, onehot(lanes == lane + shift), NT)

    owner_hit = iota((peers, slots), 0) == owner
    rank_lane = jnp.where(valid, rank, 128)
    position = me * tok_rows + idx
    digits = [
        place_slot + 1,
        lax.shift_right_logical(position, 8),
        jnp.bitwise_and(position, 255),
    ]
    meta = sum(
        spread(owner_hit, d.astype(f32), rank_lane, n * pair) for n, d in enumerate(digits)
    )
    sendm[...] = jnp.broadcast_to(meta[:, None, :], sendm.shape)

    pl.semaphore_wait(pltpu.get_barrier_semaphore(), peers - 1 + 3)

    def send_meta(src, dst, k):
        def body(i, carry):
            to = lax.rem(me + i, peers)
            remote(src.at[to], dst.at[me], a2a_send.at[k], a2a_recv.at[k], "seq", to).start()
            return carry

        lax.fori_loop(1, peers, body, 0)
        dst[me] = src[me]

    send_meta(sendm, gotm, 5)

    def pack(held, send, start, width):
        def body(n, carry):
            cols = span_of(start + n * TILE, TILE)
            send[:, cols] = dot(pick[...], held[:, cols]).astype(bf16)
            return carry

        lax.fori_loop(0, width // TILE, body, 0)
        return pl.ds(start, width)

    loads[0].wait()
    for load in loads[1:]:
        load.start()
    for n in range(parts):
        cols = pack(tok, sendx, n * TILE, TILE)
        send_pairs(peers, sendx, gotx, a2a_send.at[n], a2a_recv.at[n], pair, cols)
    loads[1].wait()
    pack(cot, senddy, 0, quarter)
    source_row = jnp.sum(jnp.where(rows_i == cols_i, source, 0), axis=0, keepdims=True)
    source_ref[...] = jnp.broadcast_to(source_row, source_ref.shape)

    others = pl.ds(0, peers - 1)
    column = iota((128, slots), 0)
    within = jnp.bitwise_and(iota((128, slots), 1), pair - 1)
    sender = iota((peers, slots), 0) == iota((peers, slots), 1) // pair

    def flat(got_rows, shift):
        out = dot(got_rows, onehot(column == within + shift))
        return jnp.sum(jnp.where(sender, out, 0.0), axis=0, keepdims=True)

    await_bytes(gotm.at[others], a2a_recv.at[5])
    got_meta = gotm[:, 0, :].astype(bf16)
    slot_in = flat(got_meta, 0)
    pos_in = flat(got_meta, pair) * 256.0 + flat(got_meta, 2 * pair)
    here = iota((rows, slots), 0).astype(f32) + 1.0 == slot_in
    place[...] = onehot(here)
    row_pos = jnp.sum(jnp.where(here, pos_in, 0.0), axis=1, keepdims=True)
    qpos[...] = jnp.broadcast_to(row_pos, qpos.shape)
    kpos = as_row(row_pos).astype(jnp.int32)
    pos_digits = jnp.where(
        iota((16, rows), 0) == 0,
        lax.shift_right_logical(kpos, 8),
        jnp.bitwise_and(kpos, 255),
    )
    kv[me, rows:, :] = pos_digits.astype(f32).astype(bf16)

    def compact(got_rows, full, start, width):
        def body(n, carry):
            to = span_of(m * quarter + start + n * TILE, TILE)
            part = got_rows[:, span_of(start + n * TILE, TILE)]
            full[:, to] = dot(place[...], part).astype(bf16)
            return carry

        lax.fori_loop(0, width // TILE, body, 0)

    def arrived_span(ref, width, start=0):
        return ref.at[pl.ds(0, slots - pair), pl.ds(start, width)]

    qkv[...] = jnp.zeros_like(qkv)
    sums[...] = jnp.zeros_like(sums)

    def project(block, start, width):
        f = span_of(block * quarter + start, width)
        x = fullx[:, f].astype(f32)
        sums[0] += lane_parts(x * x)
        sums[1] += lane_parts(x * rw_ref[:, f])
        scaled = (x * gain_ref[:, f]).astype(bf16)
        split = heads * HEAD_DIM
        qkv[:, :split] += dot(scaled, wq[f, :])
        qkv[:, split:] += dot(scaled, wkv[f, :])

    rings = [Ring(fullx, x_send, x_recv, 6 * n, n * TILE, TILE) for n in range(parts)]
    for n in range(parts):
        await_bytes(arrived_span(gotx, TILE, n * TILE), a2a_recv.at[n])
        compact(gotx, fullx, n * TILE, TILE)
        rings[n].begin()
        if n > 0:
            rings[n - 1].forward()
    whole_cols = pl.ds(0, quarter)
    send_pairs(peers, senddy, gotdy, a2a_send.at[4], a2a_recv.at[4], pair, whole_cols)
    rings[parts - 1].forward()
    for n in range(2, 5):
        loads[n].wait()
    project(m, 0, quarter)
    for n in range(parts):
        rings[n].near()
        rings[n].end()

        def body(i, carry):
            project(lax.rem(m + i, 4), n * TILE, TILE)
            return carry

        lax.fori_loop(1, 4, body, 0)

    mean = jnp.sum(sums[0], axis=1, keepdims=True) * (1.0 / (4 * quarter))
    inv = lax.rsqrt(mean + norm_eps)
    inv_col[...] = jnp.broadcast_to(inv, inv_col.shape)
    router_col[...] = jnp.broadcast_to(
        jnp.sum(sums[1], axis=1, keepdims=True), router_col.shape
    )
    split = heads * HEAD_DIM
    kv[me, :rows, :] = (qkv[:, split:] * inv).astype(bf16)

    half = rows // 2
    whole, top, low = pl.ds(0, rows + 16), pl.ds(0, half), pl.ds(half, half + 16)

    def send(block, to, part=whole):
        span = kv.at[block, part]
        remote(span, span, kv_send, kv_recv.at[block], "seq", to).start()

    def receive(block):
        await_bytes(kv.at[block], kv_recv.at[block])

    send(me, at.mine(1, 0))
    send(me, at.mine(3, 0))
    send(me, at.sibling)
    dy_rings = [Ring(fulldy, d_send, d_recv, 6 * n, n * TILE, TILE) for n in range(parts)]
    await_bytes(arrived_span(gotdy, quarter), a2a_recv.at[4])
    compact(gotdy, fulldy, 0, quarter)
    dy_rings[0].begin()
    dy_rings[1].begin()
    for h in range(heads):
        part = (qkv[:, h * HEAD_DIM : (h + 1) * HEAD_DIM] * inv).astype(bf16)
        q4[h * rows : (h + 1) * rows, :] = part
    acc[...] = jnp.zeros_like(acc)
    den[...] = jnp.zeros_like(den)

    def masks(key_pos):
        mask = live(key_pos, qpos[...])
        return jnp.concatenate([mask] * (CHUNK // rows), axis=0)

    def process(block):
        keys, values, key_pos = key_block(kv, block)
        mask = masks(key_pos)
        for start in range(0, heads * rows, CHUNK):
            r = slice(start, start + CHUNK)
            t = jnp.tanh(dot(q4[r, :], keys, NT) * (SCALE / score_cap))
            w = jnp.where(mask, jnp.exp2(t * (score_cap * LOG2E)), 0.0)
            den[r] += lane_parts(w)
            acc[r] += dot(w.astype(bf16), values)

    def order(t):
        if isinstance(t, int):
            t = max(0, t)
            u = t if t < 4 else (t - 4) // 2 if t < 12 else t - 12
            return [0, 1, 3, 2][u], 0 if t < 4 else 1 + 2 * (t % 2) if t < 12 else 2
        a = lax.div(t + 12, 16)
        b = lax.div(t + 4, 16)
        u = (1 - a) * t + (a - b) * lax.div(t - 4, 2) + b * (t - 12)
        i = u + lax.div(u, 2) * (1 - 2 * lax.rem(u, 2))
        j = (a - b) * (1 + 2 * lax.rem(t, 2)) + 2 * b
        return i, j

    def take(t):
        i, j = order(t)
        block = at.mine(i, j)
        receive(block)
        if isinstance(t, int):
            if t == 1:
                send(block, at.mine(3, 0), low)
            if t == 2:
                send(block, at.mine(1, 0), top)
            if t == 1:
                send(me, at.mine(0, 1))
                send(me, at.mine(0, 3))
            if t < 4:
                send(block, at.mine(0, 1))
                send(block, at.mine(0, 3))
        else:

            @pl.when(t < 4)
            def _():
                send(block, at.mine(0, 1))
                send(block, at.mine(0, 3))

            @pl.when(jnp.logical_and(t >= 4, j == 1))
            def _():
                send(block, at.mine(0, 3), low)

            @pl.when(j == 3)
            def _():
                send(block, at.mine(0, 1), top)

        send(block, at.sibling)
        return block

    def other(t):
        block = at.theirs(*order(t))
        receive(block)
        return block

    process(me)
    for h in range(heads):
        r = slice(h * rows, (h + 1) * rows)
        qt4[:, r] = q4[r, :].T
    blocks = [take(1), take(2), other(0)]
    for block in blocks:
        process(block)

    def step(s, carry):
        t = 1 + 2 * s
        blocks = [take(t), take(t + 1), other(t - 2), other(t - 1)]

        @pl.when(s == 1)
        def _():
            for ring in dy_rings[:2]:
                ring.forward()
            for ring in dy_rings[2:]:
                ring.direct()

        for block in blocks:
            process(block)
        return carry

    lax.fori_loop(1, 7, step, 0)
    blocks = [other(13), other(14), take(15), other(15)]
    for block in blocks:
        process(block)

    loads[5].wait()
    for ring in dy_rings[:2]:
        ring.near()
        ring.end()
    for ring in dy_rings[2:]:
        ring.direct_end()
    router = router_col[...]
    dots = jnp.zeros((rows, 1), f32)
    for n in range(split // TILE):
        pulled = dot(fulldy[...], wo[n * TILE : (n + 1) * TILE, :], NT)
        for g in range(TILE // HEAD_DIM):
            h = n * (TILE // HEAD_DIM) + g
            r = slice(h * rows, (h + 1) * rows)
            mine = pulled[:, g * HEAD_DIM : (g + 1) * HEAD_DIM]
            total = jnp.sum(den[r], axis=1, keepdims=True)
            att = (acc[r] / total).astype(bf16).astype(f32)
            lden[r] = jnp.broadcast_to(jnp.log2(total), (rows, 128))
            grad = (mine * router).astype(bf16)
            g4[r, :] = grad
            gt4[:, r] = grad.T
            row_delta = jnp.sum(grad.astype(f32) * att, axis=1, keepdims=True)
            delta[r] = jnp.broadcast_to(row_delta, (rows, 128))
            dots = dots + jnp.sum(mine * att, axis=1, keepdims=True)

    def send_stats(k):
        def body(i, carry):
            to = lax.rem(m + i, 4)
            here = stats.at[k, m]
            remote(here, here, st_send.at[k], st_recv.at[k], "mp", to).start()
            return carry

        lax.fori_loop(1, 4, body, 0)

    def take_stats(k):
        await_bytes(stats.at[k, pl.ds(0, 3)], st_recv.at[k])
        return as_column((stats[k, 0] + stats[k, 1] + stats[k, 2] + stats[k, 3])[0:1])

    stats[0, m] = jnp.broadcast_to(as_row(dots), stats.shape[2:])
    send_stats(0)

    dq[...] = jnp.zeros_like(dq)

    def terms(block):
        keys, values, key_pos = key_block(kv, block)
        width = keys.shape[0]
        mask = masks(key_pos)
        probs, grads = [], []
        for start in range(0, heads * rows, CHUNK):
            r = slice(start, start + CHUNK)
            t = jnp.tanh(dot(q4[r, :], keys, NT) * (SCALE / score_cap))
            p = jnp.exp2(t * (score_cap * LOG2E) - wide(lden[r], width))
            p = jnp.where(mask, p, 0.0)
            dp = dot(g4[r, :], values, NT)
            probs.append(p.astype(bf16))
            grads.append((p * (dp - wide(delta[r], width)) * (1.0 - t * t)).astype(bf16))
        probs, grads = jnp.concatenate(probs, axis=0), jnp.concatenate(grads, axis=0)
        dq[...] += dot(grads, keys)
        dk = dot(qt4[...], grads) * SCALE
        return jnp.concatenate([dk, dot(gt4[...], probs)], axis=0)

    def pass_on(k, late, i, j):
        await_bytes(from_sib.at[k], sib_recv.at[k])

        @pl.when(late == 0)
        def _():
            summed = to_b[k].astype(f32) + from_sib[k].astype(f32)
            to_b[k] = summed.astype(bf16)
            slot = (4 - j) * 4 + i
            remote(
                to_b.at[k], from_b.at[slot], sends.at[1], b_recv.at[slot], "seq",
                at.mine(0, j),
            ).start()

        @pl.when(late == 1)
        def _():
            total = to_b[k].astype(f32) + from_sib[k].astype(f32)
            for n in range(1, 4):
                await_bytes(from_b.at[n * 4 + i], b_recv.at[n * 4 + i])
                total = total + from_b[n * 4 + i].astype(f32)

            @pl.when(k < 15)
            def _():
                to_a[i] = total.astype(bf16)
                slot = 4 - i
                remote(
                    to_a.at[i], from_a.at[slot], sends.at[2], a_recv.at[slot], "seq",
                    at.mine(i, 0),
                ).start()

            @pl.when(k == 15)
            def _():
                final = total
                for n in range(1, 4):
                    await_bytes(from_a.at[n], a_recv.at[n])
                    final = final + from_a[n].astype(f32)
                dkv[...] = final.T.astype(bf16)

    def back_step(s, carry):
        late = s // 6
        places = []
        for n in range(2):
            k = 2 * s + n
            j = (1 + k // 4) * (1 - late)
            i = lax.rem(k + late, 4)
            places.append((k, late, i, j))
        for k, _, i, j in places:
            to_sib[k] = terms(at.theirs(i, j)).astype(bf16)
            remote(
                to_sib.at[k], from_sib.at[k], sends.at[0], sib_recv.at[k], "seq", at.sibling
            ).start()
        for k, _, i, j in places:
            to_b[k] = terms(at.mine(i, j)).astype(bf16)
        for where in places:
            pass_on(*where)
        return carry

    lax.fori_loop(0, 8, back_step, 0)
    for h in range(heads):
        r = slice(h * rows, (h + 1) * rows)
        dqb[:, h * HEAD_DIM : (h + 1) * HEAD_DIM] = (dq[r] * SCALE).astype(bf16)

    chunks = quarter // TILE
    def contribution(block, n):
        f = span_of(block * quarter + n * TILE, TILE)
        total = dot(dqb[...], wq[f, :], NT) + dot(dkv[...], wkv[f, :], NT)
        return total * gain_ref[:, f]

    def rs(src, dst, n, k, to):
        k = 6 * n + k
        return remote(src, dst, rs_send.at[k], rs_recv.at[k], "mp", to)

    top, low = pl.ds(0, half), pl.ds(half, half)
    copies = []

    def hand_over(n):
        cols = pl.ds(n * TILE, TILE)
        copies[n][0].wait_recv()
        near[0, top, cols] = (
            near[0, top, cols].astype(f32) + relay[0, :, cols].astype(f32)
        ).astype(bf16)
        copies[n].append(rs(near.at[0, top, cols], arrived.at[0, top, cols], n, 4, right))
        copies[n][4].start()
        copies[n][1].wait_recv()
        near[1, low, cols] = (
            near[1, low, cols].astype(f32) + relay[1, :, cols].astype(f32)
        ).astype(bf16)
        copies[n].append(rs(near.at[1, low, cols], arrived.at[1, low, cols], n, 5, left))
        copies[n][5].start()

    back = sendx

    def finish_part(n):
        cols = pl.ds(n * TILE, TILE)
        f = span_of(m * quarter + n * TILE, TILE)
        own = contribution(m, n)
        for c in copies[n][2:]:
            c.wait_recv()
        own = own + arrived[0, :, cols].astype(f32) + arrived[1, :, cols].astype(f32)
        branch = inv * own - fullx[:, f].astype(f32) * factor + rw_ref[:, f] * router_grad
        back[:, cols] = dot(place[...], branch.astype(bf16), TN).astype(bf16)
        send_pairs(peers, back, got, back_send.at[n], back_recv.at[n], pair, cols)

    def issue(n):
        cols = pl.ds(n * TILE, TILE)
        far[:, cols] = contribution(across, n).astype(bf16)
        first = rs(far.at[top, cols], relay.at[0, :, cols], n, 0, right)
        second = rs(far.at[low, cols], relay.at[1, :, cols], n, 1, left)
        first.start()
        second.start()
        near[0, :, cols] = contribution(right, n).astype(bf16)
        third = rs(near.at[0, low, cols], arrived.at[0, low, cols], n, 2, right)
        third.start()
        near[1, :, cols] = contribution(left, n).astype(bf16)
        fourth = rs(near.at[1, top, cols], arrived.at[1, top, cols], n, 3, left)
        fourth.start()
        copies.append([first, second, third, fourth])

    issue(0)
    stat = jnp.sum(dqb[...].astype(f32) * qkv[:, :split], axis=1, keepdims=True)
    stat = stat + jnp.sum(dkv[...].astype(f32) * qkv[:, split:], axis=1, keepdims=True)
    stats[1, m] = jnp.broadcast_to(as_row(stat), stats.shape[2:])
    send_stats(1)
    issue(1)
    router_grad = take_stats(0)
    inv = inv_col[:, 0:1]
    for k in range(parts):
        await_bytes(arrived_span(sendx, TILE, k * TILE), a2a_send.at[k])
    hand_over(0)
    factor = inv * inv * inv * take_stats(1) * (1.0 / (4 * quarter))
    for n in range(1, chunks):
        if n + 1 < chunks:
            issue(n + 1)
        hand_over(n)
        finish_part(n - 1)
    finish_part(chunks - 1)

    for n in range(chunks):
        await_bytes(arrived_span(got, TILE, n * TILE), back_recv.at[n])
        await_bytes(arrived_span(back, TILE, n * TILE), back_send.at[n])
    await_bytes(arrived_span(senddy, quarter), a2a_send.at[4])
    await_bytes(sendm.at[others], a2a_send.at[5])
    for ring in rings + dy_rings[:2]:
        ring.sent()
    for ring in dy_rings[2:]:
        ring.direct_sent()
    for group in copies:
        for c in group:
            c.wait_send()
    for k in range(2):
        await_bytes(stats.at[k, pl.ds(0, 3)], st_send.at[k])
    await_bytes(to_sib, sends.at[0])
    await_bytes(to_b.at[pl.ds(0, 12)], sends.at[1])
    await_bytes(to_a.at[pl.ds(0, 3)], sends.at[2])
    await_bytes(kv.at[others], kv_send)


def sublayer(tokens, cotangent, gain, router_weight, w_query, w_key, w_value, w_out, idx, count, dest):
    peers = lax.axis_size("seq")
    tok_rows, quarter = tokens.shape
    width = 4 * quarter
    split = w_query.shape[1]
    heads = split // HEAD_DIM
    rows = ROUTED_DEV
    slots = 2 * rows
    bf16, f32 = jnp.bfloat16, jnp.float32
    vmem = pl.BlockSpec(memory_space=pltpu.VMEM)
    hbm = pl.BlockSpec(memory_space=pl.ANY)
    shape = jax.ShapeDtypeStruct
    dma = pltpu.SemaphoreType.DMA
    ram = pltpu.VMEM
    stacked = heads * rows

    def held(n):
        return ram((n, 2 * HEAD_DIM, rows), bf16)

    return pl.pallas_call(
        sublayer_kernel,
        in_specs=[vmem, vmem, pl.BlockSpec(memory_space=pltpu.SMEM), vmem, vmem] + [hbm] * 6,
        out_specs=[vmem] * 2,
        out_shape=[
            shape((slots, quarter), bf16),
            shape((8, slots), jnp.int32),
        ],
        scratch_shapes=[
            ram((tok_rows, quarter), bf16), ram((tok_rows, quarter), bf16),
            ram((width, split), bf16), ram((width, 2 * HEAD_DIM), bf16), ram((split, width), bf16),
            ram((slots, tok_rows), bf16),
            ram((slots, quarter), bf16), ram((slots, quarter), bf16),
            ram((slots, quarter), bf16), ram((slots, quarter), bf16),
            ram((peers, 8, 128), f32), ram((peers, 8, 128), f32),
            ram((rows, width), bf16), ram((rows, width), bf16),
            ram((rows, slots), bf16), ram((rows, 128), f32),
            ram((rows, split + 2 * HEAD_DIM), f32), ram((2, rows, 128), f32),
            ram((stacked, HEAD_DIM), bf16), ram((HEAD_DIM, stacked), bf16),
            ram((stacked, HEAD_DIM), bf16), ram((HEAD_DIM, stacked), bf16),
            ram((stacked, HEAD_DIM), f32), ram((stacked, 128), f32),
            ram((stacked, 128), f32), ram((stacked, 128), f32),
            ram((rows, 128), f32), ram((rows, 128), f32),
            ram((stacked, HEAD_DIM), f32), ram((rows, split), bf16),
            ram((rows, 2 * HEAD_DIM), bf16),
            ram((peers, rows + 16, 2 * HEAD_DIM), bf16),
            held(16), held(16), held(16), held(16), held(4), held(4),
            ram((rows, quarter), bf16), ram((2, rows, quarter), bf16),
            ram((2, rows // 2, quarter), bf16), ram((2, rows, quarter), bf16),
            ram((2, 4, 8, rows), f32),
            dma((6,)), dma((6,)), dma((6,)), dma((24,)), dma((24,)), dma((24,)), dma((24,)),
            dma, dma((peers,)),
            dma((3,)), dma((16,)), dma((16,)), dma((4,)), dma((24,)), dma((24,)),
            dma((4,)), dma((4,)), dma((2,)), dma((2,)),
        ],
        compiler_params=pltpu.CompilerParams(
            collective_id=0, has_side_effects=True, vmem_limit_bytes=VMEM_LIMIT
        ),
        name="sublayer",
    )(
        idx, dest, count, gain, router_weight,
        tokens, cotangent, w_query, w_key, w_value, w_out,
    )


def final_kernel(cot_hbm, got_hbm, source_ref, out_hbm, cot, got, out, loads, stores):
    block, slots = FINAL_ROWS, got.shape[0]
    steps = cot.shape[0] // block
    got_load = pltpu.make_async_copy(got_hbm, got, loads.at[steps])
    got_load.start()

    def copy(n, src, dst, sems):
        rows = pl.ds(n * block, block)
        return pltpu.make_async_copy(src.at[rows], dst.at[rows], sems.at[n])

    for n in range(steps):
        copy(n, cot_hbm, cot, loads).start()
    got_load.wait()
    for n in range(steps):
        rows = pl.ds(n * block, block)
        put = onehot(iota((block, slots), 0) + n * block == source_ref[0:1, :])
        copy(n, cot_hbm, cot, loads).wait()
        total = cot[rows, :].astype(jnp.float32) + dot(put, got[...])
        out[rows, :] = total.astype(jnp.bfloat16)
        copy(n, out, out_hbm, stores).start()
    for n in range(steps):
        copy(n, out, out_hbm, stores).wait()


def finish(cotangent, got, source):
    hbm = pl.BlockSpec(memory_space=pl.ANY)
    steps = cotangent.shape[0] // FINAL_ROWS
    return pl.pallas_call(
        final_kernel,
        in_specs=[hbm, hbm, pl.BlockSpec(memory_space=pltpu.VMEM)],
        out_specs=hbm,
        out_shape=jax.ShapeDtypeStruct(cotangent.shape, jnp.bfloat16),
        scratch_shapes=[
            pltpu.VMEM(cotangent.shape, jnp.bfloat16),
            pltpu.VMEM(got.shape, jnp.bfloat16),
            pltpu.VMEM(cotangent.shape, jnp.bfloat16),
            pltpu.SemaphoreType.DMA((steps + 1,)),
            pltpu.SemaphoreType.DMA((steps,)),
        ],
        compiler_params=pltpu.CompilerParams(vmem_limit_bytes=VMEM_LIMIT),
        name="add_branch",
    )(cotangent, got, source)


def on_device(
    tokens,
    cotangent,
    norm_gain,
    router_weight,
    w_query,
    w_key,
    w_value,
    w_out,
    routed_index,
    routed_count,
    routed_dest,
):
    got, source = sublayer(
        tokens,
        cotangent,
        norm_gain[None, :],
        router_weight[None, :],
        w_query,
        w_key,
        w_value,
        w_out,
        routed_index,
        routed_count,
        routed_dest,
    )
    return finish(cotangent, got, source)


def solution(mesh):
    in_specs = (
        P("seq", "mp"),
        P("seq", "mp"),
        P(),
        P(),
        P(None, "mp"),
        P(None, "mp"),
        P(None, "mp"),
        P("mp", None),
        P("seq", None),
        P("seq"),
        P("seq", None),
    )
    out_specs = P("seq", "mp")
    return jax.shard_map(
        on_device, mesh=mesh, in_specs=in_specs, out_specs=out_specs, check_vma=False
    )
```

```python
import jax
import jax.numpy as jnp
from jax import lax
from jax.experimental import pallas as pl
from jax.experimental.pallas import tpu as pltpu
from jax.sharding import PartitionSpec as P

HEAD_DIM = 128
ROUTED_DEV = 256
MESH = pl.DeviceIdType.MESH
NT = (((1,), (1,)), ((), ()))
NN = (((1,), (0,)), ((), ()))
TN = (((0,), (0,)), ((), ()))
MIB = 1024 * 1024
VMEM_LIMIT = 60 * MIB
norm_eps = 1e-05
score_cap = 5.0
LOG2E = 1.4426950408889634
SCALE = HEAD_DIM ** (-0.5)


def dot(a, b, dims=NN):
    return lax.dot_general(a, b, dims, preferred_element_type=jnp.float32)


def iota(shape, dim):
    return lax.broadcasted_iota(jnp.int32, shape, dim)


def onehot(mask):
    return jnp.where(mask, 1.0, 0.0).astype(jnp.bfloat16)


def remote(src, dst, send_sem, recv_sem, axis, index):
    return pltpu.make_async_remote_copy(
        src_ref=src,
        dst_ref=dst,
        send_sem=send_sem,
        recv_sem=recv_sem,
        device_id={axis: index},
        device_id_type=MESH,
    )


def await_bytes(ref, sem):
    pltpu.make_async_copy(ref, ref, sem).wait()


def greet(axis, count):
    me = lax.axis_index(axis)
    barrier = pltpu.get_barrier_semaphore()

    def body(i, carry):
        pl.semaphore_signal(
            barrier, inc=1, device_id={axis: lax.rem(me + i, count)}, device_id_type=MESH
        )
        return carry

    lax.fori_loop(1, count, body, 0)


def span_of(start, width):
    return pl.ds(pl.multiple_of(start, width), width)


def send_pairs(peers, send, got, send_sem, recv_sem, rows, cols):
    me = lax.axis_index("seq")
    mine = span_of(me * rows, rows)

    def body(i, carry):
        to = lax.rem(me + i, peers)
        block = send.at[span_of(to * rows, rows), cols]
        remote(block, got.at[mine, cols], send_sem, recv_sem, "seq", to).start()
        return carry

    lax.fori_loop(1, peers, body, 0)
    got[mine, cols] = send[mine, cols]


class Ring:
    def __init__(self, full, send_sem, recv_sem, base, start, width):
        self.full, self.send_sem, self.recv_sem = full, send_sem, recv_sem
        self.base, self.start, self.width = base, start, width
        self.quarter = full.shape[1] // 4
        half = full.shape[0] // 2
        self.top, self.low = pl.ds(0, half), pl.ds(half, half)
        self.m = lax.axis_index("mp")
        self.right, self.left = lax.rem(self.m + 1, 4), lax.rem(self.m + 3, 4)
        self.far = lax.rem(self.m + 2, 4)

    def move(self, block, rows, k, to):
        part = self.full.at[rows, span_of(block * self.quarter + self.start, self.width)]
        k = self.base + k
        return remote(part, part, self.send_sem.at[k], self.recv_sem.at[k], "mp", to)

    def begin(self):
        self.move(self.m, self.top, 0, self.right).start()
        self.move(self.m, self.low, 1, self.left).start()
        self.move(self.m, self.low, 2, self.right).start()
        self.move(self.m, self.top, 3, self.left).start()

    def forward(self):
        self.move(self.left, self.top, 0, self.right).wait_recv()
        self.move(self.left, self.top, 4, self.right).start()
        self.move(self.right, self.low, 1, self.left).wait_recv()
        self.move(self.right, self.low, 5, self.left).start()

    def near(self):
        self.move(self.left, self.low, 2, self.right).wait_recv()
        self.move(self.right, self.top, 3, self.left).wait_recv()

    def end(self):
        self.move(self.far, self.top, 4, self.right).wait_recv()
        self.move(self.far, self.low, 5, self.left).wait_recv()

    def sent(self):
        for k in range(6):
            self.move(self.m, self.top, k, self.right).wait_send()


def live(kpos_row, qpos):
    parts = [kpos_row[:, c : c + 128] <= qpos for c in range(0, kpos_row.shape[1], 128)]
    return jnp.concatenate(parts, axis=1)


def wide(column, width):
    return jnp.concatenate([column] * (width // 128), axis=1)


def lane_parts(x):
    total = x[:, :128]
    for c in range(128, x.shape[1], 128):
        total = total + x[:, c : c + 128]
    return total


def as_row(column):
    size = column.shape[0]
    eye = iota((size, size), 0) == iota((size, size), 1)
    return jnp.sum(jnp.where(eye, column, 0.0), axis=0, keepdims=True)


def as_column(row):
    size = row.shape[1]
    eye = iota((size, size), 0) == iota((size, size), 1)
    return jnp.sum(jnp.where(eye, row, 0.0), axis=1, keepdims=True)


def when(condition):
    if isinstance(condition, bool):
        return lambda f: f() if condition else None
    return pl.when(condition)


class Place:
    def __init__(self):
        self.me = lax.axis_index("seq")
        self.c = lax.rem(self.me, 2)
        self.sa = 2 + 6 * self.c
        self.sb = 8 - 6 * self.c
        self.a = lax.rem(self.me // self.sa, 4)
        self.b = lax.rem(self.me // self.sb, 4)
        self.sibling = self.me + 1 - 2 * self.c
        self.on_a = [lax.rem(self.a + i, 4) * self.sa for i in range(4)]
        self.on_b = [lax.rem(self.b + j, 4) * self.sb for j in range(4)]

    def first(self, i):
        return self.on_a[i] if isinstance(i, int) else lax.rem(self.a + i, 4) * self.sa

    def second(self, j):
        return self.on_b[j] if isinstance(j, int) else lax.rem(self.b + j, 4) * self.sb

    def mine(self, i, j):
        return self.first(i) + self.second(j) + self.c

    def theirs(self, i, j):
        return self.second(i) + self.first(j) + 1 - self.c


def key_block(kv, block):
    rows = kv[block]
    keys = rows[:ROUTED_DEV, :HEAD_DIM]
    values = rows[:ROUTED_DEV, HEAD_DIM:]
    digits = rows[ROUTED_DEV:].astype(jnp.float32)
    return keys, values, digits[0:1] * 256.0 + digits[1:2]


CHUNK = 512
FINAL_ROWS = 512
TILE = 256


def sublayer_kernel(
    idx_ref, dest_ref, count_ref, gain_ref, rw_ref,
    tok_hbm, cot_hbm, wq_hbm, wk_hbm, wv_hbm, wo_hbm,
    got, source_ref,
    tok, cot, wq, wkv, wo, pick, sendx, senddy, gotx, gotdy, sendm, gotm,
    fullx, fulldy, place, qpos, qkv, sums, q4, qt4, g4, gt4, acc, den, lden, delta,
    inv_col, router_col, dq, dqb, dkv,
    kv, to_sib, from_sib, to_b, from_b, to_a, from_a, far, near, relay, arrived, stats,
    load_sem, a2a_send, a2a_recv, x_send, x_recv, d_send, d_recv, kv_send, kv_recv,
    sends, sib_recv, b_recv, a_recv, rs_send, rs_recv, back_send, back_recv, st_send, st_recv,
):
    peers = lax.axis_size("seq")
    m = lax.axis_index("mp")
    at = Place()
    me = at.me
    bf16, f32 = jnp.bfloat16, jnp.float32
    slots = sendx.shape[0]
    tok_rows, quarter = tok.shape
    rows = ROUTED_DEV
    heads = wq.shape[1] // HEAD_DIM
    pair = slots // peers
    parts = quarter // TILE
    right, left, across = lax.rem(m + 1, 4), lax.rem(m + 3, 4), lax.rem(m + 2, 4)
    loads = [
        pltpu.make_async_copy(src, dst, load_sem.at[n])
        for n, (src, dst) in enumerate(
            [
                (tok_hbm, tok),
                (cot_hbm, cot),
                (wq_hbm, wq),
                (wk_hbm, wkv.at[:, pl.ds(0, HEAD_DIM)]),
                (wv_hbm, wkv.at[:, pl.ds(HEAD_DIM, HEAD_DIM)]),
                (wo_hbm, wo),
            ]
        )
    ]
    loads[0].start()
    greet("seq", peers)
    greet("mp", 4)

    idx = idx_ref[...]
    dest = dest_ref[...]
    valid = iota((1, slots), 1) < count_ref[0]
    owner = jnp.where(valid, lax.shift_right_logical(dest, 8), peers)
    place_slot = jnp.bitwise_and(dest, rows - 1)
    rows_i = iota((slots, slots), 0)
    cols_i = iota((slots, slots), 1)
    owner_col = jnp.sum(jnp.where(rows_i == cols_i, owner, 0), axis=1, keepdims=True)
    earlier = jnp.logical_and(owner_col == owner, rows_i < cols_i)
    rank = jnp.sum(jnp.where(earlier, 1, 0), axis=0, keepdims=True)
    buffer_place = jnp.where(valid, owner * pair + rank, slots)
    hit = rows_i == buffer_place
    source = jnp.sum(jnp.where(hit, idx - tok_rows, 0), axis=1, keepdims=True) + tok_rows
    pick[...] = onehot(iota((slots, tok_rows), 1) == source)

    lanes = iota((128, slots), 0)

    def spread(hits, entries, lane, shift):
        held = jnp.where(hits, entries, 0.0).astype(bf16)
        return dot(held, onehot(lanes == lane + shift), NT)

    owner_hit = iota((peers, slots), 0) == owner
    rank_lane = jnp.where(valid, rank, 128)
    position = me * tok_rows + idx
    digits = [
        place_slot + 1,
        lax.shift_right_logical(position, 8),
        jnp.bitwise_and(position, 255),
    ]
    meta = sum(
        spread(owner_hit, d.astype(f32), rank_lane, n * pair) for n, d in enumerate(digits)
    )
    sendm[...] = jnp.broadcast_to(meta[:, None, :], sendm.shape)

    pl.semaphore_wait(pltpu.get_barrier_semaphore(), peers - 1 + 3)

    def send_meta(src, dst, k):
        def body(i, carry):
            to = lax.rem(me + i, peers)
            remote(src.at[to], dst.at[me], a2a_send.at[k], a2a_recv.at[k], "seq", to).start()
            return carry

        lax.fori_loop(1, peers, body, 0)
        dst[me] = src[me]

    send_meta(sendm, gotm, 5)

    def pack(held, send, start, width):
        def body(n, carry):
            cols = span_of(start + n * TILE, TILE)
            send[:, cols] = dot(pick[...], held[:, cols]).astype(bf16)
            return carry

        lax.fori_loop(0, width // TILE, body, 0)
        return pl.ds(start, width)

    loads[0].wait()
    for load in loads[1:]:
        load.start()
    for n in range(parts):
        cols = pack(tok, sendx, n * TILE, TILE)
        send_pairs(peers, sendx, gotx, a2a_send.at[n], a2a_recv.at[n], pair, cols)
    loads[1].wait()
    pack(cot, senddy, 0, quarter)
    whole_cols = pl.ds(0, quarter)
    send_pairs(peers, senddy, gotdy, a2a_send.at[4], a2a_recv.at[4], pair, whole_cols)
    source_row = jnp.sum(jnp.where(rows_i == cols_i, source, 0), axis=0, keepdims=True)
    source_ref[...] = jnp.broadcast_to(source_row, source_ref.shape)

    others = pl.ds(0, peers - 1)
    column = iota((128, slots), 0)
    within = jnp.bitwise_and(iota((128, slots), 1), pair - 1)
    sender = iota((peers, slots), 0) == iota((peers, slots), 1) // pair

    def flat(got_rows, shift):
        out = dot(got_rows, onehot(column == within + shift))
        return jnp.sum(jnp.where(sender, out, 0.0), axis=0, keepdims=True)

    await_bytes(gotm.at[others], a2a_recv.at[5])
    got_meta = gotm[:, 0, :].astype(bf16)
    slot_in = flat(got_meta, 0)
    pos_in = flat(got_meta, pair) * 256.0 + flat(got_meta, 2 * pair)
    here = iota((rows, slots), 0).astype(f32) + 1.0 == slot_in
    place[...] = onehot(here)
    row_pos = jnp.sum(jnp.where(here, pos_in, 0.0), axis=1, keepdims=True)
    qpos[...] = jnp.broadcast_to(row_pos, qpos.shape)
    kpos = as_row(row_pos).astype(jnp.int32)
    pos_digits = jnp.where(
        iota((16, rows), 0) == 0,
        lax.shift_right_logical(kpos, 8),
        jnp.bitwise_and(kpos, 255),
    )
    kv[me, rows:, :] = pos_digits.astype(f32).astype(bf16)

    def compact(got_rows, full, start, width):
        def body(n, carry):
            to = span_of(m * quarter + start + n * TILE, TILE)
            part = got_rows[:, span_of(start + n * TILE, TILE)]
            full[:, to] = dot(place[...], part).astype(bf16)
            return carry

        lax.fori_loop(0, width // TILE, body, 0)

    def arrived_span(ref, width, start=0):
        return ref.at[pl.ds(0, slots - pair), pl.ds(start, width)]

    qkv[...] = jnp.zeros_like(qkv)
    sums[...] = jnp.zeros_like(sums)

    def project(block, start, width):
        f = span_of(block * quarter + start, width)
        x = fullx[:, f].astype(f32)
        sums[0] += lane_parts(x * x)
        sums[1] += lane_parts(x * rw_ref[:, f])
        scaled = (x * gain_ref[:, f]).astype(bf16)
        split = heads * HEAD_DIM
        qkv[:, :split] += dot(scaled, wq[f, :])
        qkv[:, split:] += dot(scaled, wkv[f, :])

    rings = [Ring(fullx, x_send, x_recv, 6 * n, n * TILE, TILE) for n in range(parts)]
    for n in range(parts):
        await_bytes(arrived_span(gotx, TILE, n * TILE), a2a_recv.at[n])
        compact(gotx, fullx, n * TILE, TILE)
        rings[n].begin()
        if n > 0:
            rings[n - 1].forward()
    rings[parts - 1].forward()
    for n in range(2, 5):
        loads[n].wait()
    project(m, 0, quarter)
    dy_rings = [Ring(fulldy, d_send, d_recv, 6 * n, n * TILE, TILE) for n in range(parts)]
    for n in range(parts):
        if n == parts - 1:
            await_bytes(arrived_span(gotdy, quarter), a2a_recv.at[4])
            compact(gotdy, fulldy, 0, quarter)
        rings[n].near()
        rings[n].end()
        if n == parts - 1:
            for ring in dy_rings:
                ring.begin()

        def body(i, carry):
            project(lax.rem(m + i, 4), n * TILE, TILE)
            return carry

        lax.fori_loop(1, 4, body, 0)

    mean = jnp.sum(sums[0], axis=1, keepdims=True) * (1.0 / (4 * quarter))
    inv = lax.rsqrt(mean + norm_eps)
    inv_col[...] = jnp.broadcast_to(inv, inv_col.shape)
    router_col[...] = jnp.broadcast_to(
        jnp.sum(sums[1], axis=1, keepdims=True), router_col.shape
    )
    split = heads * HEAD_DIM
    kv[me, :rows, :] = (qkv[:, split:] * inv).astype(bf16)

    half = rows // 2
    whole, top, low = pl.ds(0, rows + 16), pl.ds(0, half), pl.ds(half, half + 16)

    def send(block, to, part=whole):
        span = kv.at[block, part]
        remote(span, span, kv_send, kv_recv.at[block], "seq", to).start()

    def receive(block):
        await_bytes(kv.at[block], kv_recv.at[block])

    send(me, at.mine(1, 0))
    send(me, at.mine(3, 0))
    send(me, at.sibling)
    for h in range(heads):
        part = (qkv[:, h * HEAD_DIM : (h + 1) * HEAD_DIM] * inv).astype(bf16)
        q4[h * rows : (h + 1) * rows, :] = part
    acc[...] = jnp.zeros_like(acc)
    den[...] = jnp.zeros_like(den)

    def masks(key_pos):
        mask = live(key_pos, qpos[...])
        return jnp.concatenate([mask] * (CHUNK // rows), axis=0)

    def process(block):
        keys, values, key_pos = key_block(kv, block)
        mask = masks(key_pos)
        for start in range(0, heads * rows, CHUNK):
            r = slice(start, start + CHUNK)
            t = jnp.tanh(dot(q4[r, :], keys, NT) * (SCALE / score_cap))
            w = jnp.where(mask, jnp.exp2(t * (score_cap * LOG2E)), 0.0)
            den[r] += lane_parts(w)
            acc[r] += dot(w.astype(bf16), values)

    def order(t):
        if isinstance(t, int):
            t = max(0, t)
            u = t if t < 4 else (t - 4) // 2 if t < 12 else t - 12
            return [0, 1, 3, 2][u], 0 if t < 4 else 1 + 2 * (t % 2) if t < 12 else 2
        a = lax.div(t + 12, 16)
        b = lax.div(t + 4, 16)
        u = (1 - a) * t + (a - b) * lax.div(t - 4, 2) + b * (t - 12)
        i = u + lax.div(u, 2) * (1 - 2 * lax.rem(u, 2))
        j = (a - b) * (1 + 2 * lax.rem(t, 2)) + 2 * b
        return i, j

    def take(t):
        i, j = order(t)
        block = at.mine(i, j)
        receive(block)
        if isinstance(t, int):
            if t == 1:
                send(block, at.mine(3, 0), low)
            if t == 2:
                send(block, at.mine(1, 0), top)
            if t == 1:
                send(me, at.mine(0, 1))
                send(me, at.mine(0, 3))
            if t < 4:
                send(block, at.mine(0, 1))
                send(block, at.mine(0, 3))
        else:

            @pl.when(t < 4)
            def _():
                send(block, at.mine(0, 1))
                send(block, at.mine(0, 3))

            @pl.when(jnp.logical_and(t >= 4, j == 1))
            def _():
                send(block, at.mine(0, 3), low)

            @pl.when(j == 3)
            def _():
                send(block, at.mine(0, 1), top)

        send(block, at.sibling)
        return block

    def other(t):
        block = at.theirs(*order(t))
        receive(block)
        return block

    process(me)
    for h in range(heads):
        r = slice(h * rows, (h + 1) * rows)
        qt4[:, r] = q4[r, :].T
    blocks = [take(1), take(2), other(0)]
    for block in blocks:
        process(block)

    def step(s, carry):
        t = 1 + 2 * s
        blocks = [take(t), take(t + 1), other(t - 2), other(t - 1)]

        for n in range(parts):

            @pl.when(s == n + 1)
            def _():
                dy_rings[n].forward()

        for block in blocks:
            process(block)
        return carry

    lax.fori_loop(1, 7, step, 0)
    blocks = [other(13), other(14), take(15), other(15)]
    for block in blocks:
        process(block)

    loads[5].wait()
    for ring in dy_rings:
        ring.near()
        ring.end()
    router = router_col[...]
    dots = jnp.zeros((rows, 1), f32)
    for n in range(split // TILE):
        pulled = dot(fulldy[...], wo[n * TILE : (n + 1) * TILE, :], NT)
        for g in range(TILE // HEAD_DIM):
            h = n * (TILE // HEAD_DIM) + g
            r = slice(h * rows, (h + 1) * rows)
            mine = pulled[:, g * HEAD_DIM : (g + 1) * HEAD_DIM]
            total = jnp.sum(den[r], axis=1, keepdims=True)
            att = (acc[r] / total).astype(bf16).astype(f32)
            lden[r] = jnp.broadcast_to(jnp.log2(total), (rows, 128))
            grad = (mine * router).astype(bf16)
            g4[r, :] = grad
            gt4[:, r] = grad.T
            row_delta = jnp.sum(grad.astype(f32) * att, axis=1, keepdims=True)
            delta[r] = jnp.broadcast_to(row_delta, (rows, 128))
            dots = dots + jnp.sum(mine * att, axis=1, keepdims=True)

    def send_stats(k):
        def body(i, carry):
            to = lax.rem(m + i, 4)
            here = stats.at[k, m]
            remote(here, here, st_send.at[k], st_recv.at[k], "mp", to).start()
            return carry

        lax.fori_loop(1, 4, body, 0)

    def take_stats(k):
        await_bytes(stats.at[k, pl.ds(0, 3)], st_recv.at[k])
        return as_column((stats[k, 0] + stats[k, 1] + stats[k, 2] + stats[k, 3])[0:1])

    stats[0, m] = jnp.broadcast_to(as_row(dots), stats.shape[2:])
    send_stats(0)

    dq[...] = jnp.zeros_like(dq)

    def terms(block):
        keys, values, key_pos = key_block(kv, block)
        width = keys.shape[0]
        mask = masks(key_pos)
        probs, grads = [], []
        for start in range(0, heads * rows, CHUNK):
            r = slice(start, start + CHUNK)
            t = jnp.tanh(dot(q4[r, :], keys, NT) * (SCALE / score_cap))
            p = jnp.exp2(t * (score_cap * LOG2E) - wide(lden[r], width))
            p = jnp.where(mask, p, 0.0)
            dp = dot(g4[r, :], values, NT)
            probs.append(p.astype(bf16))
            grads.append((p * (dp - wide(delta[r], width)) * (1.0 - t * t)).astype(bf16))
        probs, grads = jnp.concatenate(probs, axis=0), jnp.concatenate(grads, axis=0)
        dq[...] += dot(grads, keys)
        dk = dot(qt4[...], grads) * SCALE
        return jnp.concatenate([dk, dot(gt4[...], probs)], axis=0)

    def pass_on(k, late, i, j):
        await_bytes(from_sib.at[k], sib_recv.at[k])

        @when(late == 0)
        def _():
            summed = to_b[k].astype(f32) + from_sib[k].astype(f32)
            to_b[k] = summed.astype(bf16)
            slot = (4 - j) * 4 + i
            remote(
                to_b.at[k], from_b.at[slot], sends.at[1], b_recv.at[slot], "seq",
                at.mine(0, j),
            ).start()

        @when(late == 1)
        def _():
            total = to_b[k].astype(f32) + from_sib[k].astype(f32)
            for n in range(1, 4):
                await_bytes(from_b.at[n * 4 + i], b_recv.at[n * 4 + i])
                total = total + from_b[n * 4 + i].astype(f32)

            @when(k < 15)
            def _():
                to_a[i] = total.astype(bf16)
                slot = 4 - i
                remote(
                    to_a.at[i], from_a.at[slot], sends.at[2], a_recv.at[slot], "seq",
                    at.mine(i, 0),
                ).start()

            @when(k == 15)
            def _():
                final = total
                for n in range(1, 4):
                    await_bytes(from_a.at[n], a_recv.at[n])
                    final = final + from_a[n].astype(f32)
                dkv[...] = final.T.astype(bf16)

    def back_places(s):
        late = s // 6
        places = []
        for n in range(2):
            k = 2 * s + n
            j = (1 + k // 4) * (1 - late)
            i = (k + late) % 4
            places.append((k, late, i, j))
        return places

    def sibling_terms(places):
        for k, _, i, j in places:
            to_sib[k] = terms(at.theirs(i, j)).astype(bf16)
            remote(
                to_sib.at[k], from_sib.at[k], sends.at[0], sib_recv.at[k], "seq", at.sibling
            ).start()

    def back_step(s, carry):
        places = back_places(s)
        sibling_terms(places)
        for k, _, i, j in places:
            to_b[k] = terms(at.mine(i, j)).astype(bf16)
        for where in places:
            pass_on(*where)
        return carry

    lax.fori_loop(0, 7, back_step, 0)
    places = back_places(7)
    sibling_terms(places)
    for k, _, i, j in places:
        to_b[k] = terms(at.mine(i, j)).astype(bf16)
        if k == 14:
            pass_on(*places[0])
    for h in range(heads):
        r = slice(h * rows, (h + 1) * rows)
        dqb[:, h * HEAD_DIM : (h + 1) * HEAD_DIM] = (dq[r] * SCALE).astype(bf16)
    stat = jnp.sum(dqb[...].astype(f32) * qkv[:, :split], axis=1, keepdims=True)
    pass_on(*places[1])

    chunks = quarter // TILE
    def contribution(block, n):
        f = span_of(block * quarter + n * TILE, TILE)
        total = dot(dqb[...], wq[f, :], NT) + dot(dkv[...], wkv[f, :], NT)
        return total * gain_ref[:, f]

    def rs(src, dst, n, k, to):
        k = 6 * n + k
        return remote(src, dst, rs_send.at[k], rs_recv.at[k], "mp", to)

    top, low = pl.ds(0, half), pl.ds(half, half)
    copies = []

    def hand_over(n):
        cols = pl.ds(n * TILE, TILE)
        copies[n][0].wait_recv()
        near[0, top, cols] = (
            near[0, top, cols].astype(f32) + relay[0, :, cols].astype(f32)
        ).astype(bf16)
        copies[n].append(rs(near.at[0, top, cols], arrived.at[0, top, cols], n, 4, right))
        copies[n][4].start()
        copies[n][1].wait_recv()
        near[1, low, cols] = (
            near[1, low, cols].astype(f32) + relay[1, :, cols].astype(f32)
        ).astype(bf16)
        copies[n].append(rs(near.at[1, low, cols], arrived.at[1, low, cols], n, 5, left))
        copies[n][5].start()

    back = sendx

    def finish_part(n):
        cols = pl.ds(n * TILE, TILE)
        f = span_of(m * quarter + n * TILE, TILE)
        own = contribution(m, n)
        for c in copies[n][2:]:
            c.wait_recv()
        own = own + arrived[0, :, cols].astype(f32) + arrived[1, :, cols].astype(f32)
        branch = inv * own - fullx[:, f].astype(f32) * factor + rw_ref[:, f] * router_grad
        back[:, cols] = dot(place[...], branch.astype(bf16), TN).astype(bf16)
        send_pairs(peers, back, got, back_send.at[n], back_recv.at[n], pair, cols)

    def issue(n):
        cols = pl.ds(n * TILE, TILE)
        far[:, cols] = contribution(across, n).astype(bf16)
        first = rs(far.at[top, cols], relay.at[0, :, cols], n, 0, right)
        second = rs(far.at[low, cols], relay.at[1, :, cols], n, 1, left)
        first.start()
        second.start()
        near[0, :, cols] = contribution(right, n).astype(bf16)
        third = rs(near.at[0, low, cols], arrived.at[0, low, cols], n, 2, right)
        third.start()
        near[1, :, cols] = contribution(left, n).astype(bf16)
        fourth = rs(near.at[1, top, cols], arrived.at[1, top, cols], n, 3, left)
        fourth.start()
        copies.append([first, second, third, fourth])

    issue(0)
    stat = stat + jnp.sum(dkv[...].astype(f32) * qkv[:, split:], axis=1, keepdims=True)
    stats[1, m] = jnp.broadcast_to(as_row(stat), stats.shape[2:])
    send_stats(1)
    issue(1)
    router_grad = take_stats(0)
    inv = inv_col[:, 0:1]
    for k in range(parts):
        await_bytes(arrived_span(sendx, TILE, k * TILE), a2a_send.at[k])
    hand_over(0)
    factor = inv * inv * inv * take_stats(1) * (1.0 / (4 * quarter))
    for n in range(1, chunks):
        if n + 1 < chunks:
            issue(n + 1)
        hand_over(n)
        finish_part(n - 1)
    finish_part(chunks - 1)

    for n in range(chunks):
        await_bytes(arrived_span(got, TILE, n * TILE), back_recv.at[n])
        await_bytes(arrived_span(back, TILE, n * TILE), back_send.at[n])
    await_bytes(arrived_span(senddy, quarter), a2a_send.at[4])
    await_bytes(sendm.at[others], a2a_send.at[5])
    for ring in rings + dy_rings:
        ring.sent()
    for group in copies:
        for c in group:
            c.wait_send()
    for k in range(2):
        await_bytes(stats.at[k, pl.ds(0, 3)], st_send.at[k])
    await_bytes(to_sib, sends.at[0])
    await_bytes(to_b.at[pl.ds(0, 12)], sends.at[1])
    await_bytes(to_a.at[pl.ds(0, 3)], sends.at[2])
    await_bytes(kv.at[others], kv_send)


def sublayer(tokens, cotangent, gain, router_weight, w_query, w_key, w_value, w_out, idx, count, dest):
    peers = lax.axis_size("seq")
    tok_rows, quarter = tokens.shape
    width = 4 * quarter
    split = w_query.shape[1]
    heads = split // HEAD_DIM
    rows = ROUTED_DEV
    slots = 2 * rows
    bf16, f32 = jnp.bfloat16, jnp.float32
    vmem = pl.BlockSpec(memory_space=pltpu.VMEM)
    hbm = pl.BlockSpec(memory_space=pl.ANY)
    shape = jax.ShapeDtypeStruct
    dma = pltpu.SemaphoreType.DMA
    ram = pltpu.VMEM
    stacked = heads * rows

    def held(n):
        return ram((n, 2 * HEAD_DIM, rows), bf16)

    return pl.pallas_call(
        sublayer_kernel,
        in_specs=[vmem, vmem, pl.BlockSpec(memory_space=pltpu.SMEM), vmem, vmem] + [hbm] * 6,
        out_specs=[vmem] * 2,
        out_shape=[
            shape((slots, quarter), bf16),
            shape((8, slots), jnp.int32),
        ],
        scratch_shapes=[
            ram((tok_rows, quarter), bf16), ram((tok_rows, quarter), bf16),
            ram((width, split), bf16), ram((width, 2 * HEAD_DIM), bf16), ram((split, width), bf16),
            ram((slots, tok_rows), bf16),
            ram((slots, quarter), bf16), ram((slots, quarter), bf16),
            ram((slots, quarter), bf16), ram((slots, quarter), bf16),
            ram((peers, 8, 128), f32), ram((peers, 8, 128), f32),
            ram((rows, width), bf16), ram((rows, width), bf16),
            ram((rows, slots), bf16), ram((rows, 128), f32),
            ram((rows, split + 2 * HEAD_DIM), f32), ram((2, rows, 128), f32),
            ram((stacked, HEAD_DIM), bf16), ram((HEAD_DIM, stacked), bf16),
            ram((stacked, HEAD_DIM), bf16), ram((HEAD_DIM, stacked), bf16),
            ram((stacked, HEAD_DIM), f32), ram((stacked, 128), f32),
            ram((stacked, 128), f32), ram((stacked, 128), f32),
            ram((rows, 128), f32), ram((rows, 128), f32),
            ram((stacked, HEAD_DIM), f32), ram((rows, split), bf16),
            ram((rows, 2 * HEAD_DIM), bf16),
            ram((peers, rows + 16, 2 * HEAD_DIM), bf16),
            held(16), held(16), held(16), held(16), held(4), held(4),
            ram((rows, quarter), bf16), ram((2, rows, quarter), bf16),
            ram((2, rows // 2, quarter), bf16), ram((2, rows, quarter), bf16),
            ram((2, 4, 8, rows), f32),
            dma((6,)), dma((6,)), dma((6,)), dma((24,)), dma((24,)), dma((24,)), dma((24,)),
            dma, dma((peers,)),
            dma((3,)), dma((16,)), dma((16,)), dma((4,)), dma((24,)), dma((24,)),
            dma((4,)), dma((4,)), dma((2,)), dma((2,)),
        ],
        compiler_params=pltpu.CompilerParams(
            collective_id=0, has_side_effects=True, vmem_limit_bytes=VMEM_LIMIT
        ),
        name="sublayer",
    )(
        idx, dest, count, gain, router_weight,
        tokens, cotangent, w_query, w_key, w_value, w_out,
    )


def final_kernel(cot_hbm, got_hbm, source_ref, out_hbm, cot, got, out, loads, stores):
    block, slots = FINAL_ROWS, got.shape[0]
    steps = cot.shape[0] // block
    got_load = pltpu.make_async_copy(got_hbm, got, loads.at[steps])
    got_load.start()

    def copy(n, src, dst, sems):
        rows = pl.ds(n * block, block)
        return pltpu.make_async_copy(src.at[rows], dst.at[rows], sems.at[n])

    for n in range(steps):
        copy(n, cot_hbm, cot, loads).start()
    got_load.wait()
    for n in range(steps):
        rows = pl.ds(n * block, block)
        put = onehot(iota((block, slots), 0) + n * block == source_ref[0:1, :])
        copy(n, cot_hbm, cot, loads).wait()
        total = cot[rows, :].astype(jnp.float32) + dot(put, got[...])
        out[rows, :] = total.astype(jnp.bfloat16)
        copy(n, out, out_hbm, stores).start()
    for n in range(steps):
        copy(n, out, out_hbm, stores).wait()


def finish(cotangent, got, source):
    hbm = pl.BlockSpec(memory_space=pl.ANY)
    steps = cotangent.shape[0] // FINAL_ROWS
    return pl.pallas_call(
        final_kernel,
        in_specs=[hbm, hbm, pl.BlockSpec(memory_space=pltpu.VMEM)],
        out_specs=hbm,
        out_shape=jax.ShapeDtypeStruct(cotangent.shape, jnp.bfloat16),
        scratch_shapes=[
            pltpu.VMEM(cotangent.shape, jnp.bfloat16),
            pltpu.VMEM(got.shape, jnp.bfloat16),
            pltpu.VMEM(cotangent.shape, jnp.bfloat16),
            pltpu.SemaphoreType.DMA((steps + 1,)),
            pltpu.SemaphoreType.DMA((steps,)),
        ],
        compiler_params=pltpu.CompilerParams(vmem_limit_bytes=VMEM_LIMIT),
        name="add_branch",
    )(cotangent, got, source)


def on_device(
    tokens,
    cotangent,
    norm_gain,
    router_weight,
    w_query,
    w_key,
    w_value,
    w_out,
    routed_index,
    routed_count,
    routed_dest,
):
    got, source = sublayer(
        tokens,
        cotangent,
        norm_gain[None, :],
        router_weight[None, :],
        w_query,
        w_key,
        w_value,
        w_out,
        routed_index,
        routed_count,
        routed_dest,
    )
    return finish(cotangent, got, source)


def solution(mesh):
    in_specs = (
        P("seq", "mp"),
        P("seq", "mp"),
        P(),
        P(),
        P(None, "mp"),
        P(None, "mp"),
        P(None, "mp"),
        P("mp", None),
        P("seq", None),
        P("seq"),
        P("seq", None),
    )
    out_specs = P("seq", "mp")
    return jax.shard_map(
        on_device, mesh=mesh, in_specs=in_specs, out_specs=out_specs, check_vma=False
    )
```

```python
import jax
import jax.numpy as jnp
from jax import lax
from jax.experimental import pallas as pl
from jax.experimental.pallas import tpu as pltpu
from jax.sharding import PartitionSpec as P

HEAD_DIM = 128
ROUTED_DEV = 256
MESH = pl.DeviceIdType.MESH
NT = (((1,), (1,)), ((), ()))
NN = (((1,), (0,)), ((), ()))
TN = (((0,), (0,)), ((), ()))
MIB = 1024 * 1024
VMEM_LIMIT = 60 * MIB
norm_eps = 1e-05
score_cap = 5.0
LOG2E = 1.4426950408889634
SCALE = HEAD_DIM ** (-0.5)


def dot(a, b, dims=NN):
    return lax.dot_general(a, b, dims, preferred_element_type=jnp.float32)


def iota(shape, dim):
    return lax.broadcasted_iota(jnp.int32, shape, dim)


def onehot(mask):
    return jnp.where(mask, 1.0, 0.0).astype(jnp.bfloat16)


def remote(src, dst, send_sem, recv_sem, axis, index):
    return pltpu.make_async_remote_copy(
        src_ref=src,
        dst_ref=dst,
        send_sem=send_sem,
        recv_sem=recv_sem,
        device_id={axis: index},
        device_id_type=MESH,
    )


def await_bytes(ref, sem):
    pltpu.make_async_copy(ref, ref, sem).wait()


def greet(axis, count):
    me = lax.axis_index(axis)
    barrier = pltpu.get_barrier_semaphore()

    def body(i, carry):
        pl.semaphore_signal(
            barrier, inc=1, device_id={axis: lax.rem(me + i, count)}, device_id_type=MESH
        )
        return carry

    lax.fori_loop(1, count, body, 0)


def span_of(start, width):
    return pl.ds(pl.multiple_of(start, width), width)


def send_pairs(peers, send, got, send_sem, recv_sem, rows, cols):
    me = lax.axis_index("seq")
    mine = span_of(me * rows, rows)

    def body(i, carry):
        to = lax.rem(me + i, peers)
        block = send.at[span_of(to * rows, rows), cols]
        remote(block, got.at[mine, cols], send_sem, recv_sem, "seq", to).start()
        return carry

    lax.fori_loop(1, peers, body, 0)
    got[mine, cols] = send[mine, cols]


class Ring:
    def __init__(self, full, send_sem, recv_sem, base, start, width):
        self.full, self.send_sem, self.recv_sem = full, send_sem, recv_sem
        self.base, self.start, self.width = base, start, width
        self.quarter = full.shape[1] // 4
        half = full.shape[0] // 2
        self.top, self.low = pl.ds(0, half), pl.ds(half, half)
        self.m = lax.axis_index("mp")
        self.right, self.left = lax.rem(self.m + 1, 4), lax.rem(self.m + 3, 4)
        self.far = lax.rem(self.m + 2, 4)

    def move(self, block, rows, k, to):
        part = self.full.at[rows, span_of(block * self.quarter + self.start, self.width)]
        k = self.base + k
        return remote(part, part, self.send_sem.at[k], self.recv_sem.at[k], "mp", to)

    def begin(self):
        self.move(self.m, self.top, 0, self.right).start()
        self.move(self.m, self.low, 1, self.left).start()
        self.move(self.m, self.low, 2, self.right).start()
        self.move(self.m, self.top, 3, self.left).start()

    def forward(self):
        self.move(self.left, self.top, 0, self.right).wait_recv()
        self.move(self.left, self.top, 4, self.right).start()
        self.move(self.right, self.low, 1, self.left).wait_recv()
        self.move(self.right, self.low, 5, self.left).start()

    def near(self):
        self.move(self.left, self.low, 2, self.right).wait_recv()
        self.move(self.right, self.top, 3, self.left).wait_recv()

    def end(self):
        self.move(self.far, self.top, 4, self.right).wait_recv()
        self.move(self.far, self.low, 5, self.left).wait_recv()

    def sent(self):
        for k in range(6):
            self.move(self.m, self.top, k, self.right).wait_send()


def live(kpos_row, qpos):
    parts = [kpos_row[:, c : c + 128] <= qpos for c in range(0, kpos_row.shape[1], 128)]
    return jnp.concatenate(parts, axis=1)


def wide(column, width):
    return jnp.concatenate([column] * (width // 128), axis=1)


def lane_parts(x):
    total = x[:, :128]
    for c in range(128, x.shape[1], 128):
        total = total + x[:, c : c + 128]
    return total


def as_row(column):
    size = column.shape[0]
    eye = iota((size, size), 0) == iota((size, size), 1)
    return jnp.sum(jnp.where(eye, column, 0.0), axis=0, keepdims=True)


def as_column(row):
    size = row.shape[1]
    eye = iota((size, size), 0) == iota((size, size), 1)
    return jnp.sum(jnp.where(eye, row, 0.0), axis=1, keepdims=True)


def when(condition):
    if isinstance(condition, bool):
        return lambda f: f() if condition else None
    return pl.when(condition)


class Place:
    def __init__(self):
        self.me = lax.axis_index("seq")
        self.c = lax.rem(self.me, 2)
        self.sa = 2 + 6 * self.c
        self.sb = 8 - 6 * self.c
        self.a = lax.rem(self.me // self.sa, 4)
        self.b = lax.rem(self.me // self.sb, 4)
        self.sibling = self.me + 1 - 2 * self.c
        self.on_a = [lax.rem(self.a + i, 4) * self.sa for i in range(4)]
        self.on_b = [lax.rem(self.b + j, 4) * self.sb for j in range(4)]

    def first(self, i):
        return self.on_a[i] if isinstance(i, int) else lax.rem(self.a + i, 4) * self.sa

    def second(self, j):
        return self.on_b[j] if isinstance(j, int) else lax.rem(self.b + j, 4) * self.sb

    def mine(self, i, j):
        return self.first(i) + self.second(j) + self.c

    def theirs(self, i, j):
        return self.second(i) + self.first(j) + 1 - self.c


def key_block(kv, block):
    rows = kv[block]
    keys = rows[:ROUTED_DEV, :HEAD_DIM]
    values = rows[:ROUTED_DEV, HEAD_DIM:]
    digits = rows[ROUTED_DEV:].astype(jnp.float32)
    return keys, values, digits[0:1] * 256.0 + digits[1:2]


CHUNK = 512
TILE = 256


def sublayer_kernel(
    idx_ref, dest_ref, count_ref, gain_ref, rw_ref,
    tok_hbm, cot_hbm, wq_hbm, wk_hbm, wv_hbm, wo_hbm,
    got, source_ref,
    tok, cot, wq, wkv, wo, pick, sendx, senddy, gotx, gotdy, sendm, gotm,
    fullx, fulldy, place, qpos, qkv, sums, q4, qt4, g4, gt4, acc, den, lden, delta,
    inv_col, router_col, dq, dqb, dkv,
    kv, to_sib, from_sib, to_b, from_b, to_a, from_a, far, near, relay, arrived, stats,
    load_sem, a2a_send, a2a_recv, x_send, x_recv, d_send, d_recv, kv_send, kv_recv,
    sends, sib_recv, b_recv, a_recv, rs_send, rs_recv, back_send, back_recv, st_send, st_recv,
):
    peers = lax.axis_size("seq")
    m = lax.axis_index("mp")
    at = Place()
    me = at.me
    bf16, f32 = jnp.bfloat16, jnp.float32
    slots = sendx.shape[0]
    tok_rows, quarter = tok.shape
    rows = ROUTED_DEV
    heads = wq.shape[1] // HEAD_DIM
    pair = slots // peers
    parts = quarter // TILE
    right, left, across = lax.rem(m + 1, 4), lax.rem(m + 3, 4), lax.rem(m + 2, 4)
    loads = [
        pltpu.make_async_copy(src, dst, load_sem.at[n])
        for n, (src, dst) in enumerate(
            [
                (tok_hbm, tok),
                (cot_hbm, cot),
                (wq_hbm, wq),
                (wk_hbm, wkv.at[:, pl.ds(0, HEAD_DIM)]),
                (wv_hbm, wkv.at[:, pl.ds(HEAD_DIM, HEAD_DIM)]),
                (wo_hbm, wo),
            ]
        )
    ]
    loads[0].start()
    greet("seq", peers)
    greet("mp", 4)

    idx = idx_ref[...]
    dest = dest_ref[...]
    valid = iota((1, slots), 1) < count_ref[0]
    owner = jnp.where(valid, lax.shift_right_logical(dest, 8), peers)
    place_slot = jnp.bitwise_and(dest, rows - 1)
    rows_i = iota((slots, slots), 0)
    cols_i = iota((slots, slots), 1)
    owner_col = jnp.sum(jnp.where(rows_i == cols_i, owner, 0), axis=1, keepdims=True)
    earlier = jnp.logical_and(owner_col == owner, rows_i < cols_i)
    rank = jnp.sum(jnp.where(earlier, 1, 0), axis=0, keepdims=True)
    buffer_place = jnp.where(valid, owner * pair + rank, slots)
    hit = rows_i == buffer_place
    source = jnp.sum(jnp.where(hit, idx - tok_rows, 0), axis=1, keepdims=True) + tok_rows
    pick[...] = onehot(iota((slots, tok_rows), 1) == source)

    lanes = iota((128, slots), 0)

    def spread(hits, entries, lane, shift):
        held = jnp.where(hits, entries, 0.0).astype(bf16)
        return dot(held, onehot(lanes == lane + shift), NT)

    owner_hit = iota((peers, slots), 0) == owner
    rank_lane = jnp.where(valid, rank, 128)
    position = me * tok_rows + idx
    digits = [
        place_slot + 1,
        lax.shift_right_logical(position, 8),
        jnp.bitwise_and(position, 255),
    ]
    meta = sum(
        spread(owner_hit, d.astype(f32), rank_lane, n * pair) for n, d in enumerate(digits)
    )
    sendm[...] = jnp.broadcast_to(meta[:, None, :], sendm.shape)

    pl.semaphore_wait(pltpu.get_barrier_semaphore(), peers - 1 + 3)

    def send_meta(src, dst, k):
        def body(i, carry):
            to = lax.rem(me + i, peers)
            remote(src.at[to], dst.at[me], a2a_send.at[k], a2a_recv.at[k], "seq", to).start()
            return carry

        lax.fori_loop(1, peers, body, 0)
        dst[me] = src[me]

    send_meta(sendm, gotm, 5)

    def pack(held, send, start, width):
        def body(n, carry):
            cols = span_of(start + n * TILE, TILE)
            send[:, cols] = dot(pick[...], held[:, cols]).astype(bf16)
            return carry

        lax.fori_loop(0, width // TILE, body, 0)
        return pl.ds(start, width)

    loads[0].wait()
    for load in loads[1:]:
        load.start()
    for n in range(parts):
        cols = pack(tok, sendx, n * TILE, TILE)
        send_pairs(peers, sendx, gotx, a2a_send.at[n], a2a_recv.at[n], pair, cols)
    loads[1].wait()
    pack(cot, senddy, 0, quarter)
    whole_cols = pl.ds(0, quarter)
    send_pairs(peers, senddy, gotdy, a2a_send.at[4], a2a_recv.at[4], pair, whole_cols)
    source_row = jnp.sum(jnp.where(rows_i == cols_i, source, 0), axis=0, keepdims=True)
    source_ref[...] = jnp.broadcast_to(source_row, source_ref.shape)

    others = pl.ds(0, peers - 1)
    column = iota((128, slots), 0)
    within = jnp.bitwise_and(iota((128, slots), 1), pair - 1)
    sender = iota((peers, slots), 0) == iota((peers, slots), 1) // pair

    def flat(got_rows, shift):
        out = dot(got_rows, onehot(column == within + shift))
        return jnp.sum(jnp.where(sender, out, 0.0), axis=0, keepdims=True)

    await_bytes(gotm.at[others], a2a_recv.at[5])
    got_meta = gotm[:, 0, :].astype(bf16)
    slot_in = flat(got_meta, 0)
    pos_in = flat(got_meta, pair) * 256.0 + flat(got_meta, 2 * pair)
    here = iota((rows, slots), 0).astype(f32) + 1.0 == slot_in
    place[...] = onehot(here)
    row_pos = jnp.sum(jnp.where(here, pos_in, 0.0), axis=1, keepdims=True)
    qpos[...] = jnp.broadcast_to(row_pos, qpos.shape)
    kpos = as_row(row_pos).astype(jnp.int32)
    pos_digits = jnp.where(
        iota((16, rows), 0) == 0,
        lax.shift_right_logical(kpos, 8),
        jnp.bitwise_and(kpos, 255),
    )
    kv[me, rows:, :] = pos_digits.astype(f32).astype(bf16)

    def compact(got_rows, full, start, width):
        def body(n, carry):
            to = span_of(m * quarter + start + n * TILE, TILE)
            part = got_rows[:, span_of(start + n * TILE, TILE)]
            full[:, to] = dot(place[...], part).astype(bf16)
            return carry

        lax.fori_loop(0, width // TILE, body, 0)

    def arrived_span(ref, width, start=0):
        return ref.at[pl.ds(0, slots - pair), pl.ds(start, width)]

    qkv[...] = jnp.zeros_like(qkv)
    sums[...] = jnp.zeros_like(sums)

    def project(block, start, width):
        f = span_of(block * quarter + start, width)
        x = fullx[:, f].astype(f32)
        sums[0] += lane_parts(x * x)
        sums[1] += lane_parts(x * rw_ref[:, f])
        scaled = (x * gain_ref[:, f]).astype(bf16)
        split = heads * HEAD_DIM
        qkv[:, :split] += dot(scaled, wq[f, :])
        qkv[:, split:] += dot(scaled, wkv[f, :])

    rings = [Ring(fullx, x_send, x_recv, 6 * n, n * TILE, TILE) for n in range(parts)]
    for n in range(parts):
        await_bytes(arrived_span(gotx, TILE, n * TILE), a2a_recv.at[n])
        compact(gotx, fullx, n * TILE, TILE)
        rings[n].begin()
        if n > 0:
            rings[n - 1].forward()
    rings[parts - 1].forward()
    for n in range(2, 5):
        loads[n].wait()
    project(m, 0, quarter)
    dy_rings = [Ring(fulldy, d_send, d_recv, 6 * n, n * TILE, TILE) for n in range(parts)]
    for n in range(parts):
        if n == parts - 1:
            await_bytes(arrived_span(gotdy, quarter), a2a_recv.at[4])
            compact(gotdy, fulldy, 0, quarter)
        rings[n].near()
        rings[n].end()
        if n == parts - 1:
            for ring in dy_rings:
                ring.begin()

        def body(i, carry):
            project(lax.rem(m + i, 4), n * TILE, TILE)
            return carry

        lax.fori_loop(1, 4, body, 0)

    mean = jnp.sum(sums[0], axis=1, keepdims=True) * (1.0 / (4 * quarter))
    inv = lax.rsqrt(mean + norm_eps)
    inv_col[...] = jnp.broadcast_to(inv, inv_col.shape)
    router_col[...] = jnp.broadcast_to(
        jnp.sum(sums[1], axis=1, keepdims=True), router_col.shape
    )
    split = heads * HEAD_DIM
    kv[me, :rows, :] = (qkv[:, split:] * inv).astype(bf16)

    half = rows // 2
    whole, top, low = pl.ds(0, rows + 16), pl.ds(0, half), pl.ds(half, half + 16)

    def send(block, to, part=whole):
        span = kv.at[block, part]
        remote(span, span, kv_send, kv_recv.at[block], "seq", to).start()

    def receive(block):
        await_bytes(kv.at[block], kv_recv.at[block])

    send(me, at.mine(1, 0))
    send(me, at.mine(3, 0))
    send(me, at.mine(2, 0))
    send(me, at.sibling)
    for h in range(heads):
        part = (qkv[:, h * HEAD_DIM : (h + 1) * HEAD_DIM] * inv).astype(bf16)
        q4[h * rows : (h + 1) * rows, :] = part
    acc[...] = jnp.zeros_like(acc)
    den[...] = jnp.zeros_like(den)

    def masks(key_pos):
        mask = live(key_pos, qpos[...])
        return jnp.concatenate([mask] * (CHUNK // rows), axis=0)

    def process(block):
        keys, values, key_pos = key_block(kv, block)
        mask = masks(key_pos)
        for start in range(0, heads * rows, CHUNK):
            r = slice(start, start + CHUNK)
            t = jnp.tanh(dot(q4[r, :], keys, NT) * (SCALE / score_cap))
            w = jnp.where(mask, jnp.exp2(t * (score_cap * LOG2E)), 0.0)
            den[r] += lane_parts(w)
            acc[r] += dot(w.astype(bf16), values)

    def order(t):
        if isinstance(t, int):
            t = max(0, t)
            u = t if t < 4 else (t - 4) // 2 if t < 12 else t - 12
            return [0, 1, 3, 2][u], 0 if t < 4 else 1 + 2 * (t % 2) if t < 12 else 2
        a = lax.div(t + 12, 16)
        b = lax.div(t + 4, 16)
        u = (1 - a) * t + (a - b) * lax.div(t - 4, 2) + b * (t - 12)
        i = u + lax.div(u, 2) * (1 - 2 * lax.rem(u, 2))
        j = (a - b) * (1 + 2 * lax.rem(t, 2)) + 2 * b
        return i, j

    def take(t):
        i, j = order(t)
        block = at.mine(i, j)
        receive(block)
        if isinstance(t, int):
            if t == 1:
                send(me, at.mine(0, 1))
                send(me, at.mine(0, 3))
            if t < 4:
                send(block, at.mine(0, 1))
                send(block, at.mine(0, 3))
        else:

            @pl.when(t < 4)
            def _():
                send(block, at.mine(0, 1))
                send(block, at.mine(0, 3))

            @pl.when(jnp.logical_and(t >= 4, j == 1))
            def _():
                send(block, at.mine(0, 3), low)

            @pl.when(j == 3)
            def _():
                send(block, at.mine(0, 1), top)

        send(block, at.sibling)
        return block

    def other(t):
        block = at.theirs(*order(t))
        receive(block)
        return block

    process(me)
    for h in range(heads):
        r = slice(h * rows, (h + 1) * rows)
        qt4[:, r] = q4[r, :].T
    blocks = [take(1), take(2), other(0)]
    for block in blocks:
        process(block)

    def step(s, carry):
        t = 1 + 2 * s
        blocks = [take(t), take(t + 1), other(t - 2), other(t - 1)]

        for n in range(parts):

            @pl.when(s == n + 2)
            def _():
                dy_rings[n].forward()

        for block in blocks:
            process(block)
        return carry

    lax.fori_loop(1, 7, step, 0)
    blocks = [other(13), other(14), take(15), other(15)]
    for block in blocks:
        process(block)

    loads[5].wait()
    for ring in dy_rings:
        ring.near()
        ring.end()
    router = router_col[...]
    dots = jnp.zeros((rows, 1), f32)
    for n in range(split // TILE):
        pulled = dot(fulldy[...], wo[n * TILE : (n + 1) * TILE, :], NT)
        for g in range(TILE // HEAD_DIM):
            h = n * (TILE // HEAD_DIM) + g
            r = slice(h * rows, (h + 1) * rows)
            mine = pulled[:, g * HEAD_DIM : (g + 1) * HEAD_DIM]
            total = jnp.sum(den[r], axis=1, keepdims=True)
            att = (acc[r] / total).astype(bf16).astype(f32)
            lden[r] = jnp.broadcast_to(jnp.log2(total), (rows, 128))
            grad = (mine * router).astype(bf16)
            g4[r, :] = grad
            gt4[:, r] = grad.T
            row_delta = jnp.sum(grad.astype(f32) * att, axis=1, keepdims=True)
            delta[r] = jnp.broadcast_to(row_delta, (rows, 128))
            dots = dots + jnp.sum(mine * att, axis=1, keepdims=True)

    def send_stats(k):
        def body(i, carry):
            to = lax.rem(m + i, 4)
            here = stats.at[k, m]
            remote(here, here, st_send.at[k], st_recv.at[k], "mp", to).start()
            return carry

        lax.fori_loop(1, 4, body, 0)

    def take_stats(k):
        await_bytes(stats.at[k, pl.ds(0, 3)], st_recv.at[k])
        return as_column((stats[k, 0] + stats[k, 1] + stats[k, 2] + stats[k, 3])[0:1])

    stats[0, m] = jnp.broadcast_to(as_row(dots), stats.shape[2:])
    send_stats(0)

    dq[...] = jnp.zeros_like(dq)

    def terms(block):
        keys, values, key_pos = key_block(kv, block)
        width = keys.shape[0]
        mask = masks(key_pos)
        probs, grads = [], []
        for start in range(0, heads * rows, CHUNK):
            r = slice(start, start + CHUNK)
            t = jnp.tanh(dot(q4[r, :], keys, NT) * (SCALE / score_cap))
            p = jnp.exp2(t * (score_cap * LOG2E) - wide(lden[r], width))
            p = jnp.where(mask, p, 0.0)
            dp = dot(g4[r, :], values, NT)
            probs.append(p.astype(bf16))
            grads.append((p * (dp - wide(delta[r], width)) * (1.0 - t * t)).astype(bf16))
        probs, grads = jnp.concatenate(probs, axis=0), jnp.concatenate(grads, axis=0)
        dq[...] += dot(grads, keys)
        dk = dot(qt4[...], grads) * SCALE
        return jnp.concatenate([dk, dot(gt4[...], probs)], axis=0)

    def pass_on(k, late, i, j):
        await_bytes(from_sib.at[k], sib_recv.at[k])

        @when(late == 0)
        def _():
            summed = to_b[k].astype(f32) + from_sib[k].astype(f32)
            to_b[k] = summed.astype(bf16)
            slot = (4 - j) * 4 + i
            remote(
                to_b.at[k], from_b.at[slot], sends.at[1], b_recv.at[slot], "seq",
                at.mine(0, j),
            ).start()

        @when(late == 1)
        def _():
            total = to_b[k].astype(f32) + from_sib[k].astype(f32)
            for n in range(1, 4):
                await_bytes(from_b.at[n * 4 + i], b_recv.at[n * 4 + i])
                total = total + from_b[n * 4 + i].astype(f32)

            @when(k < 15)
            def _():
                to_a[i] = total.astype(bf16)
                slot = 4 - i
                remote(
                    to_a.at[i], from_a.at[slot], sends.at[2], a_recv.at[slot], "seq",
                    at.mine(i, 0),
                ).start()

            @when(k == 15)
            def _():
                final = total
                for n in range(1, 4):
                    await_bytes(from_a.at[n], a_recv.at[n])
                    final = final + from_a[n].astype(f32)
                dkv[...] = final.T.astype(bf16)

    def back_places(s):
        late = s // 6
        places = []
        for n in range(2):
            k = 2 * s + n
            j = (1 + k // 4) * (1 - late)
            i = (k + late) % 4
            places.append((k, late, i, j))
        return places

    def sibling_terms(places):
        for k, _, i, j in places:
            to_sib[k] = terms(at.theirs(i, j)).astype(bf16)
            remote(
                to_sib.at[k], from_sib.at[k], sends.at[0], sib_recv.at[k], "seq", at.sibling
            ).start()

    def back_step(s, carry):
        places = back_places(s)
        sibling_terms(places)
        for k, _, i, j in places:
            to_b[k] = terms(at.mine(i, j)).astype(bf16)
        for where in places:
            pass_on(*where)
        return carry

    lax.fori_loop(0, 7, back_step, 0)
    places = back_places(7)
    sibling_terms(places)
    for k, _, i, j in places:
        to_b[k] = terms(at.mine(i, j)).astype(bf16)
        if k == 14:
            pass_on(*places[0])
    for h in range(heads):
        r = slice(h * rows, (h + 1) * rows)
        dqb[:, h * HEAD_DIM : (h + 1) * HEAD_DIM] = (dq[r] * SCALE).astype(bf16)
    stat = jnp.sum(dqb[...].astype(f32) * qkv[:, :split], axis=1, keepdims=True)
    pass_on(*places[1])

    chunks = quarter // TILE
    def contribution(block, n):
        f = span_of(block * quarter + n * TILE, TILE)
        total = dot(dqb[...], wq[f, :], NT) + dot(dkv[...], wkv[f, :], NT)
        return total * gain_ref[:, f]

    def rs(src, dst, n, k, to):
        k = 6 * n + k
        return remote(src, dst, rs_send.at[k], rs_recv.at[k], "mp", to)

    top, low = pl.ds(0, half), pl.ds(half, half)
    copies = []

    def hand_over(n):
        cols = pl.ds(n * TILE, TILE)
        copies[n][0].wait_recv()
        near[0, top, cols] = (
            near[0, top, cols].astype(f32) + relay[0, :, cols].astype(f32)
        ).astype(bf16)
        copies[n].append(rs(near.at[0, top, cols], arrived.at[0, top, cols], n, 4, right))
        copies[n][4].start()
        copies[n][1].wait_recv()
        near[1, low, cols] = (
            near[1, low, cols].astype(f32) + relay[1, :, cols].astype(f32)
        ).astype(bf16)
        copies[n].append(rs(near.at[1, low, cols], arrived.at[1, low, cols], n, 5, left))
        copies[n][5].start()

    back = sendx

    def finish_part(n):
        cols = pl.ds(n * TILE, TILE)
        f = span_of(m * quarter + n * TILE, TILE)
        own = contribution(m, n)
        for c in copies[n][2:]:
            c.wait_recv()
        own = own + arrived[0, :, cols].astype(f32) + arrived[1, :, cols].astype(f32)
        branch = inv * own - fullx[:, f].astype(f32) * factor + rw_ref[:, f] * router_grad
        back[:, cols] = dot(place[...], branch.astype(bf16), TN).astype(bf16)
        send_pairs(peers, back, got, back_send.at[n], back_recv.at[n], pair, cols)

    def issue(n):
        cols = pl.ds(n * TILE, TILE)
        far[:, cols] = contribution(across, n).astype(bf16)
        first = rs(far.at[top, cols], relay.at[0, :, cols], n, 0, right)
        second = rs(far.at[low, cols], relay.at[1, :, cols], n, 1, left)
        first.start()
        second.start()
        near[0, :, cols] = contribution(right, n).astype(bf16)
        third = rs(near.at[0, low, cols], arrived.at[0, low, cols], n, 2, right)
        third.start()
        near[1, :, cols] = contribution(left, n).astype(bf16)
        fourth = rs(near.at[1, top, cols], arrived.at[1, top, cols], n, 3, left)
        fourth.start()
        copies.append([first, second, third, fourth])

    issue(0)
    stat = stat + jnp.sum(dkv[...].astype(f32) * qkv[:, split:], axis=1, keepdims=True)
    stats[1, m] = jnp.broadcast_to(as_row(stat), stats.shape[2:])
    send_stats(1)
    issue(1)
    router_grad = take_stats(0)
    inv = inv_col[:, 0:1]
    for k in range(parts):
        await_bytes(arrived_span(sendx, TILE, k * TILE), a2a_send.at[k])
    hand_over(0)
    factor = inv * inv * inv * take_stats(1) * (1.0 / (4 * quarter))
    for n in range(1, chunks):
        if n + 1 < chunks:
            issue(n + 1)
        hand_over(n)
        finish_part(n - 1)
    finish_part(chunks - 1)

    for n in range(chunks):
        await_bytes(arrived_span(got, TILE, n * TILE), back_recv.at[n])
        await_bytes(arrived_span(back, TILE, n * TILE), back_send.at[n])
    await_bytes(arrived_span(senddy, quarter), a2a_send.at[4])
    await_bytes(sendm.at[others], a2a_send.at[5])
    for ring in rings + dy_rings:
        ring.sent()
    for group in copies:
        for c in group:
            c.wait_send()
    for k in range(2):
        await_bytes(stats.at[k, pl.ds(0, 3)], st_send.at[k])
    await_bytes(to_sib, sends.at[0])
    await_bytes(to_b.at[pl.ds(0, 12)], sends.at[1])
    await_bytes(to_a.at[pl.ds(0, 3)], sends.at[2])
    await_bytes(kv.at[others], kv_send)


def sublayer(tokens, cotangent, gain, router_weight, w_query, w_key, w_value, w_out, idx, count, dest):
    peers = lax.axis_size("seq")
    tok_rows, quarter = tokens.shape
    width = 4 * quarter
    split = w_query.shape[1]
    heads = split // HEAD_DIM
    rows = ROUTED_DEV
    slots = 2 * rows
    bf16, f32 = jnp.bfloat16, jnp.float32
    vmem = pl.BlockSpec(memory_space=pltpu.VMEM)
    hbm = pl.BlockSpec(memory_space=pl.ANY)
    shape = jax.ShapeDtypeStruct
    dma = pltpu.SemaphoreType.DMA
    ram = pltpu.VMEM
    stacked = heads * rows

    def held(n):
        return ram((n, 2 * HEAD_DIM, rows), bf16)

    return pl.pallas_call(
        sublayer_kernel,
        in_specs=[vmem, vmem, pl.BlockSpec(memory_space=pltpu.SMEM), vmem, vmem] + [hbm] * 6,
        out_specs=[vmem] * 2,
        out_shape=[
            shape((slots, quarter), bf16),
            shape((8, slots), jnp.int32),
        ],
        scratch_shapes=[
            ram((tok_rows, quarter), bf16), ram((tok_rows, quarter), bf16),
            ram((width, split), bf16), ram((width, 2 * HEAD_DIM), bf16), ram((split, width), bf16),
            ram((slots, tok_rows), bf16),
            ram((slots, quarter), bf16), ram((slots, quarter), bf16),
            ram((slots, quarter), bf16), ram((slots, quarter), bf16),
            ram((peers, 8, 128), f32), ram((peers, 8, 128), f32),
            ram((rows, width), bf16), ram((rows, width), bf16),
            ram((rows, slots), bf16), ram((rows, 128), f32),
            ram((rows, split + 2 * HEAD_DIM), f32), ram((2, rows, 128), f32),
            ram((stacked, HEAD_DIM), bf16), ram((HEAD_DIM, stacked), bf16),
            ram((stacked, HEAD_DIM), bf16), ram((HEAD_DIM, stacked), bf16),
            ram((stacked, HEAD_DIM), f32), ram((stacked, 128), f32),
            ram((stacked, 128), f32), ram((stacked, 128), f32),
            ram((rows, 128), f32), ram((rows, 128), f32),
            ram((stacked, HEAD_DIM), f32), ram((rows, split), bf16),
            ram((rows, 2 * HEAD_DIM), bf16),
            ram((peers, rows + 16, 2 * HEAD_DIM), bf16),
            held(16), held(16), held(16), held(16), held(4), held(4),
            ram((rows, quarter), bf16), ram((2, rows, quarter), bf16),
            ram((2, rows // 2, quarter), bf16), ram((2, rows, quarter), bf16),
            ram((2, 4, 8, rows), f32),
            dma((6,)), dma((6,)), dma((6,)), dma((24,)), dma((24,)), dma((24,)), dma((24,)),
            dma, dma((peers,)),
            dma((3,)), dma((16,)), dma((16,)), dma((4,)), dma((24,)), dma((24,)),
            dma((4,)), dma((4,)), dma((2,)), dma((2,)),
        ],
        compiler_params=pltpu.CompilerParams(
            collective_id=0, has_side_effects=True, vmem_limit_bytes=VMEM_LIMIT
        ),
        name="sublayer",
    )(
        idx, dest, count, gain, router_weight,
        tokens, cotangent, w_query, w_key, w_value, w_out,
    )


def on_device(
    tokens,
    cotangent,
    norm_gain,
    router_weight,
    w_query,
    w_key,
    w_value,
    w_out,
    routed_index,
    routed_count,
    routed_dest,
):
    got, source = sublayer(
        tokens,
        cotangent,
        norm_gain[None, :],
        router_weight[None, :],
        w_query,
        w_key,
        w_value,
        w_out,
        routed_index,
        routed_count,
        routed_dest,
    )
    slots = jnp.arange(cotangent.shape[0], dtype=jnp.int32)
    put = (slots[:, None] == source[0:1]).astype(jnp.bfloat16)
    return (cotangent.astype(jnp.float32) + dot(put, got)).astype(jnp.bfloat16)


def solution(mesh):
    in_specs = (
        P("seq", "mp"),
        P("seq", "mp"),
        P(),
        P(),
        P(None, "mp"),
        P(None, "mp"),
        P(None, "mp"),
        P("mp", None),
        P("seq", None),
        P("seq"),
        P("seq", None),
    )
    out_specs = P("seq", "mp")
    return jax.shard_map(
        on_device, mesh=mesh, in_specs=in_specs, out_specs=out_specs, check_vma=False
    )
```
